32 devices in a mesh: grp: 8 (over z, core), clu: 4 (over y, x).
Axes of the slice: x: 2, y: 2, z: 4, core: 2. Of those that a mesh axis runs over, the one named last changes fastest.
Arguments:
- strengths: bfloat16 [4096, 128], P(('grp', 'clu')), may hold values from -6 to 6
- adjoint_weights: bfloat16 [4096, 128], P(('grp', 'clu')), may hold values from -6 to 6
- kernels: bfloat16 [6144, 2, 128, 128], P(('grp', 'clu')), may hold values from -0.02734375 to 0.02734375
- target_ids: int32 [6144], P(('grp', 'clu')), may hold values from 0 to 31, as said below
- source_ids: int32 [6144], P(('grp', 'clu')), may hold values from 0 to 31, as said below
- live_slots: int32 [32], P(('grp', 'clu')), may hold values from 48 to 192, as said below
Outputs:
- potential: float32 [4096, 128], P(('grp', 'clu'))
- adjoint_field: float32 [4096, 128], P(('grp', 'clu'))
The draws below stay inside these ranges and needn't reach their ends.
Inputs may be any that keep to these rules, and one draw needn't show every extreme that they name: `target_ids`: a slot's target block is one of the 4 blocks owned by the devices with the slot's grp index. `source_ids`: a slot's source block is owned by a device whose grp index equals that of the slot's device or differs from it by one. `live_slots`: some device uses all 192 slots.
All inputs are finite; a program needn't handle non-finite values.
Results may differ from the reference program's by a relative error of at most 0.0003.
Values may be sent and summed in bfloat16 or wider, within the bound.
No kernel may reach another device: no remote copies, remote signals or barrier semaphores. Data moves between devices by JAX's collectives and lax.ppermute only.
A program may use at most 128 MiB of HBM per device.

```python
import jax
import jax.numpy as jnp
from jax import lax

PB = 128
BLK_DEV = 1
NNZ_DEV = 192
COLS = 128
GROUPS = 8
GROUP_BLOCKS = 4
NBLK = 32
NPANEL = 4096
SLOTS = 6144
N_CLU = 4
DEVICES = 32


def draw_target_ids(key, part):
    device = jnp.arange(SLOTS, dtype=jnp.int32) // NNZ_DEV
    group = device // N_CLU
    within = jax.random.randint(jax.random.fold_in(key, 11), (SLOTS,), 0, GROUP_BLOCKS)
    return (group * GROUP_BLOCKS + within).astype(jnp.int32)


def draw_source_ids(key, part):
    device = jnp.arange(SLOTS, dtype=jnp.int32) // NNZ_DEV
    group = device // N_CLU
    offset = jax.random.randint(jax.random.fold_in(key, 23), (SLOTS,), -1, 2)
    shifted = group + offset
    shifted = jnp.where((shifted < 0) | (shifted >= GROUPS), group, shifted)
    within = jax.random.randint(jax.random.fold_in(key, 29), (SLOTS,), 0, GROUP_BLOCKS)
    return (shifted * GROUP_BLOCKS + within).astype(jnp.int32)


def draw_live_slots(key, part):
    lowest = max(NNZ_DEV // 4, 1)
    counts = jax.random.randint(jax.random.fold_in(key, 31), (DEVICES,), lowest, NNZ_DEV + 1)
    fullest = jax.random.randint(jax.random.fold_in(key, 37), (), 0, DEVICES)
    return jnp.where(jnp.arange(DEVICES, dtype=jnp.int32) == fullest, NNZ_DEV, counts).astype(jnp.int32)


def levels(key, extent, cuts, smallest, top_value):
    loudness = 1.0
    for position, parts in cuts:
        heights = jax.random.uniform(jax.random.fold_in(jax.random.fold_in(key, 6), position), (parts,), jnp.float32, smallest / len(cuts), top_value / len(cuts))
        loudness = loudness * jnp.repeat(jnp.exp(heights), extent[position] // parts).reshape((-1,) + (1,) * (len(extent) - 1 - position))
    return loudness


def gaussian(rng, shape, scale, bound, shards=(), kind=jnp.bfloat16):
    level = levels(rng, shape, shards, -0.22, 0.18) if shards else 1.0
    values = jax.random.normal(rng, shape, jnp.float32) * scale * level
    return jnp.minimum(jnp.maximum(values, -bound), bound).astype(kind)


def setup_inputs(seed: int = 0) -> dict:
    key_of = jax.random.split(jax.random.key(seed), 7)
    return {
        "strengths": gaussian(key_of[0], (NPANEL, COLS), 1.0, 6.0, ((0, 32),)),
        "adjoint_weights": gaussian(key_of[1], (NPANEL, COLS), 1.0, 6.0, ((0, 32),)),
        "kernels": gaussian(key_of[2], (SLOTS, 2, PB, PB), (2 * PB * NNZ_DEV // BLK_DEV) ** -0.5, 0.02734375, ((0, 32),)),
        "target_ids": draw_target_ids(jax.random.fold_in(key_of[6], 71), 0),
        "source_ids": draw_source_ids(jax.random.fold_in(key_of[6], 71), 0),
        "live_slots": draw_live_slots(jax.random.fold_in(key_of[6], 71), 0),
    }


def complex_join(prod):
    half = prod.shape[-1] // 2
    real_part = prod[:, 0, :, :half] - prod[:, 1, :, half:]
    imag_part = prod[:, 0, :, half:] + prod[:, 1, :, :half]
    return jnp.concatenate([real_part, imag_part], axis=-1)


def reference(strengths, adjoint_weights, kernels, target_ids, source_ids, live_slots):
    sig_blocks = strengths.reshape(NBLK, PB, COLS).astype(jnp.float32)
    mu_blocks = adjoint_weights.reshape(NBLK, PB, COLS).astype(jnp.float32)
    kern = kernels.reshape(DEVICES, NNZ_DEV, 2, PB, PB)
    tgt = target_ids.reshape(DEVICES, NNZ_DEV)
    src = source_ids.reshape(DEVICES, NNZ_DEV)

    def step(carry, inputs):
        phi, psi = carry
        k_dev, t_dev, s_dev, count = inputs
        live = (jnp.arange(NNZ_DEV, dtype=jnp.int32) < count).astype(jnp.float32)[:, None, None]
        kf = k_dev.astype(jnp.float32)
        fwd = jnp.einsum('nkpq,nqc->nkpc', kf, sig_blocks[s_dev], precision=lax.Precision.HIGHEST)
        bwd = jnp.einsum('nkpq,npc->nkqc', kf, mu_blocks[t_dev], precision=lax.Precision.HIGHEST)
        phi = phi.at[t_dev].add(complex_join(fwd) * live)
        psi = psi.at[s_dev].add(complex_join(bwd) * live)
        return (phi, psi), None

    start = jnp.zeros((NBLK, PB, COLS), jnp.float32)
    (phi, psi), _ = lax.scan(step, (start, start), (kern, tgt, src, live_slots))
    return phi.reshape(NPANEL, COLS), psi.reshape(NPANEL, COLS)
```

```python
import functools

import jax
import jax.numpy as jnp
from jax import lax
from jax.experimental import pallas as pl
from jax.experimental.pallas import tpu as pltpu
from jax.sharding import PartitionSpec as P

VMEM_BYTES = 50 * 1024 * 1024


def shifted(value, axis, steps):
    count = lax.axis_size(axis)
    first, last = (max(0, -steps), min(count, count - steps))
    return lax.ppermute(value, axis, [(source, source + steps) for source in range(first, last)])


def to_partner(value, axis, step):
    count = lax.axis_size(axis)
    return lax.ppermute(value, axis, [(i, i ^ step) for i in range(count)])


def turned(block):
    half = block.shape[1] // 2
    wide = pltpu.roll(block.astype(jnp.float32), half, axis=1)
    lane = lax.broadcasted_iota(jnp.int32, wide.shape, 1)
    return jnp.where(lane < half, -wide, wide).astype(block.dtype)


def turned_rows(block):
    half = block.shape[0] // 2
    return jnp.concatenate([-block[half:], block[:half]], axis=0)


def slot_place(target_ref, source_ref, slot, blocks, clusters):
    group, me = lax.axis_index("grp"), lax.axis_index("clu")
    group_blocks = blocks * clusters

    def relative(within):
        return ((within // blocks) ^ me) * blocks + within % blocks

    target = relative(target_ref[slot] - group * group_blocks)
    source = source_ref[slot] - (group - 1) * group_blocks
    return target, source // group_blocks * group_blocks + relative(source % group_blocks)


def start_fetch(live, chunk, kernels_ref, held, sems):
    for c in range(held.shape[0] // chunk):
        rows = pl.ds(c * chunk, chunk)

        @pl.when(c * chunk < live)
        def _():
            pltpu.make_async_copy(kernels_ref.at[rows], held.at[rows], sems.at[c]).start()


def each_slot(live, chunk, kernels_ref, held, sems, work):
    @pl.loop(0, pl.cdiv(live, chunk))
    def _(c):
        rows = pl.ds(c * chunk, chunk)
        pltpu.make_async_copy(kernels_ref.at[rows], held.at[rows], sems.at[c]).wait()

        @pl.loop(c * chunk, jnp.minimum((c + 1) * chunk, live))
        def _(slot):
            work(slot)


def combine_kernel(blocks, clusters, chunk, live_ref, target_ref, source_ref, kernels_ref, out_ref, held, total, sems):
    live = live_ref[0]
    sources = 3 * blocks * clusters
    start_fetch(live, chunk, kernels_ref, held, sems)

    @pl.loop(0, total.shape[0])
    def _(pair):
        total[pair] = jnp.zeros(total.shape[1:], total.dtype)

    def add(slot):
        target, source = slot_place(target_ref, source_ref, slot, blocks, clusters)
        pair = target * sources + source
        total[pair] += held[slot].reshape(total.shape[1:]).astype(jnp.float32)

    each_slot(live, chunk, kernels_ref, held, sems, add)

    @pl.loop(0, total.shape[0])
    def _(pair):
        value = total[pair]
        high = value.astype(jnp.bfloat16)
        out_ref[0, pair] = high
        out_ref[1, pair] = (value - high.astype(jnp.float32)).astype(jnp.bfloat16)


def weights_across(gathered, blocks, panels, part):
    across = []
    for ref in gathered:
        for b in range(blocks):
            block = ref[pl.ds((part * blocks + b) * panels, panels), :].astype(jnp.float32).T
            across += [block, turned_rows(block)]
    return jnp.concatenate(across, axis=1).astype(jnp.bfloat16)


def adjoint_of(pairs_ref, weights, sources, first, count, out_ref):
    targets = pairs_ref.shape[1] // sources
    width = pairs_ref.shape[3]
    both = jnp.concatenate([weights, weights], axis=1)
    step = 2 if count % 2 == 0 else 1
    for i in range(0, count, step):
        columns = []
        for j in range(step):
            tiles = [pairs_ref[h, t * sources + first + i + j] for h in range(2) for t in range(targets)]
            columns.append(jnp.concatenate(tiles, axis=0))
        rhs = jnp.concatenate(columns, axis=1)
        product = jnp.dot(both, rhs, preferred_element_type=jnp.float32)
        for j in range(step):
            out_ref[i + j] = product[:, j * width : (j + 1) * width]


def outer_kernel(blocks, clusters, panels, pairs_ref, *refs):
    gathered, (lower_ref, upper_ref) = refs[:clusters], refs[clusters:]
    group_blocks = blocks * clusters
    weights = weights_across(gathered, blocks, panels, 3)
    adjoint_of(pairs_ref, weights, 3 * group_blocks, 0, group_blocks, lower_ref)
    adjoint_of(pairs_ref, weights, 3 * group_blocks, 2 * group_blocks, group_blocks, upper_ref)


def inner_kernel(blocks, clusters, panels, pairs_ref, *refs):
    gathered, (potential_ref, middle_ref) = refs[:clusters], refs[clusters:]
    group_blocks = blocks * clusters
    sources = 3 * group_blocks
    weights = weights_across(gathered, blocks, panels, 3)
    adjoint_of(pairs_ref, weights, sources, group_blocks, group_blocks, middle_ref)
    stack = []
    for offset in range(3):
        for ref in gathered:
            for b in range(blocks):
                block = ref[pl.ds((offset * blocks + b) * panels, panels), :]
                stack += [block, turned(block)]
    stack = jnp.concatenate(stack, axis=0)
    for t in range(group_blocks):
        halves = []
        for h in range(2):
            tiles = []
            for s in range(sources):
                tiles += [pairs_ref[h, t * sources + s, :panels], pairs_ref[h, t * sources + s, panels:]]
            halves.append(jnp.concatenate(tiles, axis=1))
        product = jnp.dot(jnp.concatenate(halves, axis=0), stack, preferred_element_type=jnp.float32)
        potential_ref[t] = product[:panels] + product[panels:]


def slots_kernel(blocks, clusters, panels, chunk, live_ref, target_ref, source_ref, kernels_ref, *refs):
    gathered, rest = refs[:clusters], refs[clusters:]
    potential_ref, adjoint_ref, held, stack, across, sems = rest
    live = live_ref[0]
    group_blocks = blocks * clusters
    start_fetch(live, chunk, kernels_ref, held, sems)
    potential_ref[...] = jnp.zeros(potential_ref.shape, potential_ref.dtype)
    adjoint_ref[...] = jnp.zeros(adjoint_ref.shape, adjoint_ref.dtype)
    for k, ref in enumerate(gathered):
        for b in range(blocks):
            for offset in range(3):
                block = ref[pl.ds((offset * blocks + b) * panels, panels), :]
                place = offset * group_blocks + k * blocks + b
                stack[place] = jnp.concatenate([block, turned(block)], axis=0)
            block = ref[pl.ds((3 * blocks + b) * panels, panels), :].astype(jnp.float32).T
            wide = jnp.concatenate([block, turned_rows(block)], axis=1)
            across[k * blocks + b] = wide.astype(jnp.bfloat16)

    def work(slot):
        target, source = slot_place(target_ref, source_ref, slot, blocks, clusters)
        real, imag = held[slot, 0], held[slot, 1]
        potential_ref[target] += jnp.dot(
            jnp.concatenate([real, imag], axis=1), stack[source], preferred_element_type=jnp.float32
        )
        adjoint_ref[source] += jnp.dot(
            across[target], jnp.concatenate([real, imag], axis=0), preferred_element_type=jnp.float32
        )

    each_slot(live, chunk, kernels_ref, held, sems, work)


def finish_kernel(blocks, *refs):
    *parts, potential_ref, adjoint_ref = refs
    total = parts[0][...]
    for part in parts[1:]:
        total = total + part[...]
    panels = total.shape[1]
    for b in range(blocks):
        potential_ref[b * panels : (b + 1) * panels] = total[b]
        adjoint_ref[b * panels : (b + 1) * panels] = total[blocks + b].T


def local(strengths, adjoint_weights, kernels, target_ids, source_ids, live_slots):
    slots, _, panels, _ = kernels.shape
    width = strengths.shape[1]
    blocks = strengths.shape[0] // panels
    clusters = lax.axis_size("clu")
    group_blocks = clusters * blocks
    sources = 3 * group_blocks
    pairs = group_blocks * sources
    chunk = 8 if slots % 8 == 0 else 1
    in_vmem, in_smem = (pl.BlockSpec(memory_space=m) for m in (pltpu.VMEM, pltpu.SMEM))
    params = pltpu.CompilerParams(vmem_limit_bytes=VMEM_BYTES)
    f32, bf16 = jnp.float32, jnp.bfloat16
    slot_args = (live_slots, target_ids, source_ids, kernels)
    slot_specs = [in_smem] * 3 + [pl.BlockSpec(memory_space=pl.ANY)]
    fetch = [pltpu.VMEM(kernels.shape, bf16), pltpu.SemaphoreType.DMA((slots // chunk,))]

    from_lower, from_upper = shifted(strengths, "grp", 1), shifted(strengths, "grp", -1)
    mine = jnp.concatenate([from_lower, strengths, from_upper, adjoint_weights], axis=0)
    gathered = [mine] + [to_partner(mine, "clu", k) for k in range(1, clusters)]

    block_sums = jax.ShapeDtypeStruct((group_blocks, panels, width), f32)
    if pairs <= slots:
        pair_blocks = pl.pallas_call(
            functools.partial(combine_kernel, blocks, clusters, chunk),
            out_shape=jax.ShapeDtypeStruct((2, pairs, 2 * panels, panels), bf16),
            in_specs=slot_specs,
            out_specs=in_vmem,
            scratch_shapes=[fetch[0], pltpu.VMEM((pairs, 2 * panels, panels), f32), fetch[1]],
            compiler_params=params,
            cost_estimate=pl.CostEstimate(
                flops=slots * 2 * panels * panels, bytes_accessed=2 * kernels.size, transcendentals=0
            ),
        )(*slot_args)
        lower, upper = pl.pallas_call(
            functools.partial(outer_kernel, blocks, clusters, panels),
            out_shape=(block_sums, block_sums),
            in_specs=[in_vmem] * (1 + clusters),
            out_specs=(in_vmem, in_vmem),
            compiler_params=params,
        )(pair_blocks, *gathered)
        potential, middle = pl.pallas_call(
            functools.partial(inner_kernel, blocks, clusters, panels),
            out_shape=(block_sums, block_sums),
            in_specs=[in_vmem] * (1 + clusters),
            out_specs=(in_vmem, in_vmem),
            compiler_params=params,
        )(pair_blocks, *gathered)
    else:
        potential, adjoint = pl.pallas_call(
            functools.partial(slots_kernel, blocks, clusters, panels, chunk),
            out_shape=(block_sums, jax.ShapeDtypeStruct((sources, width, panels), f32)),
            in_specs=slot_specs + [in_vmem] * clusters,
            out_specs=(in_vmem, in_vmem),
            scratch_shapes=[
                fetch[0],
                pltpu.VMEM((sources, 2 * panels, width), bf16),
                pltpu.VMEM((group_blocks, width, 2 * panels), bf16),
                fetch[1],
            ],
            compiler_params=params,
        )(*slot_args, *gathered)
        lower, middle, upper = (adjoint[i * group_blocks : (i + 1) * group_blocks] for i in range(3))

    adjoint = middle + shifted(lower, "grp", -1) + shifted(upper, "grp", 1)
    parts = []
    for k in range(clusters):
        rows = slice(k * blocks, (k + 1) * blocks)
        part = jnp.concatenate([potential[rows], adjoint[rows]], axis=0)
        parts.append(to_partner(part, "clu", k) if k else part)
    out = jax.ShapeDtypeStruct((blocks * panels, width), f32)
    return tuple(
        pl.pallas_call(
            functools.partial(finish_kernel, blocks),
            out_shape=(out, out),
            in_specs=[in_vmem] * clusters,
            out_specs=(in_vmem, in_vmem),
            compiler_params=params,
        )(*parts)
    )


def solution(mesh):
    return jax.shard_map(
        local,
        mesh=mesh,
        in_specs=(
            P(("grp", "clu"), None),
            P(("grp", "clu"), None),
            P(("grp", "clu"), None, None, None),
            P(("grp", "clu")),
            P(("grp", "clu")),
            P(("grp", "clu")),
        ),
        out_specs=(P(("grp", "clu"), None), P(("grp", "clu"), None)),
        check_vma=False,
    )
```

```python
import functools

import jax
import jax.numpy as jnp
from jax import lax
from jax.experimental import pallas as pl
from jax.experimental.pallas import tpu as pltpu
from jax.sharding import PartitionSpec as P


def shifted(value, axis, steps):
    count = lax.axis_size(axis)
    first, last = (max(0, -steps), min(count, count - steps))
    return lax.ppermute(value, axis, [(source, source + steps) for source in range(first, last)])


def turned(block):
    half = block.shape[1] // 2
    wide = pltpu.roll(block.astype(jnp.float32), half, axis=1)
    lane = lax.broadcasted_iota(jnp.int32, wide.shape, 1)
    return jnp.where(lane < half, -wide, wide).astype(block.dtype)


def turned_rows(block):
    half = block.shape[0] // 2
    return jnp.concatenate([-block[half:], block[:half]], axis=0)


def place(target_ref, source_ref, slot, group_blocks):
    group = lax.axis_index("grp")
    return target_ref[slot] - group * group_blocks, source_ref[slot] - (group - 1) * group_blocks


def each_slot(chunk, refs, held, ids, id_sems, sems, prepare, work):
    live_ref, *id_refs, kernels_ref = refs
    chunks = held.shape[0] // chunk
    copies = [pltpu.make_async_copy(ref, kept, id_sems.at[i]) for i, (ref, kept) in enumerate(zip(id_refs, ids))]

    def fetch(c):
        rows = pl.ds(c * chunk, chunk)
        return pltpu.make_async_copy(kernels_ref.at[rows], held.at[rows], sems.at[c])

    for copy in copies:
        copy.start()
    for c in range(chunks):
        fetch(c).start()
    prepare()
    for copy in copies:
        copy.wait()
    live = live_ref[0]

    @pl.loop(0, chunks)
    def _(c):
        fetch(c).wait()
        first = c * chunk

        @pl.when(first + chunk <= live)
        def _():
            for i in range(chunk):
                work(first + i)

        @pl.when(first + chunk > live)
        def _():
            @pl.loop(first, jnp.maximum(live, first))
            def _(slot):
                work(slot)


def combine_kernel(group_blocks, chunk, *refs):
    slot_refs, (out_ref, held, total, *ids, id_sems, sems) = refs[:4], refs[4:]
    sources = 3 * group_blocks

    def clear():
        @pl.loop(0, total.shape[0])
        def _(pair):
            total[pair] = jnp.zeros(total.shape[1:], total.dtype)

    def add(slot):
        target, source = place(*ids, slot, group_blocks)
        pair = target * sources + source
        total[pair] += held[slot].reshape(total.shape[1:]).astype(jnp.float32)

    each_slot(chunk, slot_refs, held, ids, id_sems, sems, clear, add)

    @pl.loop(0, total.shape[0])
    def _(pair):
        value = total[pair]
        high = value.astype(jnp.bfloat16)
        out_ref[0, pair] = high
        out_ref[1, pair] = (value - high.astype(jnp.float32)).astype(jnp.bfloat16)


def gather_kernel(lower_ref, middle_ref, upper_ref, weights_ref, _, out_ref):
    rows = middle_ref.shape[0]
    for c in range(out_ref.shape[0]):
        for i, ref in enumerate((lower_ref, middle_ref, upper_ref, weights_ref)):
            out_ref[c, i * rows : (i + 1) * rows] = ref[...]


def part_of(gathered_ref, blocks, panels, part):
    for c in range(gathered_ref.shape[0]):
        for b in range(blocks):
            yield gathered_ref[c, pl.ds((part * blocks + b) * panels, panels), :]


def weights_across(gathered_ref, blocks, panels):
    across = []
    for block in part_of(gathered_ref, blocks, panels, 3):
        block = block.astype(jnp.float32).T
        across += [block, turned_rows(block)]
    return jnp.concatenate(across, axis=1).astype(jnp.bfloat16)


def strengths_stacked(gathered_ref, blocks, panels):
    stack = []
    for offset in range(3):
        for block in part_of(gathered_ref, blocks, panels, offset):
            stack += [block, turned(block)]
    return jnp.concatenate(stack, axis=0)


def adjoint_of(pairs_ref, weights, first, count):
    width = pairs_ref.shape[3]
    targets = weights.shape[1] // pairs_ref.shape[2]
    sources = pairs_ref.shape[1] // targets
    both = jnp.concatenate([weights, weights], axis=1)
    step = 2 if count % 2 == 0 else 1
    for i in range(0, count, step):
        columns = []
        for j in range(step):
            tiles = [pairs_ref[h, t * sources + first + i + j] for h in range(2) for t in range(targets)]
            columns.append(jnp.concatenate(tiles, axis=0))
        product = jnp.dot(both, jnp.concatenate(columns, axis=1), preferred_element_type=jnp.float32)
        for j in range(step):
            yield i + j, product[:, j * width : (j + 1) * width]


def outer_kernel(blocks, panels, pairs_ref, gathered_ref, lower_ref, upper_ref):
    count = lower_ref.shape[0]
    weights = weights_across(gathered_ref, blocks, panels)
    for i, value in adjoint_of(pairs_ref, weights, 0, count):
        lower_ref[i] = value
    for i, value in adjoint_of(pairs_ref, weights, 2 * count, count):
        upper_ref[i] = value


def forward_kernel(blocks, panels, pairs_ref, gathered_ref, potential_ref):
    targets = potential_ref.shape[0]
    sources = pairs_ref.shape[1] // targets
    stack = strengths_stacked(gathered_ref, blocks, panels)
    for t in range(targets):
        halves = []
        for h in range(2):
            tiles = []
            for s in range(sources):
                tiles += [pairs_ref[h, t * sources + s, :panels], pairs_ref[h, t * sources + s, panels:]]
            halves.append(jnp.concatenate(tiles, axis=1))
        product = jnp.dot(jnp.concatenate(halves, axis=0), stack, preferred_element_type=jnp.float32)
        potential_ref[t] = product[:panels] + product[panels:]


def middle_kernel(blocks, panels, pairs_ref, gathered_ref, potential_ref, above_ref, below_ref, out_ref):
    count = potential_ref.shape[0]
    weights = weights_across(gathered_ref, blocks, panels)
    for i, value in adjoint_of(pairs_ref, weights, count, count):
        owner, b = i // blocks, i % blocks
        out_ref[owner, b] = potential_ref[i]
        out_ref[owner, blocks + b] = value + above_ref[i] + below_ref[i]


def slots_kernel(blocks, panels, chunk, *refs):
    slot_refs, gathered_ref, rest = refs[:4], refs[4], refs[5:]
    potential_ref, adjoint_ref, held, stack, across, *ids, id_sems, sems = rest
    group_blocks = potential_ref.shape[0]

    def prepare():
        potential_ref[...] = jnp.zeros(potential_ref.shape, potential_ref.dtype)
        adjoint_ref[...] = jnp.zeros(adjoint_ref.shape, adjoint_ref.dtype)
        for offset in range(3):
            for i, block in enumerate(part_of(gathered_ref, blocks, panels, offset)):
                stack[offset * group_blocks + i] = jnp.concatenate([block, turned(block)], axis=0)
        for i, block in enumerate(part_of(gathered_ref, blocks, panels, 3)):
            block = block.astype(jnp.float32).T
            across[i] = jnp.concatenate([block, turned_rows(block)], axis=1).astype(jnp.bfloat16)

    def work(slot):
        target, source = place(*ids, slot, group_blocks)
        real, imag = held[slot, 0], held[slot, 1]
        potential_ref[target] += jnp.dot(
            jnp.concatenate([real, imag], axis=1), stack[source], preferred_element_type=jnp.float32
        )
        adjoint_ref[source] += jnp.dot(
            across[target], jnp.concatenate([real, imag], axis=0), preferred_element_type=jnp.float32
        )

    each_slot(chunk, slot_refs, held, ids, id_sems, sems, prepare, work)


def finish_kernel(blocks, parts_ref, potential_ref, adjoint_ref):
    total = parts_ref[0]
    for c in range(1, parts_ref.shape[0]):
        total = total + parts_ref[c]
    panels = total.shape[1]
    for b in range(blocks):
        potential_ref[b * panels : (b + 1) * panels] = total[b]
        adjoint_ref[b * panels : (b + 1) * panels] = total[blocks + b].T


def local(strengths, adjoint_weights, kernels, target_ids, source_ids, live_slots):
    slots, _, panels, _ = kernels.shape
    width = strengths.shape[1]
    blocks = strengths.shape[0] // panels
    clusters = lax.axis_size("clu")
    group_blocks = clusters * blocks
    sources = 3 * group_blocks
    pairs = group_blocks * sources
    chunk = 8 if slots % 8 == 0 else 1
    in_vmem, in_smem, in_hbm = (pl.BlockSpec(memory_space=m) for m in (pltpu.VMEM, pltpu.SMEM, pltpu.HBM))
    f32, bf16 = jnp.float32, jnp.bfloat16
    slot_args = (live_slots,) + tuple(
        pltpu.with_memory_space_constraint(x, pltpu.HBM) for x in (target_ids, source_ids, kernels)
    )
    held = pltpu.VMEM(kernels.shape, bf16)
    fetch = [
        pltpu.SMEM(target_ids.shape, jnp.int32),
        pltpu.SMEM(source_ids.shape, jnp.int32),
        pltpu.SemaphoreType.DMA((2,)),
        pltpu.SemaphoreType.DMA((slots // chunk,)),
    ]

    def call(body, shapes, args, specs=None, scratch=(), mib=8, flops=0):
        single = not isinstance(shapes, tuple)
        return pl.pallas_call(
            body,
            out_shape=shapes,
            in_specs=specs or [in_vmem] * len(args),
            out_specs=in_vmem if single else (in_vmem,) * len(shapes),
            scratch_shapes=scratch,
            compiler_params=pltpu.CompilerParams(vmem_limit_bytes=mib << 20),
            cost_estimate=pl.CostEstimate(flops=flops, bytes_accessed=1 << 20, transcendentals=0),
        )(*args)

    def shape(*dims, kind=f32):
        return jax.ShapeDtypeStruct(dims, kind)

    def with_halo(token):
        from_lower, from_upper = shifted(strengths, "grp", 1), shifted(strengths, "grp", -1)
        mine = call(
            gather_kernel,
            shape(clusters, 4 * blocks * panels, width, kind=bf16),
            (from_lower, strengths, from_upper, adjoint_weights, token),
            [in_vmem] * 4 + [in_hbm],
        )
        return lax.all_to_all(mine, "clu", 0, 0, tiled=True)

    block_sums = shape(group_blocks, panels, width)
    if pairs <= slots:
        pair_blocks = call(
            functools.partial(combine_kernel, group_blocks, chunk),
            pltpu.VMEM((2, pairs, 2 * panels, panels), bf16),
            slot_args,
            [in_smem] + [in_hbm] * 3,
            [held, pltpu.VMEM((pairs, 2 * panels, panels), f32), *fetch],
            mib=28,
            flops=1 << 30,
        )
        gathered = with_halo(pair_blocks)
        kept = pltpu.with_memory_space_constraint(pair_blocks, pltpu.VMEM)
        lower, upper = call(
            functools.partial(outer_kernel, blocks, panels), (block_sums, block_sums), (kept, gathered), flops=1 << 30
        )
        potential = call(
            functools.partial(forward_kernel, blocks, panels), block_sums, (kept, gathered), flops=1 << 30
        )
        above, below = shifted(lower, "grp", -1), shifted(upper, "grp", 1)
        parts = call(
            functools.partial(middle_kernel, blocks, panels),
            shape(clusters, 2 * blocks, panels, width),
            (kept, gathered, potential, above, below),
        )
    else:
        gathered = with_halo(strengths)
        potential, adjoint = call(
            functools.partial(slots_kernel, blocks, panels, chunk),
            (block_sums, shape(sources, width, panels)),
            (*slot_args, gathered),
            [in_smem] + [in_hbm] * 3 + [in_vmem],
            [
                held,
                pltpu.VMEM((sources, 2 * panels, width), bf16),
                pltpu.VMEM((group_blocks, width, 2 * panels), bf16),
                *fetch,
            ],
            mib=40,
        )
        lower, middle, upper = (adjoint[i * group_blocks : (i + 1) * group_blocks] for i in range(3))
        adjoint = middle + shifted(lower, "grp", -1) + shifted(upper, "grp", 1)
        split = (clusters, blocks, panels, width)
        parts = jnp.concatenate([potential.reshape(split), adjoint.reshape(split)], axis=1)

    parts = lax.all_to_all(parts, "clu", 0, 0, tiled=True)
    out = shape(blocks * panels, width)
    return tuple(call(functools.partial(finish_kernel, blocks), (out, out), (parts,)))


def solution(mesh):
    return jax.shard_map(
        local,
        mesh=mesh,
        in_specs=(
            P(("grp", "clu"), None),
            P(("grp", "clu"), None),
            P(("grp", "clu"), None, None, None),
            P(("grp", "clu")),
            P(("grp", "clu")),
            P(("grp", "clu")),
        ),
        out_specs=(P(("grp", "clu"), None), P(("grp", "clu"), None)),
        check_vma=False,
    )
```

```python
import functools

import jax
import jax.numpy as jnp
from jax import lax
from jax.experimental import pallas as pl
from jax.experimental.pallas import tpu as pltpu
from jax.sharding import PartitionSpec as P


def exchange(value, axis, step):
    return lax.ppermute(value, axis, [(i, i ^ step) for i in range(lax.axis_size(axis))])


def exchange_beside(value, axis, first):
    pairs = [(i, i + 1) for i in range(first, lax.axis_size(axis) - 1, 2)]
    return lax.ppermute(value, axis, pairs + [(j, i) for i, j in pairs])


def turned(block):
    half = block.shape[1] // 2
    wide = pltpu.roll(block.astype(jnp.float32), half, axis=1)
    lane = lax.broadcasted_iota(jnp.int32, wide.shape, 1)
    return jnp.where(lane < half, -wide, wide).astype(block.dtype)


def turned_rows(block):
    half = block.shape[0] // 2
    return jnp.concatenate([-block[half:], block[:half]], axis=0)


def place(target_ref, source_ref, slot, group_blocks, blocks):
    group, mine = lax.axis_index("grp"), lax.axis_index("clu") * blocks
    target = (target_ref[slot] - group * group_blocks) ^ mine
    source = (source_ref[slot] - (group - 1) * group_blocks) ^ mine
    offset = lax.div(source, group_blocks) - 1
    return target, jnp.where(group % 2 == 0, source - 2 * offset * group_blocks, source)


def each_slot(chunk, refs, held, ids, id_sems, sems, prepare, work):
    live_ref, *id_refs, kernels_ref = refs
    chunks = held.shape[0] // chunk
    copies = [pltpu.make_async_copy(ref, kept, id_sems.at[i]) for i, (ref, kept) in enumerate(zip(id_refs, ids))]

    def fetch(c):
        rows = pl.ds(c * chunk, chunk)
        return pltpu.make_async_copy(kernels_ref.at[rows], held.at[rows], sems.at[c])

    for copy in copies:
        copy.start()
    for c in range(chunks):
        fetch(c).start()
    prepare()
    for copy in copies:
        copy.wait()
    live = live_ref[0]

    @pl.loop(0, chunks)
    def _(c):
        fetch(c).wait()
        first = c * chunk

        @pl.when(first + chunk <= live)
        def _():
            for i in range(chunk):
                work(first + i)

        @pl.when(first + chunk > live)
        def _():
            @pl.loop(first, jnp.maximum(live, first))
            def _(slot):
                work(slot)


def combine_kernel(group_blocks, blocks, chunk, *refs):
    slot_refs, (total, held, *ids, id_sems, sems) = refs[:4], refs[4:]
    sources = 3 * group_blocks

    def clear():
        @pl.loop(0, total.shape[0])
        def _(pair):
            total[pair] = jnp.zeros(total.shape[1:], total.dtype)

    def add(slot):
        target, source = place(*ids, slot, group_blocks, blocks)
        pair = target * sources + source
        total[pair] += held[slot].reshape(total.shape[1:]).astype(jnp.float32)

    each_slot(chunk, slot_refs, held, ids, id_sems, sems, clear, add)


def split_kernel(total, out_ref):
    @pl.loop(0, total.shape[0])
    def _(pair):
        value = total[pair]
        high = value.astype(jnp.bfloat16)
        out_ref[0, pair] = high
        out_ref[1, pair] = (value - high.astype(jnp.float32)).astype(jnp.bfloat16)


def join_kernel(first_ref, own_ref, second_ref, weights_ref, _, out_ref):
    rows = own_ref.shape[0]
    for i, ref in enumerate((first_ref, own_ref, second_ref, weights_ref)):
        out_ref[i * rows : (i + 1) * rows] = ref[...]


def part_of(gathered, blocks, panels, part):
    for ref in gathered:
        for b in range(blocks):
            yield ref[pl.ds((part * blocks + b) * panels, panels), :]


def weights_across(gathered, blocks, panels):
    across = []
    for block in part_of(gathered, blocks, panels, 3):
        block = block.astype(jnp.float32).T
        across += [block, turned_rows(block)]
    return jnp.concatenate(across, axis=1).astype(jnp.bfloat16)


def strengths_stacked(gathered, blocks, panels):
    stack = []
    for offset in range(3):
        for block in part_of(gathered, blocks, panels, offset):
            stack += [block, turned(block)]
    return jnp.concatenate(stack, axis=0)


def adjoint_of(pairs_ref, weights, first, count):
    width = pairs_ref.shape[3]
    targets = weights.shape[1] // pairs_ref.shape[2]
    sources = pairs_ref.shape[1] // targets
    both = jnp.concatenate([weights, weights], axis=1)
    step = 2 if count % 2 == 0 else 1
    for i in range(0, count, step):
        columns = []
        for j in range(step):
            tiles = [pairs_ref[h, t * sources + first + i + j] for h in range(2) for t in range(targets)]
            columns.append(jnp.concatenate(tiles, axis=0))
        product = jnp.dot(both, jnp.concatenate(columns, axis=1), preferred_element_type=jnp.float32)
        for j in range(step):
            yield i + j, product[:, j * width : (j + 1) * width]


def outer_kernel(blocks, panels, pairs_ref, *refs):
    *gathered, first_ref, second_ref = refs
    count = first_ref.shape[0]
    weights = weights_across(gathered, blocks, panels)
    for i, value in adjoint_of(pairs_ref, weights, 0, count):
        first_ref[i] = value
    for i, value in adjoint_of(pairs_ref, weights, 2 * count, count):
        second_ref[i] = value


def forward_kernel(blocks, panels, pairs_ref, *refs):
    *gathered, potential_ref = refs
    targets = potential_ref.shape[0]
    sources = pairs_ref.shape[1] // targets
    stack = strengths_stacked(gathered, blocks, panels)
    for t in range(targets):
        halves = []
        for h in range(2):
            tiles = []
            for s in range(sources):
                tiles += [pairs_ref[h, t * sources + s, :panels], pairs_ref[h, t * sources + s, panels:]]
            halves.append(jnp.concatenate(tiles, axis=1))
        product = jnp.dot(jnp.concatenate(halves, axis=0), stack, preferred_element_type=jnp.float32)
        potential_ref[t] = product[:panels] + product[panels:]


def middle_kernel(blocks, panels, clusters, pairs_ref, *refs):
    gathered, (potential_ref, first_ref, second_ref, *outs) = refs[:clusters], refs[clusters:]
    count = potential_ref.shape[0]
    weights = weights_across(gathered, blocks, panels)
    for i, value in adjoint_of(pairs_ref, weights, count, count):
        out_ref, b = outs[i // blocks], i % blocks
        out_ref[b] = potential_ref[i]
        out_ref[blocks + b] = value + first_ref[i] + second_ref[i]


def slots_kernel(blocks, panels, clusters, chunk, *refs):
    slot_refs, gathered, rest = refs[:4], refs[4 : 4 + clusters], refs[4 + clusters :]
    potential_ref, adjoint_ref, held, stack, across, *ids, id_sems, sems = rest
    group_blocks = potential_ref.shape[0]

    def prepare():
        potential_ref[...] = jnp.zeros(potential_ref.shape, potential_ref.dtype)
        adjoint_ref[...] = jnp.zeros(adjoint_ref.shape, adjoint_ref.dtype)
        for offset in range(3):
            for i, block in enumerate(part_of(gathered, blocks, panels, offset)):
                stack[offset * group_blocks + i] = jnp.concatenate([block, turned(block)], axis=0)
        for i, block in enumerate(part_of(gathered, blocks, panels, 3)):
            block = block.astype(jnp.float32).T
            across[i] = jnp.concatenate([block, turned_rows(block)], axis=1).astype(jnp.bfloat16)

    def work(slot):
        target, source = place(*ids, slot, group_blocks, blocks)
        real, imag = held[slot, 0], held[slot, 1]
        potential_ref[target] += jnp.dot(
            jnp.concatenate([real, imag], axis=1), stack[source], preferred_element_type=jnp.float32
        )
        adjoint_ref[source] += jnp.dot(
            across[target], jnp.concatenate([real, imag], axis=0), preferred_element_type=jnp.float32
        )

    each_slot(chunk, slot_refs, held, ids, id_sems, sems, prepare, work)


def finish_kernel(blocks, *refs):
    *parts, potential_ref, adjoint_ref = refs
    total = parts[0][...]
    for part in parts[1:]:
        total = total + part[...]
    panels = total.shape[1]
    for b in range(blocks):
        potential_ref[b * panels : (b + 1) * panels] = total[b]
        adjoint_ref[b * panels : (b + 1) * panels] = total[blocks + b].T


def local(strengths, adjoint_weights, kernels, target_ids, source_ids, live_slots):
    slots, _, panels, _ = kernels.shape
    width = strengths.shape[1]
    blocks = strengths.shape[0] // panels
    clusters = lax.axis_size("clu")
    group_blocks = clusters * blocks
    sources = 3 * group_blocks
    pairs = group_blocks * sources
    chunk = 8 if slots % 8 == 0 else 1
    in_vmem, in_smem, in_hbm = (pl.BlockSpec(memory_space=m) for m in (pltpu.VMEM, pltpu.SMEM, pltpu.HBM))
    f32, bf16 = jnp.float32, jnp.bfloat16
    slot_args = (live_slots,) + tuple(
        pltpu.with_memory_space_constraint(x, pltpu.HBM) for x in (target_ids, source_ids, kernels)
    )
    held = pltpu.VMEM(kernels.shape, bf16)
    fetch = [
        pltpu.SMEM(target_ids.shape, jnp.int32),
        pltpu.SMEM(source_ids.shape, jnp.int32),
        pltpu.SemaphoreType.DMA((2,)),
        pltpu.SemaphoreType.DMA((slots // chunk,)),
    ]

    def call(body, shapes, args, specs=None, scratch=(), mib=8, flops=0):
        single = not isinstance(shapes, tuple)
        return pl.pallas_call(
            body,
            out_shape=shapes,
            in_specs=specs or [in_vmem] * len(args),
            out_specs=in_vmem if single else (in_vmem,) * len(shapes),
            scratch_shapes=scratch,
            compiler_params=pltpu.CompilerParams(vmem_limit_bytes=mib << 20),
            cost_estimate=pl.CostEstimate(flops=flops, bytes_accessed=1 << 20, transcendentals=0),
        )(*args)

    def shape(*dims, kind=f32):
        return jax.ShapeDtypeStruct(dims, kind)

    def with_halo(token):
        first, second = exchange_beside(strengths, "grp", 0), exchange_beside(strengths, "grp", 1)
        mine = call(
            join_kernel,
            shape(4 * blocks * panels, width, kind=bf16),
            (first, strengths, second, adjoint_weights, token),
            [in_vmem] * 4 + [in_hbm],
        )
        return [mine] + [exchange(mine, "clu", k) for k in range(1, clusters)]

    block_sums = shape(group_blocks, panels, width)
    if pairs <= slots:
        total = call(
            functools.partial(combine_kernel, group_blocks, blocks, chunk),
            pltpu.VMEM((pairs, 2 * panels, panels), f32),
            slot_args,
            [in_smem] + [in_hbm] * 3,
            [held, *fetch],
            mib=20,
            flops=1 << 30,
        )
        gathered = with_halo(total)
        total = pltpu.with_memory_space_constraint(total, pltpu.VMEM)
        kept = call(split_kernel, pltpu.VMEM((2, *total.shape), bf16), (total,), flops=1 << 30)
        kept = pltpu.with_memory_space_constraint(kept, pltpu.VMEM)
        first, second = call(
            functools.partial(outer_kernel, blocks, panels),
            (block_sums, block_sums),
            (kept, *gathered),
            flops=1 << 30,
        )
        potential = call(
            functools.partial(forward_kernel, blocks, panels), block_sums, (kept, *gathered), flops=1 << 30
        )
        first, second = exchange_beside(first, "grp", 0), exchange_beside(second, "grp", 1)
        parts = call(
            functools.partial(middle_kernel, blocks, panels, clusters),
            (shape(2 * blocks, panels, width),) * clusters,
            (kept, *gathered, potential, first, second),
        )
    else:
        gathered = with_halo(strengths)
        potential, adjoint = call(
            functools.partial(slots_kernel, blocks, panels, clusters, chunk),
            (block_sums, shape(sources, width, panels)),
            (*slot_args, *gathered),
            [in_smem] + [in_hbm] * 3 + [in_vmem] * clusters,
            [
                held,
                pltpu.VMEM((sources, 2 * panels, width), bf16),
                pltpu.VMEM((group_blocks, width, 2 * panels), bf16),
                *fetch,
            ],
            mib=40,
        )
        first, middle, second = (adjoint[i * group_blocks : (i + 1) * group_blocks] for i in range(3))
        adjoint = middle + exchange_beside(first, "grp", 0) + exchange_beside(second, "grp", 1)
        owned = [slice(k * blocks, (k + 1) * blocks) for k in range(clusters)]
        parts = [jnp.concatenate([potential[rows], adjoint[rows]], axis=0) for rows in owned]

    parts = [parts[0]] + [exchange(parts[k], "clu", k) for k in range(1, clusters)]
    out = shape(blocks * panels, width)
    return tuple(call(functools.partial(finish_kernel, blocks), (out, out), parts))


def solution(mesh):
    return jax.shard_map(
        local,
        mesh=mesh,
        in_specs=(
            P(("grp", "clu"), None),
            P(("grp", "clu"), None),
            P(("grp", "clu"), None, None, None),
            P(("grp", "clu")),
            P(("grp", "clu")),
            P(("grp", "clu")),
        ),
        out_specs=(P(("grp", "clu"), None), P(("grp", "clu"), None)),
        check_vma=False,
    )
```

```python
import functools

import jax
import jax.numpy as jnp
from jax import lax
from jax.experimental import pallas as pl
from jax.experimental.pallas import tpu as pltpu
from jax.sharding import PartitionSpec as P


def exchange(value, axis, step):
    return lax.ppermute(value, axis, [(i, i ^ step) for i in range(lax.axis_size(axis))])


def exchange_beside(value, axis, first):
    pairs = [(i, i + 1) for i in range(first, lax.axis_size(axis) - 1, 2)]
    return lax.ppermute(value, axis, pairs + [(j, i) for i, j in pairs])


def turned(block):
    half = block.shape[1] // 2
    wide = pltpu.roll(block.astype(jnp.float32), half, axis=1)
    lane = lax.broadcasted_iota(jnp.int32, wide.shape, 1)
    return jnp.where(lane < half, -wide, wide).astype(block.dtype)


def turned_rows(block):
    half = block.shape[0] // 2
    return jnp.concatenate([-block[half:], block[:half]], axis=0)


def place(target_ref, source_ref, slot, group_blocks, blocks):
    group, mine = lax.axis_index("grp"), lax.axis_index("clu") * blocks
    target = (target_ref[slot] - group * group_blocks) ^ mine
    source = (source_ref[slot] - (group - 1) * group_blocks) ^ mine
    offset = lax.div(source, group_blocks) - 1
    return target, jnp.where(group % 2 == 0, source - 2 * offset * group_blocks, source)


def each_slot(chunk, refs, held, ids, id_sems, sems, prepare, work):
    live_ref, *id_refs, kernels_ref = refs
    chunks = held.shape[0] // chunk
    copies = [pltpu.make_async_copy(ref, kept, id_sems.at[i]) for i, (ref, kept) in enumerate(zip(id_refs, ids))]

    def fetch(c):
        rows = pl.ds(c * chunk, chunk)
        return pltpu.make_async_copy(kernels_ref.at[rows], held.at[rows], sems.at[c])

    for copy in copies:
        copy.start()
    for c in range(chunks):
        fetch(c).start()
    prepare()
    for copy in copies:
        copy.wait()
    live = live_ref[0]

    @pl.loop(0, chunks)
    def _(c):
        fetch(c).wait()
        first = c * chunk

        @pl.when(first + chunk <= live)
        def _():
            for i in range(chunk):
                work(first + i)

        @pl.when(first + chunk > live)
        def _():
            @pl.loop(first, jnp.maximum(live, first))
            def _(slot):
                work(slot)


def combine_kernel(group_blocks, blocks, chunk, *refs):
    slot_refs, (total, held, *ids, id_sems, sems) = refs[:4], refs[4:]
    sources = 3 * group_blocks

    def clear():
        @pl.loop(0, total.shape[0])
        def _(pair):
            total[pair] = jnp.zeros(total.shape[1:], total.dtype)

    def add(slot):
        target, source = place(*ids, slot, group_blocks, blocks)
        pair = target * sources + source
        total[pair] += held[slot].reshape(total.shape[1:]).astype(jnp.float32)

    each_slot(chunk, slot_refs, held, ids, id_sems, sems, clear, add)


def split_kernel(blocks, panels, _, total, *refs):
    *gathered, out_ref, across_ref = refs

    @pl.loop(0, total.shape[0])
    def _(pair):
        value = total[pair]
        high = value.astype(jnp.bfloat16)
        out_ref[0, pair] = high
        out_ref[1, pair] = (value - high.astype(jnp.float32)).astype(jnp.bfloat16)

    for i, block in enumerate(part_of(gathered, blocks, panels, 1)):
        across_ref[:, 2 * i * panels : 2 * (i + 1) * panels] = crossed(block)


def pack_kernel(strengths_ref, weights_ref, out_ref, sems):
    rows = strengths_ref.shape[0]
    copies = [
        pltpu.make_async_copy(ref, out_ref.at[pl.ds(i * rows, rows)], sems.at[i])
        for i, ref in enumerate((strengths_ref, weights_ref))
    ]
    for copy in copies:
        copy.start()
    for copy in copies:
        copy.wait()


def group_kernel(blocks, panels, *refs):
    *gathered, _, out_ref = refs
    for i, block in enumerate(part_of(gathered, blocks, panels, 0)):
        out_ref[i * panels : (i + 1) * panels] = block


def part_of(gathered, blocks, panels, part):
    for ref in gathered:
        for b in range(blocks):
            yield ref[pl.ds((part * blocks + b) * panels, panels), :]


def crossed(block):
    block = block.astype(jnp.float32).T
    return jnp.concatenate([block, turned_rows(block)], axis=1).astype(jnp.bfloat16)


def stacked(block):
    return jnp.concatenate([block, turned(block)], axis=0)


def adjoint_of(pairs_ref, across_ref, first, count):
    width = pairs_ref.shape[3]
    weights = across_ref[...]
    targets = weights.shape[1] // pairs_ref.shape[2]
    sources = pairs_ref.shape[1] // targets
    both = jnp.concatenate([weights, weights], axis=1)
    step = 2 if count % 2 == 0 else 1
    for i in range(0, count, step):
        columns = []
        for j in range(step):
            tiles = [pairs_ref[h, t * sources + first + i + j] for h in range(2) for t in range(targets)]
            columns.append(jnp.concatenate(tiles, axis=0))
        product = jnp.dot(both, jnp.concatenate(columns, axis=1), preferred_element_type=jnp.float32)
        for j in range(step):
            yield i + j, product[:, j * width : (j + 1) * width]


def outer_kernel(pairs_ref, across_ref, first_ref, second_ref):
    count = first_ref.shape[0]
    for i, value in adjoint_of(pairs_ref, across_ref, 0, count):
        first_ref[i] = value
    for i, value in adjoint_of(pairs_ref, across_ref, 2 * count, count):
        second_ref[i] = value


def forward_kernel(pairs_ref, *refs):
    *strengths, potential_ref = refs
    targets, panels = potential_ref.shape[:2]
    sources = pairs_ref.shape[1] // targets
    stack = []
    for ref in strengths:
        stack += [stacked(ref[i : i + panels]) for i in range(0, ref.shape[0], panels)]
    stack = jnp.concatenate(stack, axis=0)
    for t in range(targets):
        halves = []
        for h in range(2):
            tiles = []
            for s in range(sources):
                tiles += [pairs_ref[h, t * sources + s, :panels], pairs_ref[h, t * sources + s, panels:]]
            halves.append(jnp.concatenate(tiles, axis=1))
        product = jnp.dot(jnp.concatenate(halves, axis=0), stack, preferred_element_type=jnp.float32)
        potential_ref[t] = product[:panels] + product[panels:]


def middle_kernel(blocks, pairs_ref, across_ref, potential_ref, first_ref, second_ref, *outs):
    count = potential_ref.shape[0]
    for i, value in adjoint_of(pairs_ref, across_ref, count, count):
        out_ref, b = outs[i // blocks], i % blocks
        out_ref[b] = potential_ref[i]
        out_ref[blocks + b] = value + first_ref[i] + second_ref[i]


def slots_kernel(blocks, panels, clusters, chunk, *refs):
    slot_refs, gathered, refs = refs[:4], refs[4 : 4 + clusters], refs[4 + clusters :]
    strengths, (potential_ref, adjoint_ref, held, stack, across, *ids, id_sems, sems) = refs[:3], refs[3:]
    group_blocks = potential_ref.shape[0]

    def prepare():
        potential_ref[...] = jnp.zeros(potential_ref.shape, potential_ref.dtype)
        adjoint_ref[...] = jnp.zeros(adjoint_ref.shape, adjoint_ref.dtype)
        for offset, ref in enumerate(strengths):
            for i in range(group_blocks):
                stack[offset * group_blocks + i] = stacked(ref[i * panels : (i + 1) * panels])
        for i, block in enumerate(part_of(gathered, blocks, panels, 1)):
            across[i] = crossed(block)

    def work(slot):
        target, source = place(*ids, slot, group_blocks, blocks)
        real, imag = held[slot, 0], held[slot, 1]
        potential_ref[target] += jnp.dot(
            jnp.concatenate([real, imag], axis=1), stack[source], preferred_element_type=jnp.float32
        )
        adjoint_ref[source] += jnp.dot(
            across[target], jnp.concatenate([real, imag], axis=0), preferred_element_type=jnp.float32
        )

    each_slot(chunk, slot_refs, held, ids, id_sems, sems, prepare, work)


def finish_kernel(blocks, *refs):
    *parts, potential_ref, adjoint_ref = refs
    total = parts[0][...]
    for part in parts[1:]:
        total = total + part[...]
    panels = total.shape[1]
    for b in range(blocks):
        potential_ref[b * panels : (b + 1) * panels] = total[b]
        adjoint_ref[b * panels : (b + 1) * panels] = total[blocks + b].T


def local(strengths, adjoint_weights, kernels, target_ids, source_ids, live_slots):
    slots, _, panels, _ = kernels.shape
    width = strengths.shape[1]
    blocks = strengths.shape[0] // panels
    clusters = lax.axis_size("clu")
    group_blocks = clusters * blocks
    sources = 3 * group_blocks
    pairs = group_blocks * sources
    chunk = 8 if slots % 8 == 0 else 1
    in_vmem, in_smem, in_hbm = (pl.BlockSpec(memory_space=m) for m in (pltpu.VMEM, pltpu.SMEM, pltpu.HBM))
    f32, bf16 = jnp.float32, jnp.bfloat16
    slot_args = (live_slots,) + tuple(
        pltpu.with_memory_space_constraint(x, pltpu.HBM) for x in (target_ids, source_ids, kernels)
    )
    held = pltpu.VMEM(kernels.shape, bf16)
    fetch = [
        pltpu.SMEM(target_ids.shape, jnp.int32),
        pltpu.SMEM(source_ids.shape, jnp.int32),
        pltpu.SemaphoreType.DMA((2,)),
        pltpu.SemaphoreType.DMA((slots // chunk,)),
    ]

    def call(body, shapes, args, specs=None, scratch=(), mib=8, flops=0):
        single = not isinstance(shapes, tuple)
        return pl.pallas_call(
            body,
            out_shape=shapes,
            in_specs=specs or [in_vmem] * len(args),
            out_specs=in_vmem if single else (in_vmem,) * len(shapes),
            scratch_shapes=scratch,
            compiler_params=pltpu.CompilerParams(vmem_limit_bytes=mib << 20),
            cost_estimate=pl.CostEstimate(flops=flops, bytes_accessed=1 << 20, transcendentals=0),
        )(*args)

    def shape(*dims, kind=f32):
        return jax.ShapeDtypeStruct(dims, kind)

    mine = call(
        pack_kernel,
        shape(2 * blocks * panels, width, kind=bf16),
        [pltpu.with_memory_space_constraint(x, pltpu.HBM) for x in (strengths, adjoint_weights)],
        [in_hbm] * 2,
        [pltpu.SemaphoreType.DMA((2,))],
    )
    gathered = [mine] + [exchange(mine, "clu", k) for k in range(1, clusters)]

    def group_strengths(token):
        own = call(
            functools.partial(group_kernel, blocks, panels),
            shape(group_blocks * panels, width, kind=bf16),
            (*gathered, token),
            [in_vmem] * clusters + [in_hbm],
        )
        return exchange_beside(own, "grp", 0), own, exchange_beside(own, "grp", 1)

    block_sums = shape(group_blocks, panels, width)
    if pairs <= slots:
        total = call(
            functools.partial(combine_kernel, group_blocks, blocks, chunk),
            pltpu.VMEM((pairs, 2 * panels, panels), f32),
            slot_args,
            [in_smem] + [in_hbm] * 3,
            [held, *fetch],
            mib=20,
            flops=1 << 33,
        )
        first, own, second = group_strengths(total)
        total = pltpu.with_memory_space_constraint(total, pltpu.VMEM)
        kept, across = call(
            functools.partial(split_kernel, blocks, panels),
            (pltpu.VMEM((2, *total.shape), bf16), shape(width, 2 * group_blocks * panels, kind=bf16)),
            (own, total, *gathered),
            [in_hbm] + [in_vmem] * (1 + clusters),
            flops=1 << 33,
        )
        kept = pltpu.with_memory_space_constraint(kept, pltpu.VMEM)
        lower, upper = call(outer_kernel, (block_sums, block_sums), (kept, across), flops=1 << 33)
        potential = call(forward_kernel, block_sums, (kept, first, own, second), flops=1 << 33)
        lower, upper = exchange_beside(lower, "grp", 0), exchange_beside(upper, "grp", 1)
        parts = call(
            functools.partial(middle_kernel, blocks),
            (shape(2 * blocks, panels, width),) * clusters,
            (kept, across, potential, lower, upper),
        )
    else:
        potential, adjoint = call(
            functools.partial(slots_kernel, blocks, panels, clusters, chunk),
            (block_sums, shape(sources, width, panels)),
            (*slot_args, *gathered, *group_strengths(strengths)),
            [in_smem] + [in_hbm] * 3 + [in_vmem] * (clusters + 3),
            [
                held,
                pltpu.VMEM((sources, 2 * panels, width), bf16),
                pltpu.VMEM((group_blocks, width, 2 * panels), bf16),
                *fetch,
            ],
            mib=40,
        )
        first, middle, second = (adjoint[i * group_blocks : (i + 1) * group_blocks] for i in range(3))
        adjoint = middle + exchange_beside(first, "grp", 0) + exchange_beside(second, "grp", 1)
        owned = [slice(k * blocks, (k + 1) * blocks) for k in range(clusters)]
        parts = [jnp.concatenate([potential[rows], adjoint[rows]], axis=0) for rows in owned]

    parts = [parts[0]] + [exchange(parts[k], "clu", k) for k in range(1, clusters)]
    out = shape(blocks * panels, width)
    return tuple(call(functools.partial(finish_kernel, blocks), (out, out), parts))


def solution(mesh):
    return jax.shard_map(
        local,
        mesh=mesh,
        in_specs=(
            P(("grp", "clu"), None),
            P(("grp", "clu"), None),
            P(("grp", "clu"), None, None, None),
            P(("grp", "clu")),
            P(("grp", "clu")),
            P(("grp", "clu")),
        ),
        out_specs=(P(("grp", "clu"), None), P(("grp", "clu"), None)),
        check_vma=False,
    )
```

```python
import functools

import jax
import jax.numpy as jnp
from jax import lax
from jax.experimental import pallas as pl
from jax.experimental.pallas import tpu as pltpu
from jax.sharding import PartitionSpec as P


def exchange(value, axis, step):
    return lax.ppermute(value, axis, [(i, i ^ step) for i in range(lax.axis_size(axis))])


def exchange_beside(value, axis, first):
    pairs = [(i, i + 1) for i in range(first, lax.axis_size(axis) - 1, 2)]
    return lax.ppermute(value, axis, pairs + [(j, i) for i, j in pairs])


def turned(block):
    half = block.shape[1] // 2
    wide = pltpu.roll(block.astype(jnp.float32), half, axis=1)
    lane = lax.broadcasted_iota(jnp.int32, wide.shape, 1)
    return jnp.where(lane < half, -wide, wide).astype(block.dtype)


def turned_rows(block):
    half = block.shape[0] // 2
    return jnp.concatenate([-block[half:], block[:half]], axis=0)


def place(target_ref, source_ref, slot, group_blocks, blocks):
    group, mine = lax.axis_index("grp"), lax.axis_index("clu") * blocks
    target = (target_ref[slot] - group * group_blocks) ^ mine
    source = (source_ref[slot] - (group - 1) * group_blocks) ^ mine
    offset = lax.div(source, group_blocks) - 1
    return target, jnp.where(group % 2 == 0, source - 2 * offset * group_blocks, source)


def each_slot(start, chunk, refs, held, ids, id_sems, sems, prepare, work):
    live_ref, *id_refs, kernels_ref = refs
    chunks = held.shape[0] // chunk
    copies = [pltpu.make_async_copy(ref, kept, id_sems.at[i]) for i, (ref, kept) in enumerate(zip(id_refs, ids))]

    def fetch(c):
        return pltpu.make_async_copy(
            kernels_ref.at[pl.ds(start + c * chunk, chunk)], held.at[pl.ds(c * chunk, chunk)], sems.at[c]
        )

    for copy in copies:
        copy.start()
    for c in range(chunks):
        fetch(c).start()
    prepare()
    for copy in copies:
        copy.wait()
    live = live_ref[0] - start

    @pl.loop(0, chunks)
    def _(c):
        fetch(c).wait()
        first = c * chunk

        @pl.when(first + chunk <= live)
        def _():
            for i in range(chunk):
                work(start + first + i, held.at[first + i])

        @pl.when(first + chunk > live)
        def _():
            @pl.loop(first, jnp.maximum(live, first))
            def _(i):
                work(start + i, held.at[i])


def combine_kernel(group_blocks, blocks, start, chunk, *refs):
    slot_refs, (_, total, held, *ids, id_sems, sems) = refs[:4], refs[4:]
    sources = 3 * group_blocks

    def clear():
        @pl.loop(0, total.shape[0])
        def _(pair):
            total[pair] = jnp.zeros(total.shape[1:], total.dtype)

    def add(slot, block):
        target, source = place(*ids, slot, group_blocks, blocks)
        pair = target * sources + source
        total[pair] += block[...].reshape(total.shape[1:]).astype(jnp.float32)

    each_slot(start, chunk, slot_refs, held, ids, id_sems, sems, clear, add)


def split_kernel(blocks, panels, _, early, late, *refs):
    *gathered, out_ref, across_ref = refs

    @pl.loop(0, early.shape[0])
    def _(pair):
        value = early[pair] + late[pair]
        high = value.astype(jnp.bfloat16)
        out_ref[0, pair] = high
        out_ref[1, pair] = (value - high.astype(jnp.float32)).astype(jnp.bfloat16)

    for i, block in enumerate(part_of(gathered, blocks, panels, 1)):
        across_ref[:, 2 * i * panels : 2 * (i + 1) * panels] = crossed(block)


def join_kernel(_, *refs):
    *parts, out_ref = refs
    rows = parts[0].shape[0]
    for i, ref in enumerate(parts):
        out_ref[i * rows : (i + 1) * rows] = ref[...]


def group_kernel(blocks, panels, _, *refs):
    *gathered, out_ref = refs
    for i, block in enumerate(part_of(gathered, blocks, panels, 0)):
        out_ref[i * panels : (i + 1) * panels] = block


def part_of(gathered, blocks, panels, part):
    for ref in gathered:
        for b in range(blocks):
            yield ref[pl.ds((part * blocks + b) * panels, panels), :]


def strengths_of(first_ref, gathered, blocks, panels):
    for i in range(0, first_ref.shape[0], panels):
        yield first_ref[i : i + panels]
    yield from part_of(gathered, blocks, panels, 0)
    yield from part_of(gathered, blocks, panels, 2)


def crossed(block):
    block = block.astype(jnp.float32).T
    return jnp.concatenate([block, turned_rows(block)], axis=1).astype(jnp.bfloat16)


def stacked(block):
    return jnp.concatenate([block, turned(block)], axis=0)


def adjoint_of(pairs_ref, across_ref, first, count):
    width = pairs_ref.shape[3]
    weights = across_ref[...]
    targets = weights.shape[1] // pairs_ref.shape[2]
    sources = pairs_ref.shape[1] // targets
    both = jnp.concatenate([weights, weights], axis=1)
    step = 2 if count % 2 == 0 else 1
    for i in range(0, count, step):
        columns = []
        for j in range(step):
            tiles = [pairs_ref[h, t * sources + first + i + j] for h in range(2) for t in range(targets)]
            columns.append(jnp.concatenate(tiles, axis=0))
        product = jnp.dot(both, jnp.concatenate(columns, axis=1), preferred_element_type=jnp.float32)
        for j in range(step):
            yield i + j, product[:, j * width : (j + 1) * width]


def outer_kernel(pairs_ref, across_ref, first_ref, second_ref):
    count = first_ref.shape[0]
    for i, value in adjoint_of(pairs_ref, across_ref, 0, count):
        first_ref[i] = value
    for i, value in adjoint_of(pairs_ref, across_ref, 2 * count, count):
        second_ref[i] = value


def inner_kernel(blocks, pairs_ref, across_ref, first_ref, *refs):
    *gathered, potential_ref, middle_ref = refs
    targets, panels = potential_ref.shape[:2]
    sources = pairs_ref.shape[1] // targets
    stack = jnp.concatenate([stacked(x) for x in strengths_of(first_ref, gathered, blocks, panels)], axis=0)
    for t in range(targets):
        halves = []
        for h in range(2):
            tiles = []
            for s in range(sources):
                tiles += [pairs_ref[h, t * sources + s, :panels], pairs_ref[h, t * sources + s, panels:]]
            halves.append(jnp.concatenate(tiles, axis=1))
        product = jnp.dot(jnp.concatenate(halves, axis=0), stack, preferred_element_type=jnp.float32)
        potential_ref[t] = product[:panels] + product[panels:]
    for i, value in adjoint_of(pairs_ref, across_ref, targets, targets):
        middle_ref[i] = value


def parts_kernel(blocks, potential_ref, middle_ref, first_ref, second_ref, *outs):
    for i in range(potential_ref.shape[0]):
        out_ref, b = outs[i // blocks], i % blocks
        out_ref[b] = potential_ref[i]
        out_ref[blocks + b] = middle_ref[i] + first_ref[i] + second_ref[i]


def slots_kernel(blocks, panels, chunk, *refs):
    slot_refs, (first_ref, *gathered), refs = refs[:4], refs[4:-9], refs[-9:]
    potential_ref, adjoint_ref, held, stack, across, *ids, id_sems, sems = refs
    group_blocks = potential_ref.shape[0]

    def prepare():
        potential_ref[...] = jnp.zeros(potential_ref.shape, potential_ref.dtype)
        adjoint_ref[...] = jnp.zeros(adjoint_ref.shape, adjoint_ref.dtype)
        for i, block in enumerate(strengths_of(first_ref, gathered, blocks, panels)):
            stack[i] = stacked(block)
        for i, block in enumerate(part_of(gathered, blocks, panels, 1)):
            across[i] = crossed(block)

    def work(slot, block):
        target, source = place(*ids, slot, group_blocks, blocks)
        real, imag = block[0], block[1]
        potential_ref[target] += jnp.dot(
            jnp.concatenate([real, imag], axis=1), stack[source], preferred_element_type=jnp.float32
        )
        adjoint_ref[source] += jnp.dot(
            across[target], jnp.concatenate([real, imag], axis=0), preferred_element_type=jnp.float32
        )

    each_slot(0, chunk, slot_refs, held, ids, id_sems, sems, prepare, work)


def finish_kernel(blocks, *refs):
    *parts, potential_ref, adjoint_ref = refs
    total = parts[0][...]
    for part in parts[1:]:
        total = total + part[...]
    panels = total.shape[1]
    for b in range(blocks):
        potential_ref[b * panels : (b + 1) * panels] = total[b]
        adjoint_ref[b * panels : (b + 1) * panels] = total[blocks + b].T


def local(strengths, adjoint_weights, kernels, target_ids, source_ids, live_slots):
    slots, _, panels, _ = kernels.shape
    width = strengths.shape[1]
    blocks = strengths.shape[0] // panels
    clusters = lax.axis_size("clu")
    group_blocks = clusters * blocks
    sources = 3 * group_blocks
    pairs = group_blocks * sources
    chunk = 8 if slots % 8 == 0 else 1
    in_vmem, in_smem, in_hbm = (pl.BlockSpec(memory_space=m) for m in (pltpu.VMEM, pltpu.SMEM, pltpu.HBM))
    f32, bf16 = jnp.float32, jnp.bfloat16
    slot_args = (live_slots,) + tuple(
        pltpu.with_memory_space_constraint(x, pltpu.HBM) for x in (target_ids, source_ids, kernels)
    )

    def fetched(count):
        return [
            pltpu.VMEM((count, *kernels.shape[1:]), bf16),
            pltpu.SMEM(target_ids.shape, jnp.int32),
            pltpu.SMEM(source_ids.shape, jnp.int32),
            pltpu.SemaphoreType.DMA((2,)),
            pltpu.SemaphoreType.DMA((count // chunk,)),
        ]

    def call(body, shapes, args, specs=None, scratch=(), mib=8, flops=0):
        single = not isinstance(shapes, tuple)
        return pl.pallas_call(
            body,
            out_shape=shapes,
            in_specs=specs or [in_vmem] * len(args),
            out_specs=in_vmem if single else (in_vmem,) * len(shapes),
            scratch_shapes=scratch,
            compiler_params=pltpu.CompilerParams(vmem_limit_bytes=mib << 20),
            cost_estimate=pl.CostEstimate(flops=flops, bytes_accessed=1 << 20, transcendentals=0),
        )(*args)

    def shape(*dims, kind=f32):
        return jax.ShapeDtypeStruct(dims, kind)

    def gather(token):
        mine = call(
            join_kernel,
            shape(3 * blocks * panels, width, kind=bf16),
            (token, strengths, adjoint_weights, beside),
            [in_hbm] + [in_vmem] * 3,
        )
        return [mine] + [exchange(mine, "clu", k) for k in range(1, clusters)]

    def group_strengths(token):
        return call(
            functools.partial(group_kernel, blocks, panels),
            shape(group_blocks * panels, width, kind=bf16),
            (token, *gathered),
            [in_hbm] + [in_vmem] * clusters,
        )

    def combine(start, count, token):
        total = call(
            functools.partial(combine_kernel, group_blocks, blocks, start, chunk),
            pltpu.VMEM((pairs, 2 * panels, panels), f32),
            (*slot_args, token),
            [in_smem] + [in_hbm] * 4,
            fetched(count),
            mib=20,
            flops=1 << 33,
        )
        return total, pltpu.with_memory_space_constraint(total, pltpu.VMEM)

    beside = exchange_beside(strengths, "grp", 1)
    block_sums = shape(group_blocks, panels, width)
    if pairs <= slots:
        early_slots = max(slots // chunk // 3, 1) * chunk
        token, early = combine(0, early_slots, slot_args[1])
        gathered = gather(token)
        token, late = combine(early_slots, slots - early_slots, gathered[0])
        own = group_strengths(token)
        first = exchange_beside(own, "grp", 0)
        kept, across = call(
            functools.partial(split_kernel, blocks, panels),
            (pltpu.VMEM((2, pairs, 2 * panels, panels), bf16), shape(width, 2 * group_blocks * panels, kind=bf16)),
            (own, early, late, *gathered),
            [in_hbm] + [in_vmem] * (2 + clusters),
            flops=1 << 33,
        )
        kept = pltpu.with_memory_space_constraint(kept, pltpu.VMEM)
        lower, upper = call(outer_kernel, (block_sums, block_sums), (kept, across), flops=1 << 33)
        potential, middle = call(
            functools.partial(inner_kernel, blocks),
            (block_sums, block_sums),
            (kept, across, first, *gathered),
            flops=1 << 33,
        )
        lower, upper = exchange_beside(lower, "grp", 0), exchange_beside(upper, "grp", 1)
        parts = call(
            functools.partial(parts_kernel, blocks),
            (shape(2 * blocks, panels, width),) * clusters,
            (potential, middle, lower, upper),
        )
    else:
        gathered = gather(strengths)
        first = exchange_beside(group_strengths(strengths), "grp", 0)
        potential, adjoint = call(
            functools.partial(slots_kernel, blocks, panels, chunk),
            (block_sums, shape(sources, width, panels)),
            (*slot_args, first, *gathered),
            [in_smem] + [in_hbm] * 3 + [in_vmem] * (1 + clusters),
            [
                *fetched(slots)[:1],
                pltpu.VMEM((sources, 2 * panels, width), bf16),
                pltpu.VMEM((group_blocks, width, 2 * panels), bf16),
                *fetched(slots)[1:],
            ],
            mib=40,
        )
        lower, middle, upper = (adjoint[i * group_blocks : (i + 1) * group_blocks] for i in range(3))
        adjoint = middle + exchange_beside(lower, "grp", 0) + exchange_beside(upper, "grp", 1)
        owned = [slice(k * blocks, (k + 1) * blocks) for k in range(clusters)]
        parts = [jnp.concatenate([potential[rows], adjoint[rows]], axis=0) for rows in owned]

    parts = [parts[0]] + [exchange(parts[k], "clu", k) for k in range(1, clusters)]
    out = shape(blocks * panels, width)
    return tuple(call(functools.partial(finish_kernel, blocks), (out, out), parts))


def solution(mesh):
    return jax.shard_map(
        local,
        mesh=mesh,
        in_specs=(
            P(("grp", "clu"), None),
            P(("grp", "clu"), None),
            P(("grp", "clu"), None, None, None),
            P(("grp", "clu")),
            P(("grp", "clu")),
            P(("grp", "clu")),
        ),
        out_specs=(P(("grp", "clu"), None), P(("grp", "clu"), None)),
        check_vma=False,
    )
```

```python
import functools

import jax
import jax.numpy as jnp
from jax import lax
from jax.experimental import pallas as pl
from jax.experimental.pallas import tpu as pltpu
from jax.sharding import PartitionSpec as P


def exchange(value, axis, step):
    return lax.ppermute(value, axis, [(i, i ^ step) for i in range(lax.axis_size(axis))])


def exchange_beside(value, first, step=0):
    groups, clusters = lax.axis_size("grp"), lax.axis_size("clu")
    pairs = [(i, i + 1) for i in range(first, groups - 1, 2)]
    pairs += [(j, i) for i, j in pairs]
    moves = [(i * clusters + c, j * clusters + (c ^ step)) for i, j in pairs for c in range(clusters)]
    return lax.ppermute(value, ("grp", "clu"), moves)


def turned(block):
    half = block.shape[1] // 2
    wide = pltpu.roll(block.astype(jnp.float32), half, axis=1)
    lane = lax.broadcasted_iota(jnp.int32, wide.shape, 1)
    return jnp.where(lane < half, -wide, wide).astype(block.dtype)


def turned_rows(block):
    half = block.shape[0] // 2
    return jnp.concatenate([-block[half:], block[:half]], axis=0)


def place(target_ref, source_ref, slot, group_blocks, blocks):
    group, mine = lax.axis_index("grp"), lax.axis_index("clu") * blocks
    target = (target_ref[slot] - group * group_blocks) ^ mine
    source = (source_ref[slot] - (group - 1) * group_blocks) ^ mine
    offset = lax.div(source, group_blocks) - 1
    return target, jnp.where(group % 2 == 0, source - 2 * offset * group_blocks, source)


def each_slot(chunk, refs, held, ids, id_sems, sems, prepare, work):
    live_ref, *id_refs, kernels_ref = refs
    chunks = held.shape[0] // chunk
    copies = [pltpu.make_async_copy(ref, kept, id_sems.at[i]) for i, (ref, kept) in enumerate(zip(id_refs, ids))]

    def fetch(c):
        rows = pl.ds(c * chunk, chunk)
        return pltpu.make_async_copy(kernels_ref.at[rows], held.at[rows], sems.at[c])

    for copy in copies:
        copy.start()
    for c in range(chunks):
        fetch(c).start()
    prepare()
    for copy in copies:
        copy.wait()
    live = live_ref[0]

    @pl.loop(0, chunks)
    def _(c):
        fetch(c).wait()
        first = c * chunk

        @pl.when(first + chunk <= live)
        def _():
            for i in range(chunk):
                work(first + i)

        @pl.when(first + chunk > live)
        def _():
            @pl.loop(first, jnp.maximum(live, first))
            def _(slot):
                work(slot)


def combine_kernel(group_blocks, blocks, chunk, *refs):
    slot_refs, (total, held, *ids, id_sems, sems) = refs[:4], refs[4:]
    sources = 3 * group_blocks

    def clear():
        @pl.loop(0, total.shape[0])
        def _(pair):
            total[pair] = jnp.zeros(total.shape[1:], total.dtype)

    def add(slot):
        target, source = place(*ids, slot, group_blocks, blocks)
        pair = target * sources + source
        total[pair] += held[slot].reshape(total.shape[1:]).astype(jnp.float32)

    each_slot(chunk, slot_refs, held, ids, id_sems, sems, clear, add)


def split_kernel(blocks, panels, _, total, *refs):
    *gathered, out_ref, across_ref = refs

    @pl.loop(0, total.shape[0])
    def _(pair):
        value = total[pair]
        high = value.astype(jnp.bfloat16)
        out_ref[0, pair] = high
        out_ref[1, pair] = (value - high.astype(jnp.float32)).astype(jnp.bfloat16)

    for i, block in enumerate(part_of(gathered, blocks, panels, 1)):
        across_ref[:, 2 * i * panels : 2 * (i + 1) * panels] = crossed(block)


def pack_kernel(strengths_ref, weights_ref, out_ref, sems):
    rows = strengths_ref.shape[0]
    copies = [
        pltpu.make_async_copy(ref, out_ref.at[pl.ds(i * rows, rows)], sems.at[i])
        for i, ref in enumerate((strengths_ref, weights_ref))
    ]
    for copy in copies:
        copy.start()
    for copy in copies:
        copy.wait()


def group_kernel(blocks, panels, _, *refs):
    *gathered, out_ref = refs
    for i, block in enumerate(part_of(gathered, blocks, panels, 0)):
        out_ref[i * panels : (i + 1) * panels] = block


def part_of(gathered, blocks, panels, part):
    for ref in gathered:
        for b in range(blocks):
            yield ref[pl.ds((part * blocks + b) * panels, panels), :]


def strengths_of(first_ref, gathered, second, blocks, panels):
    for i in range(0, first_ref.shape[0], panels):
        yield first_ref[i : i + panels]
    yield from part_of(gathered, blocks, panels, 0)
    yield from part_of(second, blocks, panels, 0)


def crossed(block):
    block = block.astype(jnp.float32).T
    return jnp.concatenate([block, turned_rows(block)], axis=1).astype(jnp.bfloat16)


def stacked(block):
    return jnp.concatenate([block, turned(block)], axis=0)


def adjoint_of(pairs_ref, across_ref, first, count):
    width = pairs_ref.shape[3]
    weights = across_ref[...]
    targets = weights.shape[1] // pairs_ref.shape[2]
    sources = pairs_ref.shape[1] // targets
    both = jnp.concatenate([weights, weights], axis=1)
    step = 2 if count % 2 == 0 else 1
    for i in range(0, count, step):
        columns = []
        for j in range(step):
            tiles = [pairs_ref[h, t * sources + first + i + j] for h in range(2) for t in range(targets)]
            columns.append(jnp.concatenate(tiles, axis=0))
        product = jnp.dot(both, jnp.concatenate(columns, axis=1), preferred_element_type=jnp.float32)
        for j in range(step):
            yield i + j, product[:, j * width : (j + 1) * width]


def outer_kernel(pairs_ref, across_ref, first_ref, second_ref):
    count = first_ref.shape[0]
    for i, value in adjoint_of(pairs_ref, across_ref, 0, count):
        first_ref[i] = value
    for i, value in adjoint_of(pairs_ref, across_ref, 2 * count, count):
        second_ref[i] = value


def inner_kernel(blocks, pairs_ref, across_ref, first_ref, *refs):
    *others, potential_ref, middle_ref = refs
    gathered, second = others[: len(others) // 2], others[len(others) // 2 :]
    targets, panels = potential_ref.shape[:2]
    sources = pairs_ref.shape[1] // targets
    stack = jnp.concatenate([stacked(x) for x in strengths_of(first_ref, gathered, second, blocks, panels)], axis=0)
    for t in range(targets):
        halves = []
        for h in range(2):
            tiles = []
            for s in range(sources):
                tiles += [pairs_ref[h, t * sources + s, :panels], pairs_ref[h, t * sources + s, panels:]]
            halves.append(jnp.concatenate(tiles, axis=1))
        product = jnp.dot(jnp.concatenate(halves, axis=0), stack, preferred_element_type=jnp.float32)
        potential_ref[t] = product[:panels] + product[panels:]
    for i, value in adjoint_of(pairs_ref, across_ref, targets, targets):
        middle_ref[i] = value


def parts_kernel(blocks, potential_ref, middle_ref, first_ref, second_ref, *outs):
    for i in range(potential_ref.shape[0]):
        out_ref, b = outs[i // blocks], i % blocks
        out_ref[b] = potential_ref[i]
        out_ref[blocks + b] = middle_ref[i] + first_ref[i] + second_ref[i]


def slots_kernel(blocks, panels, chunk, *refs):
    slot_refs, (first_ref, *others), refs = refs[:4], refs[4:-9], refs[-9:]
    gathered, second = others[: len(others) // 2], others[len(others) // 2 :]
    potential_ref, adjoint_ref, held, stack, across, *ids, id_sems, sems = refs
    group_blocks = potential_ref.shape[0]

    def prepare():
        potential_ref[...] = jnp.zeros(potential_ref.shape, potential_ref.dtype)
        adjoint_ref[...] = jnp.zeros(adjoint_ref.shape, adjoint_ref.dtype)
        for i, block in enumerate(strengths_of(first_ref, gathered, second, blocks, panels)):
            stack[i] = stacked(block)
        for i, block in enumerate(part_of(gathered, blocks, panels, 1)):
            across[i] = crossed(block)

    def work(slot):
        target, source = place(*ids, slot, group_blocks, blocks)
        real, imag = held[slot, 0], held[slot, 1]
        potential_ref[target] += jnp.dot(
            jnp.concatenate([real, imag], axis=1), stack[source], preferred_element_type=jnp.float32
        )
        adjoint_ref[source] += jnp.dot(
            across[target], jnp.concatenate([real, imag], axis=0), preferred_element_type=jnp.float32
        )

    each_slot(chunk, slot_refs, held, ids, id_sems, sems, prepare, work)


def finish_kernel(blocks, *refs):
    *parts, potential_ref, adjoint_ref = refs
    total = parts[0][...]
    for part in parts[1:]:
        total = total + part[...]
    panels = total.shape[1]
    for b in range(blocks):
        potential_ref[b * panels : (b + 1) * panels] = total[b]
        adjoint_ref[b * panels : (b + 1) * panels] = total[blocks + b].T


def local(strengths, adjoint_weights, kernels, target_ids, source_ids, live_slots):
    slots, _, panels, _ = kernels.shape
    width = strengths.shape[1]
    blocks = strengths.shape[0] // panels
    clusters = lax.axis_size("clu")
    group_blocks = clusters * blocks
    sources = 3 * group_blocks
    pairs = group_blocks * sources
    chunk = 8 if slots % 8 == 0 else 1
    in_vmem, in_smem, in_hbm = (pl.BlockSpec(memory_space=m) for m in (pltpu.VMEM, pltpu.SMEM, pltpu.HBM))
    f32, bf16 = jnp.float32, jnp.bfloat16
    slot_args = (live_slots,) + tuple(
        pltpu.with_memory_space_constraint(x, pltpu.HBM) for x in (target_ids, source_ids, kernels)
    )
    held = pltpu.VMEM(kernels.shape, bf16)
    fetch = [
        pltpu.SMEM(target_ids.shape, jnp.int32),
        pltpu.SMEM(source_ids.shape, jnp.int32),
        pltpu.SemaphoreType.DMA((2,)),
        pltpu.SemaphoreType.DMA((slots // chunk,)),
    ]

    def call(body, shapes, args, specs=None, scratch=(), mib=8, flops=0):
        single = not isinstance(shapes, tuple)
        return pl.pallas_call(
            body,
            out_shape=shapes,
            in_specs=specs or [in_vmem] * len(args),
            out_specs=in_vmem if single else (in_vmem,) * len(shapes),
            scratch_shapes=scratch,
            compiler_params=pltpu.CompilerParams(vmem_limit_bytes=mib << 20),
            cost_estimate=pl.CostEstimate(flops=flops, bytes_accessed=1 << 20, transcendentals=0),
        )(*args)

    def shape(*dims, kind=f32):
        return jax.ShapeDtypeStruct(dims, kind)

    second = [exchange_beside(strengths, 1, k) for k in range(clusters)]
    mine = call(
        pack_kernel,
        shape(2 * blocks * panels, width, kind=bf16),
        [pltpu.with_memory_space_constraint(x, pltpu.HBM) for x in (strengths, adjoint_weights)],
        [in_hbm] * 2,
        [pltpu.SemaphoreType.DMA((2,))],
    )
    gathered = [mine] + [exchange(mine, "clu", k) for k in range(1, clusters)]

    def group_strengths(token):
        return call(
            functools.partial(group_kernel, blocks, panels),
            shape(group_blocks * panels, width, kind=bf16),
            (token, *gathered),
            [in_hbm] + [in_vmem] * clusters,
        )

    block_sums = shape(group_blocks, panels, width)
    if pairs <= slots:
        total = call(
            functools.partial(combine_kernel, group_blocks, blocks, chunk),
            pltpu.VMEM((pairs, 2 * panels, panels), f32),
            slot_args,
            [in_smem] + [in_hbm] * 3,
            [held, *fetch],
            mib=20,
            flops=1 << 33,
        )
        own = group_strengths(total)
        first = exchange_beside(own, 0)
        total = pltpu.with_memory_space_constraint(total, pltpu.VMEM)
        kept, across = call(
            functools.partial(split_kernel, blocks, panels),
            (pltpu.VMEM((2, pairs, 2 * panels, panels), bf16), shape(width, 2 * group_blocks * panels, kind=bf16)),
            (own, total, *gathered),
            [in_hbm] + [in_vmem] * (1 + clusters),
            flops=1 << 33,
        )
        kept = pltpu.with_memory_space_constraint(kept, pltpu.VMEM)
        lower, upper = call(outer_kernel, (block_sums, block_sums), (kept, across), flops=1 << 33)
        potential, middle = call(
            functools.partial(inner_kernel, blocks),
            (block_sums, block_sums),
            (kept, across, first, *gathered, *second),
            flops=1 << 33,
        )
        lower, upper = exchange_beside(lower, 0), exchange_beside(upper, 1)
        parts = call(
            functools.partial(parts_kernel, blocks),
            (shape(2 * blocks, panels, width),) * clusters,
            (potential, middle, lower, upper),
        )
    else:
        first = exchange_beside(group_strengths(mine), 0)
        potential, adjoint = call(
            functools.partial(slots_kernel, blocks, panels, chunk),
            (block_sums, shape(sources, width, panels)),
            (*slot_args, first, *gathered, *second),
            [in_smem] + [in_hbm] * 3 + [in_vmem] * (1 + 2 * clusters),
            [
                held,
                pltpu.VMEM((sources, 2 * panels, width), bf16),
                pltpu.VMEM((group_blocks, width, 2 * panels), bf16),
                *fetch,
            ],
            mib=40,
        )
        lower, middle, upper = (adjoint[i * group_blocks : (i + 1) * group_blocks] for i in range(3))
        adjoint = middle + exchange_beside(lower, 0) + exchange_beside(upper, 1)
        owned = [slice(k * blocks, (k + 1) * blocks) for k in range(clusters)]
        parts = [jnp.concatenate([potential[rows], adjoint[rows]], axis=0) for rows in owned]

    parts = [parts[0]] + [exchange(parts[k], "clu", k) for k in range(1, clusters)]
    out = shape(blocks * panels, width)
    return tuple(call(functools.partial(finish_kernel, blocks), (out, out), parts))


def solution(mesh):
    return jax.shard_map(
        local,
        mesh=mesh,
        in_specs=(
            P(("grp", "clu"), None),
            P(("grp", "clu"), None),
            P(("grp", "clu"), None, None, None),
            P(("grp", "clu")),
            P(("grp", "clu")),
            P(("grp", "clu")),
        ),
        out_specs=(P(("grp", "clu"), None), P(("grp", "clu"), None)),
        check_vma=False,
    )
```

```python
import functools

import jax
import jax.numpy as jnp
from jax import lax
from jax.experimental import pallas as pl
from jax.experimental.pallas import tpu as pltpu
from jax.sharding import PartitionSpec as P

EXPONENT_ROWS = 16
TINY = 2.0**-100


def exchange(value, axis, step):
    return lax.ppermute(value, axis, [(i, i ^ step) for i in range(lax.axis_size(axis))])


def exchange_beside(value, first):
    groups = lax.axis_size("grp")
    partner = [i + 1 if (i - first) % 2 == 0 else i - 1 for i in range(groups)]
    return lax.ppermute(value, "grp", [(i, j if 0 <= j < groups else i) for i, j in enumerate(partner)])


def rows_of(index, panels):
    return pl.ds(index * panels, panels)


def encode(values, out_ref):
    exponents = []
    for i, value in enumerate(values):
        largest = jnp.max(jnp.abs(value), axis=0, keepdims=True)
        exponent = jnp.floor(jnp.log2(jnp.maximum(largest, TINY))) + 1.0
        scaled = jnp.round(value * jnp.exp2(15.0 - exponent))
        scaled = jnp.minimum(jnp.maximum(scaled, -32767.0), 32767.0)
        out_ref[rows_of(i, value.shape[0])] = scaled.astype(jnp.int32).astype(jnp.int16)
        exponents.append(exponent)
    last = out_ref.shape[0] - EXPONENT_ROWS * pl.cdiv(len(values), EXPONENT_ROWS)
    exponents += [jnp.zeros_like(exponents[0])] * (out_ref.shape[0] - last - len(exponents))
    table = jnp.concatenate(exponents, axis=0)
    out_ref[last:] = table.astype(jnp.int32).astype(jnp.int16)


def decode(ref, count, panels):
    table = ref[count * panels :].astype(jnp.int32).astype(jnp.float32)
    for i in range(count):
        value = ref[rows_of(i, panels)].astype(jnp.int32).astype(jnp.float32)
        yield value * jnp.exp2(table[i : i + 1] - 15.0)


def turned(block):
    half = block.shape[1] // 2
    wide = pltpu.roll(block.astype(jnp.float32), half, axis=1)
    lane = lax.broadcasted_iota(jnp.int32, wide.shape, 1)
    return jnp.where(lane < half, -wide, wide).astype(block.dtype)


def turned_rows(block):
    half = block.shape[0] // 2
    return jnp.concatenate([-block[half:], block[:half]], axis=0)


def place(target_ref, source_ref, slot, group_blocks, blocks):
    group, mine = lax.axis_index("grp"), lax.axis_index("clu") * blocks
    target = (target_ref[slot] - group * group_blocks) ^ mine
    source = (source_ref[slot] - (group - 1) * group_blocks) ^ mine
    offset = lax.div(source, group_blocks) - 1
    return target, jnp.where(group % 2 == 0, source - 2 * offset * group_blocks, source)


def each_slot(chunk, refs, held, ids, id_sems, sems, prepare, work):
    live_ref, *id_refs, kernels_ref = refs
    chunks = held.shape[0] // chunk
    copies = [pltpu.make_async_copy(ref, kept, id_sems.at[i]) for i, (ref, kept) in enumerate(zip(id_refs, ids))]

    def fetch(c):
        rows = pl.ds(c * chunk, chunk)
        return pltpu.make_async_copy(kernels_ref.at[rows], held.at[rows], sems.at[c])

    for copy in copies:
        copy.start()
    for c in range(chunks):
        fetch(c).start()
    prepare()
    for copy in copies:
        copy.wait()
    live = live_ref[0]

    @pl.loop(0, chunks)
    def _(c):
        fetch(c).wait()
        first = c * chunk

        @pl.when(first + chunk <= live)
        def _():
            for i in range(chunk):
                work(first + i)

        @pl.when(first + chunk > live)
        def _():
            @pl.loop(first, jnp.maximum(live, first))
            def _(slot):
                work(slot)


def combine_kernel(group_blocks, blocks, chunk, *refs):
    slot_refs, (total, held, *ids, id_sems, sems) = refs[:4], refs[4:]
    sources = 3 * group_blocks

    def clear():
        @pl.loop(0, total.shape[0])
        def _(pair):
            total[pair] = jnp.zeros(total.shape[1:], total.dtype)

    def add(slot):
        target, source = place(*ids, slot, group_blocks, blocks)
        pair = target * sources + source
        total[pair] += held[slot].reshape(total.shape[1:]).astype(jnp.float32)

    each_slot(chunk, slot_refs, held, ids, id_sems, sems, clear, add)


def split_kernel(blocks, panels, _, total, *refs):
    *gathered, out_ref, across_ref = refs

    @pl.loop(0, total.shape[0])
    def _(pair):
        value = total[pair]
        high = value.astype(jnp.bfloat16)
        out_ref[0, pair] = high
        out_ref[1, pair] = (value - high.astype(jnp.float32)).astype(jnp.bfloat16)

    for i, block in enumerate(part_of(gathered, blocks, panels, 1)):
        across_ref[:, 2 * i * panels : 2 * (i + 1) * panels] = crossed(block)


def pack_kernel(strengths_ref, weights_ref, out_ref, sems):
    rows = strengths_ref.shape[0]
    copies = [
        pltpu.make_async_copy(ref, out_ref.at[pl.ds(i * rows, rows)], sems.at[i])
        for i, ref in enumerate((strengths_ref, weights_ref))
    ]
    for copy in copies:
        copy.start()
    for copy in copies:
        copy.wait()


def group_kernel(blocks, panels, _, *refs):
    *gathered, out_ref = refs
    for i, block in enumerate(part_of(gathered, blocks, panels, 0)):
        out_ref[i * panels : (i + 1) * panels] = block


def part_of(gathered, blocks, panels, part):
    for ref in gathered:
        for b in range(blocks):
            yield ref[pl.ds((part * blocks + b) * panels, panels), :]


def strengths_of(first_ref, gathered, second_ref, blocks, panels):
    for i in range(first_ref.shape[0] // panels):
        yield first_ref[rows_of(i, panels)]
    yield from part_of(gathered, blocks, panels, 0)
    for i in range(second_ref.shape[0] // panels):
        yield second_ref[rows_of(i, panels)]


def crossed(block):
    block = block.astype(jnp.float32).T
    return jnp.concatenate([block, turned_rows(block)], axis=1).astype(jnp.bfloat16)


def stacked(block):
    return jnp.concatenate([block, turned(block)], axis=0)


def adjoint_of(pairs_ref, across_ref, first, count):
    width = pairs_ref.shape[3]
    weights = across_ref[...]
    targets = weights.shape[1] // pairs_ref.shape[2]
    sources = pairs_ref.shape[1] // targets
    both = jnp.concatenate([weights, weights], axis=1)
    step = 2 if count % 2 == 0 else 1
    for i in range(0, count, step):
        columns = []
        for j in range(step):
            tiles = [pairs_ref[h, t * sources + first + i + j] for h in range(2) for t in range(targets)]
            columns.append(jnp.concatenate(tiles, axis=0))
        product = jnp.dot(both, jnp.concatenate(columns, axis=1), preferred_element_type=jnp.float32)
        for j in range(step):
            yield i + j, product[:, j * width : (j + 1) * width]


def outer_kernel(count, pairs_ref, across_ref, first_ref, second_ref):
    encode([value for _, value in adjoint_of(pairs_ref, across_ref, 0, count)], first_ref)
    encode([value for _, value in adjoint_of(pairs_ref, across_ref, 2 * count, count)], second_ref)


def inner_kernel(blocks, pairs_ref, across_ref, first_ref, second_ref, *refs):
    *gathered, potential_ref, middle_ref = refs
    targets, panels = potential_ref.shape[:2]
    sources = pairs_ref.shape[1] // targets
    stack = jnp.concatenate([stacked(x) for x in strengths_of(first_ref, gathered, second_ref, blocks, panels)], axis=0)
    for t in range(targets):
        halves = []
        for h in range(2):
            tiles = []
            for s in range(sources):
                tiles += [pairs_ref[h, t * sources + s, :panels], pairs_ref[h, t * sources + s, panels:]]
            halves.append(jnp.concatenate(tiles, axis=1))
        product = jnp.dot(jnp.concatenate(halves, axis=0), stack, preferred_element_type=jnp.float32)
        potential_ref[t] = product[:panels] + product[panels:]
    for i, value in adjoint_of(pairs_ref, across_ref, targets, targets):
        middle_ref[i] = value


def parts_kernel(blocks, potential_ref, middle_ref, first_ref, second_ref, own_ref, *outs):
    count, panels = potential_ref.shape[:2]
    potential = [potential_ref[i] for i in range(count)]
    others = zip(decode(first_ref, count, panels), decode(second_ref, count, panels))
    adjoint = [middle_ref[i] + first + second for i, (first, second) in enumerate(others)]
    for i in range(blocks):
        own_ref[rows_of(i, panels)] = potential[i]
        own_ref[rows_of(blocks + i, panels)] = adjoint[i]
    for k, out_ref in enumerate(outs, 1):
        rows = slice(k * blocks, (k + 1) * blocks)
        encode(potential[rows] + adjoint[rows], out_ref)


def slots_kernel(blocks, panels, chunk, *refs):
    slot_refs, (first_ref, second_ref, *gathered), refs = refs[:4], refs[4:-9], refs[-9:]
    potential_ref, adjoint_ref, held, stack, across, *ids, id_sems, sems = refs
    group_blocks = potential_ref.shape[0]

    def prepare():
        potential_ref[...] = jnp.zeros(potential_ref.shape, potential_ref.dtype)
        adjoint_ref[...] = jnp.zeros(adjoint_ref.shape, adjoint_ref.dtype)
        for i, block in enumerate(strengths_of(first_ref, gathered, second_ref, blocks, panels)):
            stack[i] = stacked(block)
        for i, block in enumerate(part_of(gathered, blocks, panels, 1)):
            across[i] = crossed(block)

    def work(slot):
        target, source = place(*ids, slot, group_blocks, blocks)
        real, imag = held[slot, 0], held[slot, 1]
        potential_ref[target] += jnp.dot(
            jnp.concatenate([real, imag], axis=1), stack[source], preferred_element_type=jnp.float32
        )
        adjoint_ref[source] += jnp.dot(
            across[target], jnp.concatenate([real, imag], axis=0), preferred_element_type=jnp.float32
        )

    each_slot(chunk, slot_refs, held, ids, id_sems, sems, prepare, work)


def code_kernel(*refs):
    for ref, out_ref in zip(refs[:2], refs[2:]):
        encode([ref[i] for i in range(ref.shape[0])], out_ref)


def finish_kernel(blocks, panels, own_ref, *refs):
    *parts, potential_ref, adjoint_ref = refs
    total = [own_ref[rows_of(i, panels)] for i in range(2 * blocks)]
    for ref in parts:
        total = [a + b for a, b in zip(total, decode(ref, 2 * blocks, panels))]
    for b in range(blocks):
        potential_ref[rows_of(b, panels)] = total[b]
        adjoint_ref[rows_of(b, panels)] = total[blocks + b].T


def local(strengths, adjoint_weights, kernels, target_ids, source_ids, live_slots):
    slots, _, panels, _ = kernels.shape
    width = strengths.shape[1]
    blocks = strengths.shape[0] // panels
    clusters = lax.axis_size("clu")
    group_blocks = clusters * blocks
    sources = 3 * group_blocks
    pairs = group_blocks * sources
    chunk = 8 if slots % 8 == 0 else 1
    in_vmem, in_smem, in_hbm = (pl.BlockSpec(memory_space=m) for m in (pltpu.VMEM, pltpu.SMEM, pltpu.HBM))
    f32, bf16 = jnp.float32, jnp.bfloat16
    slot_args = (live_slots,) + tuple(
        pltpu.with_memory_space_constraint(x, pltpu.HBM) for x in (target_ids, source_ids, kernels)
    )
    held = pltpu.VMEM(kernels.shape, bf16)
    fetch = [
        pltpu.SMEM(target_ids.shape, jnp.int32),
        pltpu.SMEM(source_ids.shape, jnp.int32),
        pltpu.SemaphoreType.DMA((2,)),
        pltpu.SemaphoreType.DMA((slots // chunk,)),
    ]

    def call(body, shapes, args, specs=None, scratch=(), mib=8, flops=0):
        single = not isinstance(shapes, tuple)
        return pl.pallas_call(
            body,
            out_shape=shapes,
            in_specs=specs or [in_vmem] * len(args),
            out_specs=in_vmem if single else (in_vmem,) * len(shapes),
            scratch_shapes=scratch,
            compiler_params=pltpu.CompilerParams(vmem_limit_bytes=mib << 20),
            cost_estimate=pl.CostEstimate(flops=flops, bytes_accessed=1 << 20, transcendentals=0),
        )(*args)

    def shape(*dims, kind=f32):
        return jax.ShapeDtypeStruct(dims, kind)

    mine = call(
        pack_kernel,
        shape(2 * blocks * panels, width, kind=bf16),
        [pltpu.with_memory_space_constraint(x, pltpu.HBM) for x in (strengths, adjoint_weights)],
        [in_hbm] * 2,
        [pltpu.SemaphoreType.DMA((2,))],
    )
    gathered = [mine] + [exchange(mine, "clu", k) for k in range(1, clusters)]

    def group_strengths(token):
        return call(
            functools.partial(group_kernel, blocks, panels),
            shape(group_blocks * panels, width, kind=bf16),
            (token, *gathered),
            [in_hbm] + [in_vmem] * clusters,
        )

    def coded(count):
        return shape(count * panels + EXPONENT_ROWS * pl.cdiv(count, EXPONENT_ROWS), width, kind=jnp.int16)

    block_sums = shape(group_blocks, panels, width)
    if pairs <= slots:
        total = call(
            functools.partial(combine_kernel, group_blocks, blocks, chunk),
            pltpu.VMEM((pairs, 2 * panels, panels), f32),
            slot_args,
            [in_smem] + [in_hbm] * 3,
            [held, *fetch],
            mib=20,
            flops=1 << 33,
        )
        own = group_strengths(total)
        first, second = exchange_beside(own, 0), exchange_beside(own, 1)
        total = pltpu.with_memory_space_constraint(total, pltpu.VMEM)
        kept, across = call(
            functools.partial(split_kernel, blocks, panels),
            (pltpu.VMEM((2, pairs, 2 * panels, panels), bf16), shape(width, 2 * group_blocks * panels, kind=bf16)),
            (own, total, *gathered),
            [in_hbm] + [in_vmem] * (1 + clusters),
            flops=1 << 33,
        )
        kept = pltpu.with_memory_space_constraint(kept, pltpu.VMEM)
        lower, upper = call(
            functools.partial(outer_kernel, group_blocks), (coded(group_blocks),) * 2, (kept, across), flops=1 << 33
        )
        potential, middle = call(
            functools.partial(inner_kernel, blocks),
            (block_sums, block_sums),
            (kept, across, first, second, *gathered),
            flops=1 << 33,
        )
    else:
        own = group_strengths(mine)
        first, second = exchange_beside(own, 0), exchange_beside(own, 1)
        potential, adjoint = call(
            functools.partial(slots_kernel, blocks, panels, chunk),
            (block_sums, shape(sources, width, panels)),
            (*slot_args, first, second, *gathered),
            [in_smem] + [in_hbm] * 3 + [in_vmem] * (2 + clusters),
            [
                held,
                pltpu.VMEM((sources, 2 * panels, width), bf16),
                pltpu.VMEM((group_blocks, width, 2 * panels), bf16),
                *fetch,
            ],
            mib=40,
        )
        lower, middle, upper = (adjoint[i * group_blocks : (i + 1) * group_blocks] for i in range(3))
        lower, upper = call(code_kernel, (coded(group_blocks),) * 2, (lower, upper))
    lower, upper = exchange_beside(lower, 0), exchange_beside(upper, 1)
    mine, *parts = call(
        functools.partial(parts_kernel, blocks),
        (shape(2 * blocks * panels, width),) + (coded(2 * blocks),) * (clusters - 1),
        (potential, middle, lower, upper),
    )
    parts = [exchange(part, "clu", k) for k, part in enumerate(parts, 1)]
    out = shape(blocks * panels, width)
    return tuple(call(functools.partial(finish_kernel, blocks, panels), (out, out), (mine, *parts)))


def solution(mesh):
    return jax.shard_map(
        local,
        mesh=mesh,
        in_specs=(
            P(("grp", "clu"), None),
            P(("grp", "clu"), None),
            P(("grp", "clu"), None, None, None),
            P(("grp", "clu")),
            P(("grp", "clu")),
            P(("grp", "clu")),
        ),
        out_specs=(P(("grp", "clu"), None), P(("grp", "clu"), None)),
        check_vma=False,
    )
```

```python
import functools

import jax
import jax.numpy as jnp
from jax import lax
from jax.experimental import pallas as pl
from jax.experimental.pallas import tpu as pltpu
from jax.sharding import PartitionSpec as P

EXPONENT_ROWS = 16
TINY = 2.0**-100


def exchange(value, axis, step):
    return lax.ppermute(value, axis, [(i, i ^ step) for i in range(lax.axis_size(axis))])


def exchange_beside(value, first):
    groups = lax.axis_size("grp")
    partner = [i + 1 if (i - first) % 2 == 0 else i - 1 for i in range(groups)]
    return lax.ppermute(value, "grp", [(i, j if 0 <= j < groups else i) for i, j in enumerate(partner)])


def rows_of(index, panels):
    return pl.ds(index * panels, panels)


def encode(values, out_ref):
    exponents = []
    for i, value in enumerate(values):
        largest = jnp.max(jnp.abs(value), axis=0, keepdims=True)
        exponent = jnp.floor(jnp.log2(jnp.maximum(largest, TINY))) + 1.0
        scaled = jnp.round(value * jnp.exp2(15.0 - exponent))
        scaled = jnp.minimum(jnp.maximum(scaled, -32767.0), 32767.0)
        out_ref[rows_of(i, value.shape[0])] = scaled.astype(jnp.int32).astype(jnp.int16)
        exponents.append(exponent)
    last = out_ref.shape[0] - EXPONENT_ROWS * pl.cdiv(len(values), EXPONENT_ROWS)
    exponents += [jnp.zeros_like(exponents[0])] * (out_ref.shape[0] - last - len(exponents))
    table = jnp.concatenate(exponents, axis=0)
    out_ref[last:] = table.astype(jnp.int32).astype(jnp.int16)


def decode(ref, count, panels):
    table = ref[count * panels :].astype(jnp.int32).astype(jnp.float32)
    for i in range(count):
        value = ref[rows_of(i, panels)].astype(jnp.int32).astype(jnp.float32)
        yield value * jnp.exp2(table[i : i + 1] - 15.0)


def turned(block):
    half = block.shape[1] // 2
    wide = pltpu.roll(block.astype(jnp.float32), half, axis=1)
    lane = lax.broadcasted_iota(jnp.int32, wide.shape, 1)
    return jnp.where(lane < half, -wide, wide).astype(block.dtype)


def turned_rows(block):
    half = block.shape[0] // 2
    return jnp.concatenate([-block[half:], block[:half]], axis=0)


def place(target_ref, source_ref, slot, group_blocks, blocks):
    group, mine = lax.axis_index("grp"), lax.axis_index("clu") * blocks
    target = (target_ref[slot] - group * group_blocks) ^ mine
    source = (source_ref[slot] - (group - 1) * group_blocks) ^ mine
    offset = lax.div(source, group_blocks) - 1
    return target, jnp.where(group % 2 == 0, source - 2 * offset * group_blocks, source)


def each_slot(chunk, live_ref, id_refs, ids, id_sems, prepare, wait, work):
    copies = [pltpu.make_async_copy(ref, kept, id_sems.at[i]) for i, (ref, kept) in enumerate(zip(id_refs, ids))]
    for copy in copies:
        copy.start()
    prepare()
    for copy in copies:
        copy.wait()
    live = live_ref[0]

    @pl.loop(0, ids[0].shape[0] // chunk)
    def _(c):
        wait(c)
        first = c * chunk

        @pl.when(first + chunk <= live)
        def _():
            for i in range(chunk):
                work(first + i)

        @pl.when(first + chunk > live)
        def _():
            @pl.loop(first, jnp.maximum(live, first))
            def _(slot):
                work(slot)


def combine_kernel(group_blocks, blocks, chunk, live_ref, target_ref, source_ref, kernels_ref, total, *scratch):
    *ids, id_sems = scratch
    sources = 3 * group_blocks

    def clear():
        @pl.loop(0, total.shape[0])
        def _(pair):
            total[pair] = jnp.zeros(total.shape[1:], total.dtype)

    def add(slot):
        target, source = place(*ids, slot, group_blocks, blocks)
        pair = target * sources + source
        total[pair] += kernels_ref[slot].reshape(total.shape[1:]).astype(jnp.float32)

    each_slot(chunk, live_ref, (target_ref, source_ref), ids, id_sems, clear, lambda c: None, add)


def split_kernel(blocks, panels, _, total, *refs):
    *gathered, out_ref, across_ref = refs

    @pl.loop(0, total.shape[0])
    def _(pair):
        value = total[pair]
        high = value.astype(jnp.bfloat16)
        out_ref[0, pair] = high
        out_ref[1, pair] = (value - high.astype(jnp.float32)).astype(jnp.bfloat16)

    for i, block in enumerate(part_of(gathered, blocks, panels, 1)):
        across_ref[:, 2 * i * panels : 2 * (i + 1) * panels] = crossed(block)


def pack_kernel(strengths_ref, weights_ref, out_ref, sems):
    rows = strengths_ref.shape[0]
    copies = [
        pltpu.make_async_copy(ref, out_ref.at[pl.ds(i * rows, rows)], sems.at[i])
        for i, ref in enumerate((strengths_ref, weights_ref))
    ]
    for copy in copies:
        copy.start()
    for copy in copies:
        copy.wait()


def group_kernel(blocks, panels, _, *refs):
    *gathered, out_ref = refs
    for i, block in enumerate(part_of(gathered, blocks, panels, 0)):
        out_ref[i * panels : (i + 1) * panels] = block


def part_of(gathered, blocks, panels, part):
    for ref in gathered:
        for b in range(blocks):
            yield ref[pl.ds((part * blocks + b) * panels, panels), :]


def strengths_of(first_ref, gathered, second_ref, blocks, panels):
    for i in range(first_ref.shape[0] // panels):
        yield first_ref[rows_of(i, panels)]
    yield from part_of(gathered, blocks, panels, 0)
    for i in range(second_ref.shape[0] // panels):
        yield second_ref[rows_of(i, panels)]


def crossed(block):
    block = block.astype(jnp.float32).T
    return jnp.concatenate([block, turned_rows(block)], axis=1).astype(jnp.bfloat16)


def stacked(block):
    return jnp.concatenate([block, turned(block)], axis=0)


def adjoint_of(pairs_ref, across_ref, first, count):
    width = pairs_ref.shape[3]
    weights = across_ref[...]
    targets = weights.shape[1] // pairs_ref.shape[2]
    sources = pairs_ref.shape[1] // targets
    both = jnp.concatenate([weights, weights], axis=1)
    step = 2 if count % 2 == 0 else 1
    for i in range(0, count, step):
        columns = []
        for j in range(step):
            tiles = [pairs_ref[h, t * sources + first + i + j] for h in range(2) for t in range(targets)]
            columns.append(jnp.concatenate(tiles, axis=0))
        product = jnp.dot(both, jnp.concatenate(columns, axis=1), preferred_element_type=jnp.float32)
        for j in range(step):
            yield i + j, product[:, j * width : (j + 1) * width]


def outer_kernel(count, pairs_ref, across_ref, first_ref, second_ref):
    encode([value for _, value in adjoint_of(pairs_ref, across_ref, 0, count)], first_ref)
    encode([value for _, value in adjoint_of(pairs_ref, across_ref, 2 * count, count)], second_ref)


def inner_kernel(blocks, pairs_ref, across_ref, first_ref, second_ref, *refs):
    *gathered, potential_ref, middle_ref = refs
    targets, panels = potential_ref.shape[:2]
    sources = pairs_ref.shape[1] // targets
    stack = jnp.concatenate([stacked(x) for x in strengths_of(first_ref, gathered, second_ref, blocks, panels)], axis=0)
    for t in range(targets):
        halves = []
        for h in range(2):
            tiles = []
            for s in range(sources):
                tiles += [pairs_ref[h, t * sources + s, :panels], pairs_ref[h, t * sources + s, panels:]]
            halves.append(jnp.concatenate(tiles, axis=1))
        product = jnp.dot(jnp.concatenate(halves, axis=0), stack, preferred_element_type=jnp.float32)
        potential_ref[t] = product[:panels] + product[panels:]
    for i, value in adjoint_of(pairs_ref, across_ref, targets, targets):
        middle_ref[i] = value


def parts_kernel(blocks, potential_ref, middle_ref, first_ref, second_ref, own_ref, *outs):
    count, panels = potential_ref.shape[:2]
    potential = [potential_ref[i] for i in range(count)]
    others = zip(decode(first_ref, count, panels), decode(second_ref, count, panels))
    adjoint = [middle_ref[i] + first + second for i, (first, second) in enumerate(others)]
    for i in range(blocks):
        own_ref[rows_of(i, panels)] = potential[i]
        own_ref[rows_of(blocks + i, panels)] = adjoint[i]
    for k, out_ref in enumerate(outs, 1):
        rows = slice(k * blocks, (k + 1) * blocks)
        encode(potential[rows] + adjoint[rows], out_ref)


def slots_kernel(blocks, panels, chunk, *refs):
    (live_ref, *id_refs, kernels_ref), (first_ref, second_ref, *gathered) = refs[:4], refs[4:-9]
    potential_ref, adjoint_ref, held, stack, across, *ids, id_sems, sems = refs[-9:]
    group_blocks = potential_ref.shape[0]

    def fetch(c):
        rows = pl.ds(c * chunk, chunk)
        return pltpu.make_async_copy(kernels_ref.at[rows], held.at[rows], sems.at[c])

    def prepare():
        for c in range(held.shape[0] // chunk):
            fetch(c).start()
        potential_ref[...] = jnp.zeros(potential_ref.shape, potential_ref.dtype)
        adjoint_ref[...] = jnp.zeros(adjoint_ref.shape, adjoint_ref.dtype)
        for i, block in enumerate(strengths_of(first_ref, gathered, second_ref, blocks, panels)):
            stack[i] = stacked(block)
        for i, block in enumerate(part_of(gathered, blocks, panels, 1)):
            across[i] = crossed(block)

    def work(slot):
        target, source = place(*ids, slot, group_blocks, blocks)
        real, imag = held[slot, 0], held[slot, 1]
        potential_ref[target] += jnp.dot(
            jnp.concatenate([real, imag], axis=1), stack[source], preferred_element_type=jnp.float32
        )
        adjoint_ref[source] += jnp.dot(
            across[target], jnp.concatenate([real, imag], axis=0), preferred_element_type=jnp.float32
        )

    each_slot(chunk, live_ref, id_refs, ids, id_sems, prepare, lambda c: fetch(c).wait(), work)


def code_kernel(*refs):
    for ref, out_ref in zip(refs[:2], refs[2:]):
        encode([ref[i] for i in range(ref.shape[0])], out_ref)


def finish_kernel(blocks, panels, own_ref, *refs):
    *parts, potential_ref, adjoint_ref = refs
    total = [own_ref[rows_of(i, panels)] for i in range(2 * blocks)]
    for ref in parts:
        total = [a + b for a, b in zip(total, decode(ref, 2 * blocks, panels))]
    for b in range(blocks):
        potential_ref[rows_of(b, panels)] = total[b]
        adjoint_ref[rows_of(b, panels)] = total[blocks + b].T


def local(strengths, adjoint_weights, kernels, target_ids, source_ids, live_slots):
    slots, _, panels, _ = kernels.shape
    width = strengths.shape[1]
    blocks = strengths.shape[0] // panels
    clusters = lax.axis_size("clu")
    group_blocks = clusters * blocks
    sources = 3 * group_blocks
    pairs = group_blocks * sources
    chunk = 8 if slots % 8 == 0 else 1
    in_vmem, in_smem, in_hbm = (pl.BlockSpec(memory_space=m) for m in (pltpu.VMEM, pltpu.SMEM, pltpu.HBM))
    f32, bf16 = jnp.float32, jnp.bfloat16
    slot_args = (live_slots,) + tuple(pltpu.with_memory_space_constraint(x, pltpu.HBM) for x in (target_ids, source_ids))
    ids = [pltpu.SMEM(x.shape, x.dtype) for x in (target_ids, source_ids)] + [pltpu.SemaphoreType.DMA((2,))]

    def call(body, shapes, args, specs=None, scratch=(), mib=8, flops=0):
        single = not isinstance(shapes, tuple)
        return pl.pallas_call(
            body,
            out_shape=shapes,
            in_specs=specs or [in_vmem] * len(args),
            out_specs=in_vmem if single else (in_vmem,) * len(shapes),
            scratch_shapes=scratch,
            compiler_params=pltpu.CompilerParams(vmem_limit_bytes=mib << 20),
            cost_estimate=pl.CostEstimate(flops=flops, bytes_accessed=1 << 20, transcendentals=0),
        )(*args)

    def shape(*dims, kind=f32):
        return jax.ShapeDtypeStruct(dims, kind)

    mine = call(
        pack_kernel,
        shape(2 * blocks * panels, width, kind=bf16),
        [pltpu.with_memory_space_constraint(x, pltpu.HBM) for x in (strengths, adjoint_weights)],
        [in_hbm] * 2,
        [pltpu.SemaphoreType.DMA((2,))],
        flops=1 << 34,
    )
    gathered = [mine] + [exchange(mine, "clu", k) for k in range(1, clusters)]

    def group_strengths(token):
        return call(
            functools.partial(group_kernel, blocks, panels),
            shape(group_blocks * panels, width, kind=bf16),
            (token, *gathered),
            [in_hbm] + [in_vmem] * clusters,
        )

    def coded(count):
        return shape(count * panels + EXPONENT_ROWS * pl.cdiv(count, EXPONENT_ROWS), width, kind=jnp.int16)

    block_sums = shape(group_blocks, panels, width)
    if pairs <= slots:
        total = call(
            functools.partial(combine_kernel, group_blocks, blocks, chunk),
            pltpu.VMEM((pairs, 2 * panels, panels), f32),
            (*slot_args, pltpu.with_memory_space_constraint(kernels, pltpu.VMEM)),
            [in_smem] + [in_hbm] * 2 + [in_vmem],
            ids,
            flops=1 << 33,
        )
        own = group_strengths(total)
        first, second = exchange_beside(own, 0), exchange_beside(own, 1)
        total = pltpu.with_memory_space_constraint(total, pltpu.VMEM)
        kept, across = call(
            functools.partial(split_kernel, blocks, panels),
            (pltpu.VMEM((2, pairs, 2 * panels, panels), bf16), shape(width, 2 * group_blocks * panels, kind=bf16)),
            (own, total, *gathered),
            [in_hbm] + [in_vmem] * (1 + clusters),
            flops=1 << 33,
        )
        kept = pltpu.with_memory_space_constraint(kept, pltpu.VMEM)
        lower, upper = call(
            functools.partial(outer_kernel, group_blocks), (coded(group_blocks),) * 2, (kept, across), flops=1 << 33
        )
        potential, middle = call(
            functools.partial(inner_kernel, blocks),
            (block_sums, block_sums),
            (kept, across, first, second, *gathered),
            flops=1 << 33,
        )
    else:
        own = group_strengths(mine)
        first, second = exchange_beside(own, 0), exchange_beside(own, 1)
        potential, adjoint = call(
            functools.partial(slots_kernel, blocks, panels, chunk),
            (block_sums, shape(sources, width, panels)),
            (*slot_args, pltpu.with_memory_space_constraint(kernels, pltpu.HBM), first, second, *gathered),
            [in_smem] + [in_hbm] * 3 + [in_vmem] * (2 + clusters),
            [
                pltpu.VMEM(kernels.shape, bf16),
                pltpu.VMEM((sources, 2 * panels, width), bf16),
                pltpu.VMEM((group_blocks, width, 2 * panels), bf16),
                *ids,
                pltpu.SemaphoreType.DMA((slots // chunk,)),
            ],
            mib=40,
        )
        lower, middle, upper = (adjoint[i * group_blocks : (i + 1) * group_blocks] for i in range(3))
        lower, upper = call(code_kernel, (coded(group_blocks),) * 2, (lower, upper))
    lower, upper = exchange_beside(lower, 0), exchange_beside(upper, 1)
    mine, *parts = call(
        functools.partial(parts_kernel, blocks),
        (shape(2 * blocks * panels, width),) + (coded(2 * blocks),) * (clusters - 1),
        (potential, middle, lower, upper),
    )
    parts = [exchange(parts[k - 1], "clu", k) for k in range(clusters - 1, 0, -1)]
    out = shape(blocks * panels, width)
    return tuple(call(functools.partial(finish_kernel, blocks, panels), (out, out), (mine, *parts)))


def solution(mesh):
    return jax.shard_map(
        local,
        mesh=mesh,
        in_specs=(
            P(("grp", "clu"), None),
            P(("grp", "clu"), None),
            P(("grp", "clu"), None, None, None),
            P(("grp", "clu")),
            P(("grp", "clu")),
            P(("grp", "clu")),
        ),
        out_specs=(P(("grp", "clu"), None), P(("grp", "clu"), None)),
        check_vma=False,
    )
```

```python
import functools

import jax
import jax.numpy as jnp
from jax import lax
from jax.experimental import pallas as pl
from jax.experimental.pallas import tpu as pltpu
from jax.sharding import PartitionSpec as P

EXPONENT_ROWS = 16
TINY = 2.0**-100


def exchange(value, axis, step):
    return lax.ppermute(value, axis, [(i, i ^ step) for i in range(lax.axis_size(axis))])


def exchange_beside(value, first):
    groups = lax.axis_size("grp")
    partner = [i + 1 if (i - first) % 2 == 0 else i - 1 for i in range(groups)]
    return lax.ppermute(value, "grp", [(i, j if 0 <= j < groups else i) for i, j in enumerate(partner)])


def rows_of(index, panels):
    return pl.ds(index * panels, panels)


def encode(values, out_ref):
    exponents = []
    for i, value in enumerate(values):
        largest = jnp.max(jnp.abs(value), axis=0, keepdims=True)
        exponent = jnp.floor(jnp.log2(jnp.maximum(largest, TINY))) + 1.0
        scaled = jnp.round(value * jnp.exp2(15.0 - exponent))
        scaled = jnp.minimum(jnp.maximum(scaled, -32767.0), 32767.0)
        out_ref[rows_of(i, value.shape[0])] = scaled.astype(jnp.int32).astype(jnp.int16)
        exponents.append(exponent)
    last = out_ref.shape[0] - EXPONENT_ROWS * pl.cdiv(len(values), EXPONENT_ROWS)
    exponents += [jnp.zeros_like(exponents[0])] * (out_ref.shape[0] - last - len(exponents))
    table = jnp.concatenate(exponents, axis=0)
    out_ref[last:] = table.astype(jnp.int32).astype(jnp.int16)


def decode(ref, count, panels):
    table = ref[count * panels :].astype(jnp.int32).astype(jnp.float32)
    for i in range(count):
        value = ref[rows_of(i, panels)].astype(jnp.int32).astype(jnp.float32)
        yield value * jnp.exp2(table[i : i + 1] - 15.0)


def turned(block):
    half = block.shape[1] // 2
    wide = pltpu.roll(block.astype(jnp.float32), half, axis=1)
    lane = lax.broadcasted_iota(jnp.int32, wide.shape, 1)
    return jnp.where(lane < half, -wide, wide).astype(block.dtype)


def turned_rows(block):
    half = block.shape[0] // 2
    return jnp.concatenate([-block[half:], block[:half]], axis=0)


def place(target_ref, source_ref, slot, group_blocks, blocks):
    group, mine = lax.axis_index("grp"), lax.axis_index("clu") * blocks
    target = (target_ref[slot] - group * group_blocks) ^ mine
    source = (source_ref[slot] - (group - 1) * group_blocks) ^ mine
    offset = lax.div(source, group_blocks) - 1
    return target, jnp.where(group % 2 == 0, source - 2 * offset * group_blocks, source)


def each_slot(chunk, live_ref, id_refs, ids, id_sems, prepare, wait, work):
    copies = [pltpu.make_async_copy(ref, kept, id_sems.at[i]) for i, (ref, kept) in enumerate(zip(id_refs, ids))]
    for copy in copies:
        copy.start()
    prepare()
    for copy in copies:
        copy.wait()
    live = live_ref[0]

    @pl.loop(0, ids[0].shape[0] // chunk)
    def _(c):
        wait(c)
        first = c * chunk

        @pl.when(first + chunk <= live)
        def _():
            for i in range(chunk):
                work(first + i)

        @pl.when(first + chunk > live)
        def _():
            @pl.loop(first, jnp.maximum(live, first))
            def _(slot):
                work(slot)


def combine_kernel(group_blocks, blocks, chunk, live_ref, target_ref, source_ref, kernels_ref, total, *scratch):
    *ids, id_sems = scratch

    def clear():
        @pl.loop(0, total.shape[0])
        def _(pair):
            total[pair] = jnp.zeros(total.shape[1:], total.dtype)

    def add(slot):
        target, source = place(*ids, slot, group_blocks, blocks)
        pair = source * group_blocks + target
        total[pair] += kernels_ref[slot].reshape(total.shape[1:]).astype(jnp.float32)

    each_slot(chunk, live_ref, (target_ref, source_ref), ids, id_sems, clear, lambda c: None, add)


def split(total, first, out_ref):
    @pl.loop(0, out_ref.shape[1])
    def _(pair):
        value = total[first + pair]
        high = value.astype(jnp.bfloat16)
        out_ref[0, pair] = high
        out_ref[1, pair] = (value - high.astype(jnp.float32)).astype(jnp.bfloat16)


def pack_kernel(strengths_ref, weights_ref, out_ref, sems):
    rows = strengths_ref.shape[0]
    copies = [
        pltpu.make_async_copy(ref, out_ref.at[pl.ds(i * rows, rows)], sems.at[i])
        for i, ref in enumerate((strengths_ref, weights_ref))
    ]
    for copy in copies:
        copy.start()
    for copy in copies:
        copy.wait()


def group_kernel(blocks, panels, _, *refs):
    *gathered, out_ref = refs
    for i, block in enumerate(part_of(gathered, blocks, panels, 0)):
        out_ref[i * panels : (i + 1) * panels] = block


def part_of(gathered, blocks, panels, part):
    for ref in gathered:
        for b in range(blocks):
            yield ref[pl.ds((part * blocks + b) * panels, panels), :]


def strengths_of(first_ref, gathered, second_ref, blocks, panels):
    for i in range(first_ref.shape[0] // panels):
        yield first_ref[rows_of(i, panels)]
    yield from part_of(gathered, blocks, panels, 0)
    for i in range(second_ref.shape[0] // panels):
        yield second_ref[rows_of(i, panels)]


def crossed(block):
    block = block.astype(jnp.float32).T
    return jnp.concatenate([block, turned_rows(block)], axis=1).astype(jnp.bfloat16)


def stacked(block):
    return jnp.concatenate([block, turned(block)], axis=0)


def adjoint_of(pairs_ref, across_ref, first, count):
    width = pairs_ref.shape[3]
    weights = across_ref[...]
    targets = weights.shape[1] // pairs_ref.shape[2]
    both = jnp.concatenate([weights, weights], axis=1)
    step = 2 if count % 2 == 0 else 1
    for i in range(0, count, step):
        columns = []
        for j in range(first + i, first + i + step):
            tiles = [pairs_ref[h, j * targets + t] for h in range(2) for t in range(targets)]
            columns.append(jnp.concatenate(tiles, axis=0))
        product = jnp.dot(both, jnp.concatenate(columns, axis=1), preferred_element_type=jnp.float32)
        for j in range(step):
            yield product[:, j * width : (j + 1) * width]


def second_kernel(blocks, panels, count, _, total, *refs):
    *gathered, pairs_ref, across_ref, out_ref = refs
    split(total, total.shape[0] - pairs_ref.shape[1], pairs_ref)
    for i, block in enumerate(part_of(gathered, blocks, panels, 1)):
        across_ref[:, 2 * i * panels : 2 * (i + 1) * panels] = crossed(block)
    encode(list(adjoint_of(pairs_ref, across_ref, 0, count)), out_ref)


def first_kernel(count, _first, _second, total, across_ref, pairs_ref, middle_ref, out_ref):
    split(total, 0, pairs_ref)
    encode(list(adjoint_of(pairs_ref, across_ref, 0, count)), out_ref)
    for i, value in enumerate(adjoint_of(pairs_ref, across_ref, count, count)):
        middle_ref[i] = value


def forward_kernel(blocks, pairs_ref, second_pairs_ref, first_ref, second_ref, *refs):
    *gathered, potential_ref = refs
    targets, panels = potential_ref.shape[:2]
    stack = jnp.concatenate([stacked(x) for x in strengths_of(first_ref, gathered, second_ref, blocks, panels)], axis=0)
    for t in range(targets):
        halves = []
        for h in range(2):
            tiles = []
            for ref in (pairs_ref, second_pairs_ref):
                for pair in range(t, ref.shape[1], targets):
                    tiles += [ref[h, pair, :panels], ref[h, pair, panels:]]
            halves.append(jnp.concatenate(tiles, axis=1))
        product = jnp.dot(jnp.concatenate(halves, axis=0), stack, preferred_element_type=jnp.float32)
        potential_ref[t] = product[:panels] + product[panels:]


def parts_kernel(blocks, potential_ref, middle_ref, first_ref, second_ref, own_ref, *outs):
    count, panels = potential_ref.shape[:2]
    potential = [potential_ref[i] for i in range(count)]
    others = zip(decode(first_ref, count, panels), decode(second_ref, count, panels))
    adjoint = [middle_ref[i] + first + second for i, (first, second) in enumerate(others)]
    for i in range(blocks):
        own_ref[rows_of(i, panels)] = potential[i]
        own_ref[rows_of(blocks + i, panels)] = adjoint[i]
    for k, out_ref in enumerate(outs, 1):
        rows = slice(k * blocks, (k + 1) * blocks)
        encode(potential[rows] + adjoint[rows], out_ref)


def slots_kernel(blocks, panels, chunk, *refs):
    (live_ref, *id_refs, kernels_ref), (first_ref, second_ref, *gathered) = refs[:4], refs[4:-9]
    potential_ref, adjoint_ref, held, stack, across, *ids, id_sems, sems = refs[-9:]
    group_blocks = potential_ref.shape[0]

    def fetch(c):
        rows = pl.ds(c * chunk, chunk)
        return pltpu.make_async_copy(kernels_ref.at[rows], held.at[rows], sems.at[c])

    def prepare():
        for c in range(held.shape[0] // chunk):
            fetch(c).start()
        potential_ref[...] = jnp.zeros(potential_ref.shape, potential_ref.dtype)
        adjoint_ref[...] = jnp.zeros(adjoint_ref.shape, adjoint_ref.dtype)
        for i, block in enumerate(strengths_of(first_ref, gathered, second_ref, blocks, panels)):
            stack[i] = stacked(block)
        for i, block in enumerate(part_of(gathered, blocks, panels, 1)):
            across[i] = crossed(block)

    def work(slot):
        target, source = place(*ids, slot, group_blocks, blocks)
        real, imag = held[slot, 0], held[slot, 1]
        potential_ref[target] += jnp.dot(
            jnp.concatenate([real, imag], axis=1), stack[source], preferred_element_type=jnp.float32
        )
        adjoint_ref[source] += jnp.dot(
            across[target], jnp.concatenate([real, imag], axis=0), preferred_element_type=jnp.float32
        )

    each_slot(chunk, live_ref, id_refs, ids, id_sems, prepare, lambda c: fetch(c).wait(), work)


def code_kernel(*refs):
    for ref, out_ref in zip(refs[:2], refs[2:]):
        encode([ref[i] for i in range(ref.shape[0])], out_ref)


def finish_kernel(blocks, panels, own_ref, *refs):
    *parts, potential_ref, adjoint_ref = refs
    total = [own_ref[rows_of(i, panels)] for i in range(2 * blocks)]
    for ref in parts:
        total = [a + b for a, b in zip(total, decode(ref, 2 * blocks, panels))]
    for b in range(blocks):
        potential_ref[rows_of(b, panels)] = total[b]
        adjoint_ref[rows_of(b, panels)] = total[blocks + b].T


def local(strengths, adjoint_weights, kernels, target_ids, source_ids, live_slots):
    slots, _, panels, _ = kernels.shape
    width = strengths.shape[1]
    blocks = strengths.shape[0] // panels
    clusters = lax.axis_size("clu")
    group_blocks = clusters * blocks
    sources = 3 * group_blocks
    pairs = group_blocks * sources
    chunk = 8 if slots % 8 == 0 else 1
    in_vmem, in_smem, in_hbm = (pl.BlockSpec(memory_space=m) for m in (pltpu.VMEM, pltpu.SMEM, pltpu.HBM))
    f32, bf16 = jnp.float32, jnp.bfloat16
    slot_args = (live_slots,) + tuple(pltpu.with_memory_space_constraint(x, pltpu.HBM) for x in (target_ids, source_ids))
    ids = [pltpu.SMEM(x.shape, x.dtype) for x in (target_ids, source_ids)] + [pltpu.SemaphoreType.DMA((2,))]

    def call(body, shapes, args, specs=None, scratch=(), mib=8, flops=0):
        single = not isinstance(shapes, tuple)
        return pl.pallas_call(
            body,
            out_shape=shapes,
            in_specs=specs or [in_vmem] * len(args),
            out_specs=in_vmem if single else (in_vmem,) * len(shapes),
            scratch_shapes=scratch,
            compiler_params=pltpu.CompilerParams(vmem_limit_bytes=mib << 20),
            cost_estimate=pl.CostEstimate(flops=flops, bytes_accessed=1 << 20, transcendentals=0),
        )(*args)

    def shape(*dims, kind=f32):
        return jax.ShapeDtypeStruct(dims, kind)

    mine = call(
        pack_kernel,
        shape(2 * blocks * panels, width, kind=bf16),
        [pltpu.with_memory_space_constraint(x, pltpu.HBM) for x in (strengths, adjoint_weights)],
        [in_hbm] * 2,
        [pltpu.SemaphoreType.DMA((2,))],
        flops=1 << 34,
    )
    gathered = [exchange(mine, "clu", k) for k in range(clusters - 1, 0, -1)]
    gathered = [mine] + gathered[::-1]

    def group_strengths(token):
        return call(
            functools.partial(group_kernel, blocks, panels),
            shape(group_blocks * panels, width, kind=bf16),
            (token, *gathered),
            [in_hbm] + [in_vmem] * clusters,
        )

    def coded(count):
        return shape(count * panels + EXPONENT_ROWS * pl.cdiv(count, EXPONENT_ROWS), width, kind=jnp.int16)

    block_sums = shape(group_blocks, panels, width)
    if pairs <= slots:
        total = call(
            functools.partial(combine_kernel, group_blocks, blocks, chunk),
            pltpu.VMEM((pairs, 2 * panels, panels), f32),
            (*slot_args, pltpu.with_memory_space_constraint(kernels, pltpu.VMEM)),
            [in_smem] + [in_hbm] * 2 + [in_vmem],
            ids,
            flops=1 << 33,
        )
        own = group_strengths(total)
        second, first = exchange_beside(own, 1), exchange_beside(own, 0)
        total = pltpu.with_memory_space_constraint(total, pltpu.VMEM)
        second_pairs = pairs // 3
        kept_second, across, upper = call(
            functools.partial(second_kernel, blocks, panels, group_blocks),
            (
                pltpu.VMEM((2, second_pairs, 2 * panels, panels), bf16),
                shape(width, 2 * group_blocks * panels, kind=bf16),
                coded(group_blocks),
            ),
            (own, total, *gathered),
            [in_hbm] + [in_vmem] * (1 + clusters),
            flops=1 << 33,
        )
        kept, middle, lower = call(
            functools.partial(first_kernel, group_blocks),
            (pltpu.VMEM((2, pairs - second_pairs, 2 * panels, panels), bf16), block_sums, coded(group_blocks)),
            (first, second, total, across),
            [in_hbm] * 2 + [in_vmem] * 2,
            flops=1 << 33,
        )
        kept, kept_second = (pltpu.with_memory_space_constraint(x, pltpu.VMEM) for x in (kept, kept_second))
        potential = call(
            functools.partial(forward_kernel, blocks),
            block_sums,
            (kept, kept_second, first, second, *gathered),
        )
    else:
        own = group_strengths(mine)
        first, second = exchange_beside(own, 0), exchange_beside(own, 1)
        potential, adjoint = call(
            functools.partial(slots_kernel, blocks, panels, chunk),
            (block_sums, shape(sources, width, panels)),
            (*slot_args, pltpu.with_memory_space_constraint(kernels, pltpu.HBM), first, second, *gathered),
            [in_smem] + [in_hbm] * 3 + [in_vmem] * (2 + clusters),
            [
                pltpu.VMEM(kernels.shape, bf16),
                pltpu.VMEM((sources, 2 * panels, width), bf16),
                pltpu.VMEM((group_blocks, width, 2 * panels), bf16),
                *ids,
                pltpu.SemaphoreType.DMA((slots // chunk,)),
            ],
            mib=40,
        )
        lower, middle, upper = (adjoint[i * group_blocks : (i + 1) * group_blocks] for i in range(3))
        lower, upper = call(code_kernel, (coded(group_blocks),) * 2, (lower, upper))
    upper, lower = exchange_beside(upper, 1), exchange_beside(lower, 0)
    mine, *parts = call(
        functools.partial(parts_kernel, blocks),
        (shape(2 * blocks * panels, width),) + (coded(2 * blocks),) * (clusters - 1),
        (potential, middle, lower, upper),
    )
    parts = [exchange(parts[k - 1], "clu", k) for k in range(clusters - 1, 0, -1)]
    out = shape(blocks * panels, width)
    return tuple(call(functools.partial(finish_kernel, blocks, panels), (out, out), (mine, *parts)))


def solution(mesh):
    return jax.shard_map(
        local,
        mesh=mesh,
        in_specs=(
            P(("grp", "clu"), None),
            P(("grp", "clu"), None),
            P(("grp", "clu"), None, None, None),
            P(("grp", "clu")),
            P(("grp", "clu")),
            P(("grp", "clu")),
        ),
        out_specs=(P(("grp", "clu"), None), P(("grp", "clu"), None)),
        check_vma=False,
    )
```

```python
import functools

import jax
import jax.numpy as jnp
from jax import lax
from jax.experimental import pallas as pl
from jax.experimental.pallas import tpu as pltpu
from jax.sharding import PartitionSpec as P

EXPONENT_ROWS = 16
TINY = 2.0**-100


def exchange(value, axis, step):
    return lax.ppermute(value, axis, [(i, i ^ step) for i in range(lax.axis_size(axis))])


def exchange_beside(value, first):
    groups = lax.axis_size("grp")
    partner = [i + 1 if (i - first) % 2 == 0 else i - 1 for i in range(groups)]
    return lax.ppermute(value, "grp", [(i, j if 0 <= j < groups else i) for i, j in enumerate(partner)])


def rows_of(index, panels):
    return pl.ds(index * panels, panels)


def encode(values, out_ref):
    exponents = []
    for i, value in enumerate(values):
        largest = jnp.max(jnp.abs(value), axis=0, keepdims=True)
        exponent = jnp.floor(jnp.log2(jnp.maximum(largest, TINY))) + 1.0
        scaled = jnp.round(value * jnp.exp2(15.0 - exponent))
        scaled = jnp.minimum(jnp.maximum(scaled, -32767.0), 32767.0)
        out_ref[rows_of(i, value.shape[0])] = scaled.astype(jnp.int32).astype(jnp.int16)
        exponents.append(exponent)
    last = out_ref.shape[0] - EXPONENT_ROWS * pl.cdiv(len(values), EXPONENT_ROWS)
    exponents += [jnp.zeros_like(exponents[0])] * (out_ref.shape[0] - last - len(exponents))
    table = jnp.concatenate(exponents, axis=0)
    out_ref[last:] = table.astype(jnp.int32).astype(jnp.int16)


def decode(ref, count, panels):
    table = ref[count * panels :].astype(jnp.int32).astype(jnp.float32)
    for i in range(count):
        value = ref[rows_of(i, panels)].astype(jnp.int32).astype(jnp.float32)
        yield value * jnp.exp2(table[i : i + 1] - 15.0)


def turned(block):
    half = block.shape[1] // 2
    wide = pltpu.roll(block.astype(jnp.float32), half, axis=1)
    lane = lax.broadcasted_iota(jnp.int32, wide.shape, 1)
    return jnp.where(lane < half, -wide, wide).astype(block.dtype)


def turned_rows(block):
    half = block.shape[0] // 2
    return jnp.concatenate([-block[half:], block[:half]], axis=0)


def place(target_ref, source_ref, slot, group_blocks, blocks):
    group, mine = lax.axis_index("grp"), lax.axis_index("clu") * blocks
    target = (target_ref[slot] - group * group_blocks) ^ mine
    source = (source_ref[slot] - (group - 1) * group_blocks) ^ mine
    offset = lax.div(source, group_blocks) - 1
    return target, jnp.where(group % 2 == 0, source - 2 * offset * group_blocks, source)


def each_slot(chunk, live_ref, id_refs, ids, id_sems, prepare, wait, work):
    copies = [pltpu.make_async_copy(ref, kept, id_sems.at[i]) for i, (ref, kept) in enumerate(zip(id_refs, ids))]
    for copy in copies:
        copy.start()
    prepare()
    for copy in copies:
        copy.wait()
    live = live_ref[0]

    @pl.loop(0, ids[0].shape[0] // chunk)
    def _(c):
        wait(c)
        first = c * chunk

        @pl.when(first + chunk <= live)
        def _():
            for i in range(chunk):
                work(first + i)

        @pl.when(first + chunk > live)
        def _():
            @pl.loop(first, jnp.maximum(live, first))
            def _(slot):
                work(slot)


def combine_kernel(group_blocks, blocks, chunk, live_ref, target_ref, source_ref, kernels_ref, total, *scratch):
    *ids, id_sems = scratch

    def clear():
        @pl.loop(0, total.shape[0])
        def _(pair):
            total[pair] = jnp.zeros(total.shape[1:], total.dtype)

    def add(slot):
        target, source = place(*ids, slot, group_blocks, blocks)
        pair = source * group_blocks + target
        total[pair] += kernels_ref[slot].reshape(total.shape[1:]).astype(jnp.float32)

    each_slot(chunk, live_ref, (target_ref, source_ref), ids, id_sems, clear, lambda c: None, add)


def split(total, first, out_ref):
    @pl.loop(0, out_ref.shape[1])
    def _(pair):
        value = total[first + pair]
        high = value.astype(jnp.bfloat16)
        out_ref[0, pair] = high
        out_ref[1, pair] = (value - high.astype(jnp.float32)).astype(jnp.bfloat16)


def pack_kernel(strengths_ref, weights_ref, out_ref, sems):
    rows = strengths_ref.shape[0]
    copies = [
        pltpu.make_async_copy(ref, out_ref.at[pl.ds(i * rows, rows)], sems.at[i])
        for i, ref in enumerate((strengths_ref, weights_ref))
    ]
    for copy in copies:
        copy.start()
    for copy in copies:
        copy.wait()


def group_kernel(blocks, panels, _, *refs):
    *gathered, out_ref = refs
    for i, block in enumerate(part_of(gathered, blocks, panels, 0)):
        out_ref[i * panels : (i + 1) * panels] = block


def part_of(gathered, blocks, panels, part):
    for ref in gathered:
        for b in range(blocks):
            yield ref[pl.ds((part * blocks + b) * panels, panels), :]


def strengths_of(first_ref, gathered, second_ref, blocks, panels):
    for i in range(first_ref.shape[0] // panels):
        yield first_ref[rows_of(i, panels)]
    yield from part_of(gathered, blocks, panels, 0)
    for i in range(second_ref.shape[0] // panels):
        yield second_ref[rows_of(i, panels)]


def crossed(block):
    block = block.astype(jnp.float32).T
    return jnp.concatenate([block, turned_rows(block)], axis=1).astype(jnp.bfloat16)


def stacked(block):
    return jnp.concatenate([block, turned(block)], axis=0)


def adjoint_of(pairs_ref, across_ref, first, count):
    width = pairs_ref.shape[3]
    weights = across_ref[...]
    targets = weights.shape[1] // pairs_ref.shape[2]
    both = jnp.concatenate([weights, weights], axis=1)
    step = 2 if count % 2 == 0 else 1
    for i in range(0, count, step):
        columns = []
        for j in range(first + i, first + i + step):
            tiles = [pairs_ref[h, j * targets + t] for h in range(2) for t in range(targets)]
            columns.append(jnp.concatenate(tiles, axis=0))
        product = jnp.dot(both, jnp.concatenate(columns, axis=1), preferred_element_type=jnp.float32)
        for j in range(step):
            yield product[:, j * width : (j + 1) * width]


def second_kernel(blocks, panels, count, _, total, *refs):
    *gathered, pairs_ref, across_ref, out_ref = refs
    split(total, total.shape[0] - pairs_ref.shape[1], pairs_ref)
    for i, block in enumerate(part_of(gathered, blocks, panels, 1)):
        across_ref[:, 2 * i * panels : 2 * (i + 1) * panels] = crossed(block)
    encode(list(adjoint_of(pairs_ref, across_ref, 0, count)), out_ref)


def first_kernel(count, _second, _first, total, across_ref, pairs_ref, middle_ref, out_ref):
    split(total, 0, pairs_ref)
    encode(list(adjoint_of(pairs_ref, across_ref, 0, count)), out_ref)
    for i, value in enumerate(adjoint_of(pairs_ref, across_ref, count, count)):
        middle_ref[i] = value


def forward_kernel(blocks, pairs_ref, second_pairs_ref, first_ref, second_ref, *refs):
    *gathered, potential_ref = refs
    targets, panels = potential_ref.shape[:2]
    stack = jnp.concatenate([stacked(x) for x in strengths_of(first_ref, gathered, second_ref, blocks, panels)], axis=0)
    for t in range(targets):
        halves = []
        for h in range(2):
            tiles = []
            for ref in (pairs_ref, second_pairs_ref):
                for pair in range(t, ref.shape[1], targets):
                    tiles += [ref[h, pair, :panels], ref[h, pair, panels:]]
            halves.append(jnp.concatenate(tiles, axis=1))
        product = jnp.dot(jnp.concatenate(halves, axis=0), stack, preferred_element_type=jnp.float32)
        potential_ref[t] = product[:panels] + product[panels:]


def parts_kernel(blocks, potential_ref, middle_ref, first_ref, second_ref, own_ref, *outs):
    count, panels = potential_ref.shape[:2]
    potential = [potential_ref[i] for i in range(count)]
    others = zip(decode(first_ref, count, panels), decode(second_ref, count, panels))
    adjoint = [middle_ref[i] + first + second for i, (first, second) in enumerate(others)]
    for i in range(blocks):
        own_ref[rows_of(i, panels)] = potential[i]
        own_ref[rows_of(blocks + i, panels)] = adjoint[i]
    for k, out_ref in enumerate(outs, 1):
        rows = slice(k * blocks, (k + 1) * blocks)
        encode(potential[rows] + adjoint[rows], out_ref)


def slots_kernel(blocks, panels, chunk, *refs):
    (live_ref, *id_refs, kernels_ref), (first_ref, second_ref, *gathered) = refs[:4], refs[4:-9]
    potential_ref, adjoint_ref, held, stack, across, *ids, id_sems, sems = refs[-9:]
    group_blocks = potential_ref.shape[0]

    def fetch(c):
        rows = pl.ds(c * chunk, chunk)
        return pltpu.make_async_copy(kernels_ref.at[rows], held.at[rows], sems.at[c])

    def prepare():
        for c in range(held.shape[0] // chunk):
            fetch(c).start()
        potential_ref[...] = jnp.zeros(potential_ref.shape, potential_ref.dtype)
        adjoint_ref[...] = jnp.zeros(adjoint_ref.shape, adjoint_ref.dtype)
        for i, block in enumerate(strengths_of(first_ref, gathered, second_ref, blocks, panels)):
            stack[i] = stacked(block)
        for i, block in enumerate(part_of(gathered, blocks, panels, 1)):
            across[i] = crossed(block)

    def work(slot):
        target, source = place(*ids, slot, group_blocks, blocks)
        real, imag = held[slot, 0], held[slot, 1]
        potential_ref[target] += jnp.dot(
            jnp.concatenate([real, imag], axis=1), stack[source], preferred_element_type=jnp.float32
        )
        adjoint_ref[source] += jnp.dot(
            across[target], jnp.concatenate([real, imag], axis=0), preferred_element_type=jnp.float32
        )

    each_slot(chunk, live_ref, id_refs, ids, id_sems, prepare, lambda c: fetch(c).wait(), work)


def code_kernel(*refs):
    for ref, out_ref in zip(refs[:2], refs[2:]):
        encode([ref[i] for i in range(ref.shape[0])], out_ref)


def finish_kernel(blocks, panels, own_ref, *refs):
    *parts, potential_ref, adjoint_ref = refs
    total = [own_ref[rows_of(i, panels)] for i in range(2 * blocks)]
    for ref in parts:
        total = [a + b for a, b in zip(total, decode(ref, 2 * blocks, panels))]
    for b in range(blocks):
        potential_ref[rows_of(b, panels)] = total[b]
        adjoint_ref[rows_of(b, panels)] = total[blocks + b].T


def local(strengths, adjoint_weights, kernels, target_ids, source_ids, live_slots):
    slots, _, panels, _ = kernels.shape
    width = strengths.shape[1]
    blocks = strengths.shape[0] // panels
    clusters = lax.axis_size("clu")
    group_blocks = clusters * blocks
    sources = 3 * group_blocks
    pairs = group_blocks * sources
    chunk = 8 if slots % 8 == 0 else 1
    in_vmem, in_smem, in_hbm = (pl.BlockSpec(memory_space=m) for m in (pltpu.VMEM, pltpu.SMEM, pltpu.HBM))
    f32, bf16 = jnp.float32, jnp.bfloat16
    slot_args = (live_slots,) + tuple(pltpu.with_memory_space_constraint(x, pltpu.HBM) for x in (target_ids, source_ids))
    ids = [pltpu.SMEM(x.shape, x.dtype) for x in (target_ids, source_ids)] + [pltpu.SemaphoreType.DMA((2,))]

    def call(body, shapes, args, specs=None, scratch=(), mib=8, flops=0):
        single = not isinstance(shapes, tuple)
        return pl.pallas_call(
            body,
            out_shape=shapes,
            in_specs=specs or [in_vmem] * len(args),
            out_specs=in_vmem if single else (in_vmem,) * len(shapes),
            scratch_shapes=scratch,
            compiler_params=pltpu.CompilerParams(vmem_limit_bytes=mib << 20),
            cost_estimate=pl.CostEstimate(flops=flops, bytes_accessed=1 << 20, transcendentals=0),
        )(*args)

    def shape(*dims, kind=f32):
        return jax.ShapeDtypeStruct(dims, kind)

    mine = call(
        pack_kernel,
        shape(2 * blocks * panels, width, kind=bf16),
        [pltpu.with_memory_space_constraint(x, pltpu.HBM) for x in (strengths, adjoint_weights)],
        [in_hbm] * 2,
        [pltpu.SemaphoreType.DMA((2,))],
        flops=1 << 34,
    )
    gathered = [exchange(mine, "clu", k) for k in range(clusters - 1, 0, -1)]
    gathered = [mine] + gathered[::-1]

    def group_strengths(token):
        return call(
            functools.partial(group_kernel, blocks, panels),
            shape(group_blocks * panels, width, kind=bf16),
            (token, *gathered),
            [in_hbm] + [in_vmem] * clusters,
        )

    def coded(count):
        return shape(count * panels + EXPONENT_ROWS * pl.cdiv(count, EXPONENT_ROWS), width, kind=jnp.int16)

    block_sums = shape(group_blocks, panels, width)
    if pairs <= slots:
        total = call(
            functools.partial(combine_kernel, group_blocks, blocks, chunk),
            pltpu.VMEM((pairs, 2 * panels, panels), f32),
            (*slot_args, pltpu.with_memory_space_constraint(kernels, pltpu.VMEM)),
            [in_smem] + [in_hbm] * 2 + [in_vmem],
            ids,
            flops=1 << 33,
        )
        own = group_strengths(total)
        first, second = exchange_beside(own, 0), exchange_beside(own, 1)
        total = pltpu.with_memory_space_constraint(total, pltpu.VMEM)
        second_pairs = pairs // 3
        kept_second, across, upper = call(
            functools.partial(second_kernel, blocks, panels, group_blocks),
            (
                pltpu.VMEM((2, second_pairs, 2 * panels, panels), bf16),
                shape(width, 2 * group_blocks * panels, kind=bf16),
                coded(group_blocks),
            ),
            (own, total, *gathered),
            [in_hbm] + [in_vmem] * (1 + clusters),
            flops=1 << 33,
        )
        kept, middle, lower = call(
            functools.partial(first_kernel, group_blocks),
            (pltpu.VMEM((2, pairs - second_pairs, 2 * panels, panels), bf16), block_sums, coded(group_blocks)),
            (second, first, total, across),
            [in_hbm] * 2 + [in_vmem] * 2,
            flops=1 << 33,
        )
        kept, kept_second = (pltpu.with_memory_space_constraint(x, pltpu.VMEM) for x in (kept, kept_second))
        potential = call(
            functools.partial(forward_kernel, blocks),
            block_sums,
            (kept, kept_second, first, second, *gathered),
        )
    else:
        own = group_strengths(mine)
        first, second = exchange_beside(own, 0), exchange_beside(own, 1)
        potential, adjoint = call(
            functools.partial(slots_kernel, blocks, panels, chunk),
            (block_sums, shape(sources, width, panels)),
            (*slot_args, pltpu.with_memory_space_constraint(kernels, pltpu.HBM), first, second, *gathered),
            [in_smem] + [in_hbm] * 3 + [in_vmem] * (2 + clusters),
            [
                pltpu.VMEM(kernels.shape, bf16),
                pltpu.VMEM((sources, 2 * panels, width), bf16),
                pltpu.VMEM((group_blocks, width, 2 * panels), bf16),
                *ids,
                pltpu.SemaphoreType.DMA((slots // chunk,)),
            ],
            mib=40,
        )
        lower, middle, upper = (adjoint[i * group_blocks : (i + 1) * group_blocks] for i in range(3))
        lower, upper = call(code_kernel, (coded(group_blocks),) * 2, (lower, upper))
    upper, lower = exchange_beside(upper, 1), exchange_beside(lower, 0)
    mine, *parts = call(
        functools.partial(parts_kernel, blocks),
        (shape(2 * blocks * panels, width),) + (coded(2 * blocks),) * (clusters - 1),
        (potential, middle, lower, upper),
    )
    parts = [exchange(parts[k - 1], "clu", k) for k in range(clusters - 1, 0, -1)]
    out = shape(blocks * panels, width)
    return tuple(call(functools.partial(finish_kernel, blocks, panels), (out, out), (mine, *parts)))


def solution(mesh):
    return jax.shard_map(
        local,
        mesh=mesh,
        in_specs=(
            P(("grp", "clu"), None),
            P(("grp", "clu"), None),
            P(("grp", "clu"), None, None, None),
            P(("grp", "clu")),
            P(("grp", "clu")),
            P(("grp", "clu")),
        ),
        out_specs=(P(("grp", "clu"), None), P(("grp", "clu"), None)),
        check_vma=False,
    )
```

```python
import functools

import jax
import jax.numpy as jnp
from jax import lax
from jax.experimental import pallas as pl
from jax.experimental.pallas import tpu as pltpu
from jax.sharding import PartitionSpec as P

EXPONENT_ROWS = 16
TINY = 2.0**-100


def exchange(value, axis, step):
    return lax.ppermute(value, axis, [(i, i ^ step) for i in range(lax.axis_size(axis))])


def exchange_beside(value, first):
    groups = lax.axis_size("grp")
    partner = [i + 1 if (i - first) % 2 == 0 else i - 1 for i in range(groups)]
    return lax.ppermute(value, "grp", [(i, j if 0 <= j < groups else i) for i, j in enumerate(partner)])


def rows_of(index, panels):
    return pl.ds(index * panels, panels)


def encode(values, out_ref):
    exponents = []
    for i, value in enumerate(values):
        largest = jnp.max(jnp.abs(value), axis=0, keepdims=True)
        exponent = jnp.floor(jnp.log2(jnp.maximum(largest, TINY))) + 1.0
        scaled = jnp.round(value * jnp.exp2(15.0 - exponent))
        scaled = jnp.minimum(jnp.maximum(scaled, -32767.0), 32767.0)
        out_ref[rows_of(i, value.shape[0])] = scaled.astype(jnp.int32).astype(jnp.int16)
        exponents.append(exponent)
    last = out_ref.shape[0] - EXPONENT_ROWS * pl.cdiv(len(values), EXPONENT_ROWS)
    exponents += [jnp.zeros_like(exponents[0])] * (out_ref.shape[0] - last - len(exponents))
    table = jnp.concatenate(exponents, axis=0)
    out_ref[last:] = table.astype(jnp.int32).astype(jnp.int16)


def decode(ref, count, panels):
    table = ref[count * panels :].astype(jnp.int32).astype(jnp.float32)
    for i in range(count):
        value = ref[rows_of(i, panels)].astype(jnp.int32).astype(jnp.float32)
        yield value * jnp.exp2(table[i : i + 1] - 15.0)


def turned(block):
    half = block.shape[1] // 2
    wide = pltpu.roll(block.astype(jnp.float32), half, axis=1)
    lane = lax.broadcasted_iota(jnp.int32, wide.shape, 1)
    return jnp.where(lane < half, -wide, wide).astype(block.dtype)


def turned_rows(block):
    half = block.shape[0] // 2
    return jnp.concatenate([-block[half:], block[:half]], axis=0)


def place(target_ref, source_ref, slot, group_blocks, blocks):
    group, mine = lax.axis_index("grp"), lax.axis_index("clu") * blocks
    target = (target_ref[slot] - group * group_blocks) ^ mine
    source = (source_ref[slot] - (group - 1) * group_blocks) ^ mine
    offset = lax.div(source, group_blocks) - 1
    return target, jnp.where(group % 2 == 0, source - 2 * offset * group_blocks, source)


def each_slot(chunk, live_ref, id_refs, ids, id_sems, prepare, wait, work):
    copies = [pltpu.make_async_copy(ref, kept, id_sems.at[i]) for i, (ref, kept) in enumerate(zip(id_refs, ids))]
    for copy in copies:
        copy.start()
    prepare()
    for copy in copies:
        copy.wait()
    live = live_ref[0]

    @pl.loop(0, ids[0].shape[0] // chunk)
    def _(c):
        wait(c)
        first = c * chunk

        @pl.when(first + chunk <= live)
        def _():
            for i in range(chunk):
                work(first + i)

        @pl.when(first + chunk > live)
        def _():
            @pl.loop(first, jnp.maximum(live, first))
            def _(slot):
                work(slot)


def combine_kernel(group_blocks, blocks, chunk, live_ref, target_ref, source_ref, kernels_ref, total, *scratch):
    *ids, id_sems = scratch

    def clear():
        @pl.loop(0, total.shape[0])
        def _(pair):
            total[pair] = jnp.zeros(total.shape[1:], total.dtype)

    def add(slot):
        target, source = place(*ids, slot, group_blocks, blocks)
        pair = source * group_blocks + target
        total[pair] += kernels_ref[slot].reshape(total.shape[1:]).astype(jnp.float32)

    each_slot(chunk, live_ref, (target_ref, source_ref), ids, id_sems, clear, lambda c: None, add)


def split(total, first, out_ref):
    @pl.loop(0, out_ref.shape[1])
    def _(pair):
        value = total[first + pair]
        high = value.astype(jnp.bfloat16)
        out_ref[0, pair] = high
        out_ref[1, pair] = (value - high.astype(jnp.float32)).astype(jnp.bfloat16)


def pack_kernel(strengths_ref, weights_ref, out_ref, sems):
    rows = strengths_ref.shape[0]
    copies = [
        pltpu.make_async_copy(ref, out_ref.at[pl.ds(i * rows, rows)], sems.at[i])
        for i, ref in enumerate((strengths_ref, weights_ref))
    ]
    for copy in copies:
        copy.start()
    for copy in copies:
        copy.wait()


def group_kernel(blocks, panels, _, *refs):
    *gathered, out_ref = refs
    for i, block in enumerate(part_of(gathered, blocks, panels, 0)):
        out_ref[i * panels : (i + 1) * panels] = block


def part_of(gathered, blocks, panels, part):
    for ref in gathered:
        for b in range(blocks):
            yield ref[pl.ds((part * blocks + b) * panels, panels), :]


def strengths_of(first_ref, gathered, second_ref, blocks, panels):
    for i in range(first_ref.shape[0] // panels):
        yield first_ref[rows_of(i, panels)]
    yield from part_of(gathered, blocks, panels, 0)
    for i in range(second_ref.shape[0] // panels):
        yield second_ref[rows_of(i, panels)]


def crossed(block):
    block = block.astype(jnp.float32).T
    return jnp.concatenate([block, turned_rows(block)], axis=1).astype(jnp.bfloat16)


def stacked(block):
    return jnp.concatenate([block, turned(block)], axis=0)


def adjoint_of(pairs_ref, across_ref, first, count):
    width = pairs_ref.shape[3]
    weights = across_ref[...]
    targets = weights.shape[1] // pairs_ref.shape[2]
    both = jnp.concatenate([weights, weights], axis=1)
    step = 2 if count % 2 == 0 else 1
    for i in range(0, count, step):
        columns = []
        for j in range(first + i, first + i + step):
            tiles = [pairs_ref[h, j * targets + t] for h in range(2) for t in range(targets)]
            columns.append(jnp.concatenate(tiles, axis=0))
        product = jnp.dot(both, jnp.concatenate(columns, axis=1), preferred_element_type=jnp.float32)
        for j in range(step):
            yield product[:, j * width : (j + 1) * width]


def second_kernel(blocks, panels, count, _, total, *refs):
    *gathered, pairs_ref, across_ref, out_ref = refs
    split(total, total.shape[0] - pairs_ref.shape[1], pairs_ref)
    for i, block in enumerate(part_of(gathered, blocks, panels, 1)):
        across_ref[:, 2 * i * panels : 2 * (i + 1) * panels] = crossed(block)
    strengths = [block.astype(jnp.float32) for block in part_of(gathered, blocks, panels, 0)]
    encode(strengths + list(adjoint_of(pairs_ref, across_ref, 0, count)), out_ref)


def first_kernel(count, _, total, across_ref, pairs_ref, middle_ref, out_ref):
    split(total, 0, pairs_ref)
    encode(list(adjoint_of(pairs_ref, across_ref, 0, count)), out_ref)
    for i, value in enumerate(adjoint_of(pairs_ref, across_ref, count, count)):
        middle_ref[i] = value


def forward_of(pairs_ref, strengths, targets):
    panels = pairs_ref.shape[2] // 2
    stack = jnp.concatenate([stacked(x) for x in strengths], axis=0)
    for t in range(targets):
        halves = []
        for h in range(2):
            tiles = []
            for pair in range(t, pairs_ref.shape[1], targets):
                tiles += [pairs_ref[h, pair, :panels], pairs_ref[h, pair, panels:]]
            halves.append(jnp.concatenate(tiles, axis=1))
        product = jnp.dot(jnp.concatenate(halves, axis=0), stack, preferred_element_type=jnp.float32)
        yield product[:panels] + product[panels:]


def forward_kernel(blocks, pairs_ref, first_ref, *refs):
    *gathered, potential_ref = refs
    targets, panels = potential_ref.shape[:2]
    strengths = [first_ref[rows_of(i, panels)] for i in range(targets)]
    strengths += part_of(gathered, blocks, panels, 0)
    for t, value in enumerate(forward_of(pairs_ref, strengths, targets)):
        potential_ref[t] = value


def parts_of(blocks, potential, adjoint, own_ref, *outs):
    panels = potential[0].shape[0]
    for i in range(blocks):
        own_ref[rows_of(i, panels)] = potential[i]
        own_ref[rows_of(blocks + i, panels)] = adjoint[i]
    for k, out_ref in enumerate(outs, 1):
        rows = slice(k * blocks, (k + 1) * blocks)
        encode(potential[rows] + adjoint[rows], out_ref)


def parts_kernel(blocks, pairs_ref, potential_ref, middle_ref, first_ref, second_ref, *outs):
    count, panels = potential_ref.shape[:2]
    received = list(decode(second_ref, 2 * count, panels))
    strengths = [block.astype(jnp.bfloat16) for block in received[:count]]
    forward = forward_of(pairs_ref, strengths, count)
    potential = [potential_ref[i] + value for i, value in enumerate(forward)]
    others = zip(decode(first_ref, count, panels), received[count:])
    adjoint = [middle_ref[i] + first + second for i, (first, second) in enumerate(others)]
    parts_of(blocks, potential, adjoint, *outs)


def slots_parts_kernel(blocks, potential_ref, adjoint_ref, first_ref, second_ref, *outs):
    count, panels = potential_ref.shape[:2]
    others = zip(decode(first_ref, count, panels), decode(second_ref, count, panels))
    adjoint = [adjoint_ref[count + i] + first + second for i, (first, second) in enumerate(others)]
    parts_of(blocks, [potential_ref[i] for i in range(count)], adjoint, *outs)


def slots_kernel(blocks, panels, chunk, *refs):
    (live_ref, *id_refs, kernels_ref), (first_ref, second_ref, *gathered) = refs[:4], refs[4:-9]
    potential_ref, adjoint_ref, held, stack, across, *ids, id_sems, sems = refs[-9:]
    group_blocks = potential_ref.shape[0]

    def fetch(c):
        rows = pl.ds(c * chunk, chunk)
        return pltpu.make_async_copy(kernels_ref.at[rows], held.at[rows], sems.at[c])

    def prepare():
        for c in range(held.shape[0] // chunk):
            fetch(c).start()
        potential_ref[...] = jnp.zeros(potential_ref.shape, potential_ref.dtype)
        adjoint_ref[...] = jnp.zeros(adjoint_ref.shape, adjoint_ref.dtype)
        for i, block in enumerate(strengths_of(first_ref, gathered, second_ref, blocks, panels)):
            stack[i] = stacked(block)
        for i, block in enumerate(part_of(gathered, blocks, panels, 1)):
            across[i] = crossed(block)

    def work(slot):
        target, source = place(*ids, slot, group_blocks, blocks)
        real, imag = held[slot, 0], held[slot, 1]
        potential_ref[target] += jnp.dot(
            jnp.concatenate([real, imag], axis=1), stack[source], preferred_element_type=jnp.float32
        )
        adjoint_ref[source] += jnp.dot(
            across[target], jnp.concatenate([real, imag], axis=0), preferred_element_type=jnp.float32
        )

    each_slot(chunk, live_ref, id_refs, ids, id_sems, prepare, lambda c: fetch(c).wait(), work)


def code_kernel(adjoint_ref, *outs):
    count = adjoint_ref.shape[0] // 3
    for first, out_ref in zip((0, 2 * count), outs):
        encode([adjoint_ref[first + i] for i in range(count)], out_ref)


def finish_kernel(blocks, panels, own_ref, *refs):
    *parts, potential_ref, adjoint_ref = refs
    total = [own_ref[rows_of(i, panels)] for i in range(2 * blocks)]
    for ref in parts:
        total = [a + b for a, b in zip(total, decode(ref, 2 * blocks, panels))]
    for b in range(blocks):
        potential_ref[rows_of(b, panels)] = total[b]
        adjoint_ref[rows_of(b, panels)] = total[blocks + b].T


def local(strengths, adjoint_weights, kernels, target_ids, source_ids, live_slots):
    slots, _, panels, _ = kernels.shape
    width = strengths.shape[1]
    blocks = strengths.shape[0] // panels
    clusters = lax.axis_size("clu")
    group_blocks = clusters * blocks
    sources = 3 * group_blocks
    pairs = group_blocks * sources
    chunk = 8 if slots % 8 == 0 else 1
    in_vmem, in_smem, in_hbm = (pl.BlockSpec(memory_space=m) for m in (pltpu.VMEM, pltpu.SMEM, pltpu.HBM))
    f32, bf16 = jnp.float32, jnp.bfloat16
    slot_args = (live_slots,) + tuple(pltpu.with_memory_space_constraint(x, pltpu.HBM) for x in (target_ids, source_ids))
    ids = [pltpu.SMEM(x.shape, x.dtype) for x in (target_ids, source_ids)] + [pltpu.SemaphoreType.DMA((2,))]

    def call(body, shapes, args, specs=None, scratch=(), mib=8, flops=0):
        single = not isinstance(shapes, tuple)
        return pl.pallas_call(
            body,
            out_shape=shapes,
            in_specs=specs or [in_vmem] * len(args),
            out_specs=in_vmem if single else (in_vmem,) * len(shapes),
            scratch_shapes=scratch,
            compiler_params=pltpu.CompilerParams(vmem_limit_bytes=mib << 20),
            cost_estimate=pl.CostEstimate(flops=flops, bytes_accessed=1 << 20, transcendentals=0),
        )(*args)

    def shape(*dims, kind=f32):
        return jax.ShapeDtypeStruct(dims, kind)

    mine = call(
        pack_kernel,
        shape(2 * blocks * panels, width, kind=bf16),
        [pltpu.with_memory_space_constraint(x, pltpu.HBM) for x in (strengths, adjoint_weights)],
        [in_hbm] * 2,
        [pltpu.SemaphoreType.DMA((2,))],
        flops=1 << 34,
    )
    gathered = [exchange(mine, "clu", k) for k in range(clusters - 1, 0, -1)]
    gathered = [mine] + gathered[::-1]

    def group_strengths(token):
        return call(
            functools.partial(group_kernel, blocks, panels),
            shape(group_blocks * panels, width, kind=bf16),
            (token, *gathered),
            [in_hbm] + [in_vmem] * clusters,
        )

    def coded(count):
        return shape(count * panels + EXPONENT_ROWS * pl.cdiv(count, EXPONENT_ROWS), width, kind=jnp.int16)

    block_sums = shape(group_blocks, panels, width)
    if pairs <= slots:
        total = call(
            functools.partial(combine_kernel, group_blocks, blocks, chunk),
            pltpu.VMEM((pairs, 2 * panels, panels), f32),
            (*slot_args, pltpu.with_memory_space_constraint(kernels, pltpu.VMEM)),
            [in_smem] + [in_hbm] * 2 + [in_vmem],
            ids,
            flops=1 << 33,
        )
        own = group_strengths(total)
        first = exchange_beside(own, 0)
        total = pltpu.with_memory_space_constraint(total, pltpu.VMEM)
        second_pairs = pairs // 3
        kept_second, across, upper = call(
            functools.partial(second_kernel, blocks, panels, group_blocks),
            (
                pltpu.VMEM((2, second_pairs, 2 * panels, panels), bf16),
                shape(width, 2 * group_blocks * panels, kind=bf16),
                coded(2 * group_blocks),
            ),
            (own, total, *gathered),
            [in_hbm] + [in_vmem] * (1 + clusters),
            flops=1 << 33,
        )
        kept, middle, lower = call(
            functools.partial(first_kernel, group_blocks),
            (pltpu.VMEM((2, pairs - second_pairs, 2 * panels, panels), bf16), block_sums, coded(group_blocks)),
            (first, total, across),
            [in_hbm] + [in_vmem] * 2,
            flops=1 << 33,
        )
        kept, kept_second = (pltpu.with_memory_space_constraint(x, pltpu.VMEM) for x in (kept, kept_second))
        potential = call(functools.partial(forward_kernel, blocks), block_sums, (kept, first, *gathered))
        upper, lower = exchange_beside(upper, 1), exchange_beside(lower, 0)
        parts_body, parts_args = parts_kernel, (kept_second, potential, middle, lower, upper)
    else:
        own = group_strengths(mine)
        first, second = exchange_beside(own, 0), exchange_beside(own, 1)
        potential, adjoint = call(
            functools.partial(slots_kernel, blocks, panels, chunk),
            (block_sums, shape(sources, width, panels)),
            (*slot_args, pltpu.with_memory_space_constraint(kernels, pltpu.HBM), first, second, *gathered),
            [in_smem] + [in_hbm] * 3 + [in_vmem] * (2 + clusters),
            [
                pltpu.VMEM(kernels.shape, bf16),
                pltpu.VMEM((sources, 2 * panels, width), bf16),
                pltpu.VMEM((group_blocks, width, 2 * panels), bf16),
                *ids,
                pltpu.SemaphoreType.DMA((slots // chunk,)),
            ],
            mib=40,
        )
        lower, upper = call(code_kernel, (coded(group_blocks),) * 2, (adjoint,))
        upper, lower = exchange_beside(upper, 1), exchange_beside(lower, 0)
        parts_body, parts_args = slots_parts_kernel, (potential, adjoint, lower, upper)
    mine, *parts = call(
        functools.partial(parts_body, blocks),
        (shape(2 * blocks * panels, width),) + (coded(2 * blocks),) * (clusters - 1),
        parts_args,
    )
    parts = [exchange(parts[k - 1], "clu", k) for k in range(clusters - 1, 0, -1)]
    out = shape(blocks * panels, width)
    return tuple(call(functools.partial(finish_kernel, blocks, panels), (out, out), (mine, *parts)))


def solution(mesh):
    return jax.shard_map(
        local,
        mesh=mesh,
        in_specs=(
            P(("grp", "clu"), None),
            P(("grp", "clu"), None),
            P(("grp", "clu"), None, None, None),
            P(("grp", "clu")),
            P(("grp", "clu")),
            P(("grp", "clu")),
        ),
        out_specs=(P(("grp", "clu"), None), P(("grp", "clu"), None)),
        check_vma=False,
    )
```

```python
import functools

import jax
import jax.numpy as jnp
from jax import lax
from jax.experimental import pallas as pl
from jax.experimental.pallas import tpu as pltpu
from jax.sharding import PartitionSpec as P

EXPONENT_ROWS = 16
TINY = 2.0**-100


def exchange(value, axis, step):
    return lax.ppermute(value, axis, [(i, i ^ step) for i in range(lax.axis_size(axis))])


def exchange_beside(value, first):
    groups = lax.axis_size("grp")
    partner = [i + 1 if (i - first) % 2 == 0 else i - 1 for i in range(groups)]
    return lax.ppermute(value, "grp", [(i, j if 0 <= j < groups else i) for i, j in enumerate(partner)])


def rows_of(index, panels):
    return pl.ds(index * panels, panels)


def encode(values, out_ref):
    exponents = []
    for i, value in enumerate(values):
        largest = jnp.max(jnp.abs(value), axis=0, keepdims=True)
        exponent = jnp.floor(jnp.log2(jnp.maximum(largest, TINY))) + 1.0
        scaled = jnp.round(value * jnp.exp2(15.0 - exponent))
        scaled = jnp.minimum(jnp.maximum(scaled, -32767.0), 32767.0)
        out_ref[rows_of(i, value.shape[0])] = scaled.astype(jnp.int32).astype(jnp.int16)
        exponents.append(exponent)
    last = out_ref.shape[0] - EXPONENT_ROWS * pl.cdiv(len(values), EXPONENT_ROWS)
    exponents += [jnp.zeros_like(exponents[0])] * (out_ref.shape[0] - last - len(exponents))
    table = jnp.concatenate(exponents, axis=0)
    out_ref[last:] = table.astype(jnp.int32).astype(jnp.int16)


def decode(ref, count, panels):
    table = ref[count * panels :].astype(jnp.int32).astype(jnp.float32)
    for i in range(count):
        value = ref[rows_of(i, panels)].astype(jnp.int32).astype(jnp.float32)
        yield value * jnp.exp2(table[i : i + 1] - 15.0)


def turned(block):
    half = block.shape[1] // 2
    wide = pltpu.roll(block.astype(jnp.float32), half, axis=1)
    lane = lax.broadcasted_iota(jnp.int32, wide.shape, 1)
    return jnp.where(lane < half, -wide, wide).astype(block.dtype)


def turned_rows(block):
    half = block.shape[0] // 2
    return jnp.concatenate([-block[half:], block[:half]], axis=0)


def place(target_ref, source_ref, slot, group_blocks, blocks):
    group, mine = lax.axis_index("grp"), lax.axis_index("clu") * blocks
    target = (target_ref[slot] - group * group_blocks) ^ mine
    source = (source_ref[slot] - (group - 1) * group_blocks) ^ mine
    offset = lax.div(source, group_blocks) - 1
    return target, jnp.where(group % 2 == 0, source - 2 * offset * group_blocks, source)


def each_slot(chunk, live_ref, id_refs, ids, id_sems, prepare, wait, work):
    copies = [pltpu.make_async_copy(ref, kept, id_sems.at[i]) for i, (ref, kept) in enumerate(zip(id_refs, ids))]
    for copy in copies:
        copy.start()
    prepare()
    for copy in copies:
        copy.wait()
    live = live_ref[0]

    @pl.loop(0, ids[0].shape[0] // chunk)
    def _(c):
        wait(c)
        first = c * chunk

        @pl.when(first + chunk <= live)
        def _():
            for i in range(chunk):
                work(first + i)

        @pl.when(first + chunk > live)
        def _():
            @pl.loop(first, jnp.maximum(live, first))
            def _(slot):
                work(slot)


def combine_kernel(group_blocks, blocks, chunk, live_ref, target_ref, source_ref, kernels_ref, _, total, *scratch):
    *ids, id_sems = scratch

    def add(slot):
        target, source = place(*ids, slot, group_blocks, blocks)
        pair = source * group_blocks + target
        total[pair] += kernels_ref[slot].reshape(total.shape[1:]).astype(jnp.float32)

    each_slot(chunk, live_ref, (target_ref, source_ref), ids, id_sems, lambda: None, lambda c: None, add)


def split(total, first, out_ref):
    @pl.loop(0, out_ref.shape[1])
    def _(pair):
        value = total[first + pair]
        high = value.astype(jnp.bfloat16)
        out_ref[0, pair] = high
        out_ref[1, pair] = (value - high.astype(jnp.float32)).astype(jnp.bfloat16)


def pack_kernel(strengths_ref, weights_ref, out_ref, *rest):
    *zeros, sems = rest
    rows = strengths_ref.shape[0]
    copies = [
        pltpu.make_async_copy(ref, out_ref.at[pl.ds(i * rows, rows)], sems.at[i])
        for i, ref in enumerate((strengths_ref, weights_ref))
    ]
    for copy in copies:
        copy.start()
    for ref in zeros:

        @pl.loop(0, ref.shape[0])
        def _(i):
            ref[i] = jnp.zeros(ref.shape[1:], ref.dtype)

    for copy in copies:
        copy.wait()


def group_kernel(blocks, panels, _, *refs):
    *gathered, out_ref = refs
    for i, block in enumerate(part_of(gathered, blocks, panels, 0)):
        out_ref[i * panels : (i + 1) * panels] = block


def part_of(gathered, blocks, panels, part):
    for ref in gathered:
        for b in range(blocks):
            yield ref[pl.ds((part * blocks + b) * panels, panels), :]


def strengths_of(first_ref, gathered, second_ref, blocks, panels):
    for i in range(first_ref.shape[0] // panels):
        yield first_ref[rows_of(i, panels)]
    yield from part_of(gathered, blocks, panels, 0)
    for i in range(second_ref.shape[0] // panels):
        yield second_ref[rows_of(i, panels)]


def crossed(block):
    block = block.astype(jnp.float32).T
    return jnp.concatenate([block, turned_rows(block)], axis=1).astype(jnp.bfloat16)


def stacked(block):
    return jnp.concatenate([block, turned(block)], axis=0)


def adjoint_of(pairs_ref, across_ref, first, count):
    width = pairs_ref.shape[3]
    weights = across_ref[...]
    targets = weights.shape[1] // pairs_ref.shape[2]
    both = jnp.concatenate([weights, weights], axis=1)
    step = 2 if count % 2 == 0 else 1
    for i in range(0, count, step):
        columns = []
        for j in range(first + i, first + i + step):
            tiles = [pairs_ref[h, j * targets + t] for h in range(2) for t in range(targets)]
            columns.append(jnp.concatenate(tiles, axis=0))
        product = jnp.dot(both, jnp.concatenate(columns, axis=1), preferred_element_type=jnp.float32)
        for j in range(step):
            yield product[:, j * width : (j + 1) * width]


def second_kernel(blocks, panels, count, total, *refs):
    *gathered, pairs_ref, across_ref, out_ref = refs
    split(total, total.shape[0] - pairs_ref.shape[1], pairs_ref)
    for i, block in enumerate(part_of(gathered, blocks, panels, 1)):
        across_ref[:, 2 * i * panels : 2 * (i + 1) * panels] = crossed(block)
    strengths = [block.astype(jnp.float32) for block in part_of(gathered, blocks, panels, 0)]
    encode(strengths + list(adjoint_of(pairs_ref, across_ref, 0, count)), out_ref)


def first_kernel(count, _, total, across_ref, pairs_ref, middle_ref, out_ref):
    split(total, 0, pairs_ref)
    encode(list(adjoint_of(pairs_ref, across_ref, 0, count)), out_ref)
    for i, value in enumerate(adjoint_of(pairs_ref, across_ref, count, count)):
        middle_ref[i] = value


def forward_of(pairs_ref, strengths, targets):
    panels = pairs_ref.shape[2] // 2
    stack = jnp.concatenate([stacked(x) for x in strengths], axis=0)
    for t in range(targets):
        halves = []
        for h in range(2):
            tiles = []
            for pair in range(t, pairs_ref.shape[1], targets):
                tiles += [pairs_ref[h, pair, :panels], pairs_ref[h, pair, panels:]]
            halves.append(jnp.concatenate(tiles, axis=1))
        product = jnp.dot(jnp.concatenate(halves, axis=0), stack, preferred_element_type=jnp.float32)
        yield product[:panels] + product[panels:]


def forward_kernel(blocks, pairs_ref, first_ref, *refs):
    *gathered, potential_ref = refs
    targets, panels = potential_ref.shape[:2]
    strengths = [first_ref[rows_of(i, panels)] for i in range(targets)]
    strengths += part_of(gathered, blocks, panels, 0)
    for t, value in enumerate(forward_of(pairs_ref, strengths, targets)):
        potential_ref[t] = value


def parts_of(blocks, potential, adjoint, own_ref, *outs):
    panels = potential[0].shape[0]
    for i in range(blocks):
        own_ref[rows_of(i, panels)] = potential[i]
        own_ref[rows_of(blocks + i, panels)] = adjoint[i]
    for k, out_ref in enumerate(outs, 1):
        rows = slice(k * blocks, (k + 1) * blocks)
        encode(potential[rows] + adjoint[rows], out_ref)


def parts_kernel(blocks, pairs_ref, potential_ref, middle_ref, first_ref, second_ref, *outs):
    count, panels = potential_ref.shape[:2]
    received = list(decode(second_ref, 2 * count, panels))
    strengths = [block.astype(jnp.bfloat16) for block in received[:count]]
    forward = forward_of(pairs_ref, strengths, count)
    potential = [potential_ref[i] + value for i, value in enumerate(forward)]
    others = zip(decode(first_ref, count, panels), received[count:])
    adjoint = [middle_ref[i] + first + second for i, (first, second) in enumerate(others)]
    parts_of(blocks, potential, adjoint, *outs)


def slots_parts_kernel(blocks, potential_ref, adjoint_ref, first_ref, second_ref, *outs):
    count, panels = potential_ref.shape[:2]
    others = zip(decode(first_ref, count, panels), decode(second_ref, count, panels))
    adjoint = [adjoint_ref[count + i] + first + second for i, (first, second) in enumerate(others)]
    parts_of(blocks, [potential_ref[i] for i in range(count)], adjoint, *outs)


def slots_kernel(blocks, panels, chunk, *refs):
    (live_ref, *id_refs, kernels_ref), (first_ref, second_ref, *gathered) = refs[:4], refs[4:-9]
    potential_ref, adjoint_ref, held, stack, across, *ids, id_sems, sems = refs[-9:]
    group_blocks = potential_ref.shape[0]

    def fetch(c):
        rows = pl.ds(c * chunk, chunk)
        return pltpu.make_async_copy(kernels_ref.at[rows], held.at[rows], sems.at[c])

    def prepare():
        for c in range(held.shape[0] // chunk):
            fetch(c).start()
        potential_ref[...] = jnp.zeros(potential_ref.shape, potential_ref.dtype)
        adjoint_ref[...] = jnp.zeros(adjoint_ref.shape, adjoint_ref.dtype)
        for i, block in enumerate(strengths_of(first_ref, gathered, second_ref, blocks, panels)):
            stack[i] = stacked(block)
        for i, block in enumerate(part_of(gathered, blocks, panels, 1)):
            across[i] = crossed(block)

    def work(slot):
        target, source = place(*ids, slot, group_blocks, blocks)
        real, imag = held[slot, 0], held[slot, 1]
        potential_ref[target] += jnp.dot(
            jnp.concatenate([real, imag], axis=1), stack[source], preferred_element_type=jnp.float32
        )
        adjoint_ref[source] += jnp.dot(
            across[target], jnp.concatenate([real, imag], axis=0), preferred_element_type=jnp.float32
        )

    each_slot(chunk, live_ref, id_refs, ids, id_sems, prepare, lambda c: fetch(c).wait(), work)


def code_kernel(adjoint_ref, *outs):
    count = adjoint_ref.shape[0] // 3
    for first, out_ref in zip((0, 2 * count), outs):
        encode([adjoint_ref[first + i] for i in range(count)], out_ref)


def finish_kernel(blocks, panels, own_ref, *refs):
    *parts, potential_ref, adjoint_ref = refs
    total = [own_ref[rows_of(i, panels)] for i in range(2 * blocks)]
    for ref in parts:
        total = [a + b for a, b in zip(total, decode(ref, 2 * blocks, panels))]
    for b in range(blocks):
        potential_ref[rows_of(b, panels)] = total[b]
        adjoint_ref[rows_of(b, panels)] = total[blocks + b].T


def local(strengths, adjoint_weights, kernels, target_ids, source_ids, live_slots):
    slots, _, panels, _ = kernels.shape
    width = strengths.shape[1]
    blocks = strengths.shape[0] // panels
    clusters = lax.axis_size("clu")
    group_blocks = clusters * blocks
    sources = 3 * group_blocks
    pairs = group_blocks * sources
    chunk = 8 if slots % 8 == 0 else 1
    in_vmem, in_smem, in_hbm = (pl.BlockSpec(memory_space=m) for m in (pltpu.VMEM, pltpu.SMEM, pltpu.HBM))
    f32, bf16 = jnp.float32, jnp.bfloat16
    slot_args = (live_slots,) + tuple(pltpu.with_memory_space_constraint(x, pltpu.VMEM) for x in (target_ids, source_ids))
    ids = [pltpu.SMEM(x.shape, x.dtype) for x in (target_ids, source_ids)] + [pltpu.SemaphoreType.DMA((2,))]

    def call(body, shapes, args, specs=None, scratch=(), mib=8, flops=0, aliases=()):
        single = not isinstance(shapes, tuple)
        return pl.pallas_call(
            body,
            out_shape=shapes,
            input_output_aliases=dict(aliases),
            in_specs=specs or [in_vmem] * len(args),
            out_specs=in_vmem if single else (in_vmem,) * len(shapes),
            scratch_shapes=scratch,
            compiler_params=pltpu.CompilerParams(vmem_limit_bytes=mib << 20),
            cost_estimate=pl.CostEstimate(flops=flops, bytes_accessed=1 << 20, transcendentals=0),
        )(*args)

    def shape(*dims, kind=f32):
        return jax.ShapeDtypeStruct(dims, kind)

    zeros = [pltpu.VMEM((pairs, 2 * panels, panels), f32)] if pairs <= slots else []
    mine, *zeros = call(
        pack_kernel,
        (shape(2 * blocks * panels, width, kind=bf16), *zeros),
        [pltpu.with_memory_space_constraint(x, pltpu.HBM) for x in (strengths, adjoint_weights)],
        [in_hbm] * 2,
        [pltpu.SemaphoreType.DMA((2,))],
        flops=1 << 34,
    )
    gathered = [exchange(mine, "clu", k) for k in range(clusters - 1, 0, -1)]
    gathered = [mine] + gathered[::-1]

    def group_strengths(token):
        return call(
            functools.partial(group_kernel, blocks, panels),
            shape(group_blocks * panels, width, kind=bf16),
            (token, *gathered),
            [in_hbm] + [in_vmem] * clusters,
        )

    def coded(count):
        return shape(count * panels + EXPONENT_ROWS * pl.cdiv(count, EXPONENT_ROWS), width, kind=jnp.int16)

    block_sums = shape(group_blocks, panels, width)
    if pairs <= slots:
        total = call(
            functools.partial(combine_kernel, group_blocks, blocks, chunk),
            pltpu.VMEM((pairs, 2 * panels, panels), f32),
            (*slot_args, *(pltpu.with_memory_space_constraint(x, pltpu.VMEM) for x in (kernels, *zeros))),
            [in_smem] + [in_vmem] * 4,
            ids,
            flops=1 << 33,
            aliases=[(4, 0)],
        )
        total = pltpu.with_memory_space_constraint(total, pltpu.VMEM)
        second_pairs = pairs // 3
        kept_second, across, upper = call(
            functools.partial(second_kernel, blocks, panels, group_blocks),
            (
                pltpu.VMEM((2, second_pairs, 2 * panels, panels), bf16),
                shape(width, 2 * group_blocks * panels, kind=bf16),
                coded(2 * group_blocks),
            ),
            (total, *gathered),
            flops=1 << 33,
        )
        first = exchange_beside(group_strengths(across), 0)
        kept, middle, lower = call(
            functools.partial(first_kernel, group_blocks),
            (pltpu.VMEM((2, pairs - second_pairs, 2 * panels, panels), bf16), block_sums, coded(group_blocks)),
            (first, total, across),
            [in_hbm] + [in_vmem] * 2,
            flops=1 << 33,
        )
        kept, kept_second = (pltpu.with_memory_space_constraint(x, pltpu.VMEM) for x in (kept, kept_second))
        potential = call(functools.partial(forward_kernel, blocks), block_sums, (kept, first, *gathered))
        upper, lower = exchange_beside(upper, 1), exchange_beside(lower, 0)
        parts_body, parts_args = parts_kernel, (kept_second, potential, middle, lower, upper)
    else:
        own = group_strengths(mine)
        first, second = exchange_beside(own, 0), exchange_beside(own, 1)
        potential, adjoint = call(
            functools.partial(slots_kernel, blocks, panels, chunk),
            (block_sums, shape(sources, width, panels)),
            (*slot_args, pltpu.with_memory_space_constraint(kernels, pltpu.HBM), first, second, *gathered),
            [in_smem] + [in_vmem] * 2 + [in_hbm] + [in_vmem] * (2 + clusters),
            [
                pltpu.VMEM(kernels.shape, bf16),
                pltpu.VMEM((sources, 2 * panels, width), bf16),
                pltpu.VMEM((group_blocks, width, 2 * panels), bf16),
                *ids,
                pltpu.SemaphoreType.DMA((slots // chunk,)),
            ],
            mib=40,
        )
        lower, upper = call(code_kernel, (coded(group_blocks),) * 2, (adjoint,))
        upper, lower = exchange_beside(upper, 1), exchange_beside(lower, 0)
        parts_body, parts_args = slots_parts_kernel, (potential, adjoint, lower, upper)
    mine, *parts = call(
        functools.partial(parts_body, blocks),
        (shape(2 * blocks * panels, width),) + (coded(2 * blocks),) * (clusters - 1),
        parts_args,
    )
    parts = [exchange(parts[k - 1], "clu", k) for k in range(clusters - 1, 0, -1)]
    out = shape(blocks * panels, width)
    return tuple(call(functools.partial(finish_kernel, blocks, panels), (out, out), (mine, *parts)))


def solution(mesh):
    return jax.shard_map(
        local,
        mesh=mesh,
        in_specs=(
            P(("grp", "clu"), None),
            P(("grp", "clu"), None),
            P(("grp", "clu"), None, None, None),
            P(("grp", "clu")),
            P(("grp", "clu")),
            P(("grp", "clu")),
        ),
        out_specs=(P(("grp", "clu"), None), P(("grp", "clu"), None)),
        check_vma=False,
    )
```

```python
import functools

import jax
import jax.numpy as jnp
from jax import lax
from jax.experimental import pallas as pl
from jax.experimental.pallas import tpu as pltpu
from jax.sharding import PartitionSpec as P

EXPONENT_ROWS = 16
TINY = 2.0**-100


def exchange(value, axis, step):
    return lax.ppermute(value, axis, [(i, i ^ step) for i in range(lax.axis_size(axis))])


def exchange_beside(value, first):
    groups = lax.axis_size("grp")
    partner = [i + 1 if (i - first) % 2 == 0 else i - 1 for i in range(groups)]
    return lax.ppermute(value, "grp", [(i, j if 0 <= j < groups else i) for i, j in enumerate(partner)])


def rows_of(index, panels):
    return pl.ds(index * panels, panels)


def encode(values, out_ref):
    exponents = []
    for i, value in enumerate(values):
        largest = jnp.max(jnp.abs(value), axis=0, keepdims=True)
        exponent = jnp.floor(jnp.log2(jnp.maximum(largest, TINY))) + 1.0
        scaled = jnp.round(value * jnp.exp2(15.0 - exponent))
        scaled = jnp.minimum(jnp.maximum(scaled, -32767.0), 32767.0)
        out_ref[rows_of(i, value.shape[0])] = scaled.astype(jnp.int32).astype(jnp.int16)
        exponents.append(exponent)
    last = out_ref.shape[0] - EXPONENT_ROWS * pl.cdiv(len(values), EXPONENT_ROWS)
    exponents += [jnp.zeros_like(exponents[0])] * (out_ref.shape[0] - last - len(exponents))
    table = jnp.concatenate(exponents, axis=0)
    out_ref[last:] = table.astype(jnp.int32).astype(jnp.int16)


def decode(ref, count, panels):
    table = ref[count * panels :].astype(jnp.int32).astype(jnp.float32)
    for i in range(count):
        value = ref[rows_of(i, panels)].astype(jnp.int32).astype(jnp.float32)
        yield value * jnp.exp2(table[i : i + 1] - 15.0)


def turned(block):
    half = block.shape[1] // 2
    wide = pltpu.roll(block.astype(jnp.float32), half, axis=1)
    lane = lax.broadcasted_iota(jnp.int32, wide.shape, 1)
    return jnp.where(lane < half, -wide, wide).astype(block.dtype)


def turned_rows(block):
    half = block.shape[0] // 2
    return jnp.concatenate([-block[half:], block[:half]], axis=0)


def place(target_ref, source_ref, slot, group_blocks, blocks):
    group, mine = lax.axis_index("grp"), lax.axis_index("clu") * blocks
    target = (target_ref[slot] - group * group_blocks) ^ mine
    source = (source_ref[slot] - (group - 1) * group_blocks) ^ mine
    offset = lax.div(source, group_blocks) - 1
    return target, jnp.where(group % 2 == 0, source - 2 * offset * group_blocks, source)


def each_slot(chunk, live_ref, slots, work, wait=None):
    live = live_ref[0]

    @pl.loop(0, slots // chunk if wait else pl.cdiv(live, chunk))
    def _(c):
        if wait:
            wait(c)
        first = c * chunk

        @pl.when(first + chunk <= live)
        def _():
            for i in range(chunk):
                work(first + i)

        @pl.when(first + chunk > live)
        def _():
            @pl.loop(first, jnp.maximum(live, first))
            def _(slot):
                work(slot)


def combine_kernel(group_blocks, blocks, chunk, live_ref, target_ref, source_ref, kernels_ref, _, total):
    def add(slot):
        target, source = place(target_ref, source_ref, slot, group_blocks, blocks)
        pair = source * group_blocks + target
        total[pair] += kernels_ref[slot].reshape(total.shape[1:]).astype(jnp.float32)

    each_slot(chunk, live_ref, kernels_ref.shape[0], add)


def split(total, first, out_ref):
    @pl.loop(0, out_ref.shape[1])
    def _(pair):
        value = total[first + pair]
        high = value.astype(jnp.bfloat16)
        out_ref[0, pair] = high
        out_ref[1, pair] = (value - high.astype(jnp.float32)).astype(jnp.bfloat16)


def pack_kernel(strengths_ref, weights_ref, target_ref, source_ref, out_ref, *rest):
    *kept, sems = rest
    ids, zeros = kept[:2], kept[2:]
    rows = strengths_ref.shape[0]
    moves = [(ref, out_ref.at[pl.ds(i * rows, rows)]) for i, ref in enumerate((strengths_ref, weights_ref))]
    moves += zip((target_ref, source_ref), ids)
    copies = [pltpu.make_async_copy(ref, to, sems.at[i]) for i, (ref, to) in enumerate(moves)]
    for copy in copies:
        copy.start()
    for ref in zeros:

        @pl.loop(0, ref.shape[0])
        def _(i):
            ref[i] = jnp.zeros(ref.shape[1:], ref.dtype)

    for copy in copies:
        copy.wait()


def group_kernel(blocks, panels, _, *refs):
    *gathered, out_ref = refs
    for i, block in enumerate(part_of(gathered, blocks, panels, 0)):
        out_ref[i * panels : (i + 1) * panels] = block


def part_of(gathered, blocks, panels, part):
    for ref in gathered:
        for b in range(blocks):
            yield ref[pl.ds((part * blocks + b) * panels, panels), :]


def strengths_of(first_ref, gathered, second_ref, blocks, panels):
    for i in range(first_ref.shape[0] // panels):
        yield first_ref[rows_of(i, panels)]
    yield from part_of(gathered, blocks, panels, 0)
    for i in range(second_ref.shape[0] // panels):
        yield second_ref[rows_of(i, panels)]


def crossed(block):
    block = block.astype(jnp.float32).T
    return jnp.concatenate([block, turned_rows(block)], axis=1).astype(jnp.bfloat16)


def stacked(block):
    return jnp.concatenate([block, turned(block)], axis=0)


def adjoint_of(pairs_ref, across_ref, first, count):
    width = pairs_ref.shape[3]
    weights = across_ref[...]
    targets = weights.shape[1] // pairs_ref.shape[2]
    both = jnp.concatenate([weights, weights], axis=1)
    step = 2 if count % 2 == 0 else 1
    for i in range(0, count, step):
        columns = []
        for j in range(first + i, first + i + step):
            tiles = [pairs_ref[h, j * targets + t] for h in range(2) for t in range(targets)]
            columns.append(jnp.concatenate(tiles, axis=0))
        product = jnp.dot(both, jnp.concatenate(columns, axis=1), preferred_element_type=jnp.float32)
        for j in range(step):
            yield product[:, j * width : (j + 1) * width]


def second_kernel(blocks, panels, count, _, total, *refs):
    *gathered, pairs_ref, across_ref, out_ref = refs
    split(total, total.shape[0] - pairs_ref.shape[1], pairs_ref)
    for i, block in enumerate(part_of(gathered, blocks, panels, 1)):
        across_ref[:, 2 * i * panels : 2 * (i + 1) * panels] = crossed(block)
    strengths = [block.astype(jnp.float32) for block in part_of(gathered, blocks, panels, 0)]
    encode(strengths + list(adjoint_of(pairs_ref, across_ref, 0, count)), out_ref)


def first_kernel(count, _, total, across_ref, pairs_ref, middle_ref, out_ref):
    split(total, 0, pairs_ref)
    encode(list(adjoint_of(pairs_ref, across_ref, 0, count)), out_ref)
    for i, value in enumerate(adjoint_of(pairs_ref, across_ref, count, count)):
        middle_ref[i] = value


def forward_of(pairs_ref, strengths, targets):
    panels = pairs_ref.shape[2] // 2
    stack = jnp.concatenate([stacked(x) for x in strengths], axis=0)
    for t in range(targets):
        halves = []
        for h in range(2):
            tiles = []
            for pair in range(t, pairs_ref.shape[1], targets):
                tiles += [pairs_ref[h, pair, :panels], pairs_ref[h, pair, panels:]]
            halves.append(jnp.concatenate(tiles, axis=1))
        product = jnp.dot(jnp.concatenate(halves, axis=0), stack, preferred_element_type=jnp.float32)
        yield product[:panels] + product[panels:]


def forward_kernel(blocks, pairs_ref, first_ref, *refs):
    *gathered, potential_ref = refs
    targets, panels = potential_ref.shape[:2]
    strengths = [first_ref[rows_of(i, panels)] for i in range(targets)]
    strengths += part_of(gathered, blocks, panels, 0)
    for t, value in enumerate(forward_of(pairs_ref, strengths, targets)):
        potential_ref[t] = value


def parts_of(blocks, potential, adjoint, own_ref, *outs):
    panels = potential[0].shape[0]
    for i in range(blocks):
        own_ref[rows_of(i, panels)] = potential[i]
        own_ref[rows_of(blocks + i, panels)] = adjoint[i]
    for k, out_ref in enumerate(outs, 1):
        rows = slice(k * blocks, (k + 1) * blocks)
        encode(potential[rows] + adjoint[rows], out_ref)


def parts_kernel(blocks, pairs_ref, potential_ref, middle_ref, first_ref, second_ref, *outs):
    count, panels = potential_ref.shape[:2]
    received = list(decode(second_ref, 2 * count, panels))
    strengths = [block.astype(jnp.bfloat16) for block in received[:count]]
    forward = forward_of(pairs_ref, strengths, count)
    potential = [potential_ref[i] + value for i, value in enumerate(forward)]
    others = zip(decode(first_ref, count, panels), received[count:])
    adjoint = [middle_ref[i] + first + second for i, (first, second) in enumerate(others)]
    parts_of(blocks, potential, adjoint, *outs)


def slots_parts_kernel(blocks, potential_ref, adjoint_ref, first_ref, second_ref, *outs):
    count, panels = potential_ref.shape[:2]
    others = zip(decode(first_ref, count, panels), decode(second_ref, count, panels))
    adjoint = [adjoint_ref[count + i] + first + second for i, (first, second) in enumerate(others)]
    parts_of(blocks, [potential_ref[i] for i in range(count)], adjoint, *outs)


def slots_kernel(blocks, panels, chunk, *refs):
    (live_ref, *ids, kernels_ref), (first_ref, second_ref, *gathered) = refs[:4], refs[4:-6]
    potential_ref, adjoint_ref, held, stack, across, sems = refs[-6:]
    group_blocks = potential_ref.shape[0]

    def fetch(c):
        rows = pl.ds(c * chunk, chunk)
        return pltpu.make_async_copy(kernels_ref.at[rows], held.at[rows], sems.at[c])

    def prepare():
        for c in range(held.shape[0] // chunk):
            fetch(c).start()
        potential_ref[...] = jnp.zeros(potential_ref.shape, potential_ref.dtype)
        adjoint_ref[...] = jnp.zeros(adjoint_ref.shape, adjoint_ref.dtype)
        for i, block in enumerate(strengths_of(first_ref, gathered, second_ref, blocks, panels)):
            stack[i] = stacked(block)
        for i, block in enumerate(part_of(gathered, blocks, panels, 1)):
            across[i] = crossed(block)

    def work(slot):
        target, source = place(*ids, slot, group_blocks, blocks)
        real, imag = held[slot, 0], held[slot, 1]
        potential_ref[target] += jnp.dot(
            jnp.concatenate([real, imag], axis=1), stack[source], preferred_element_type=jnp.float32
        )
        adjoint_ref[source] += jnp.dot(
            across[target], jnp.concatenate([real, imag], axis=0), preferred_element_type=jnp.float32
        )

    prepare()
    each_slot(chunk, live_ref, held.shape[0], work, lambda c: fetch(c).wait())


def code_kernel(adjoint_ref, *outs):
    count = adjoint_ref.shape[0] // 3
    for first, out_ref in zip((0, 2 * count), outs):
        encode([adjoint_ref[first + i] for i in range(count)], out_ref)


def finish_kernel(blocks, panels, own_ref, *refs):
    *parts, potential_ref, adjoint_ref = refs
    total = [own_ref[rows_of(i, panels)] for i in range(2 * blocks)]
    for ref in parts:
        total = [a + b for a, b in zip(total, decode(ref, 2 * blocks, panels))]
    for b in range(blocks):
        potential_ref[rows_of(b, panels)] = total[b]
        adjoint_ref[rows_of(b, panels)] = total[blocks + b].T


def local(strengths, adjoint_weights, kernels, target_ids, source_ids, live_slots):
    slots, _, panels, _ = kernels.shape
    width = strengths.shape[1]
    blocks = strengths.shape[0] // panels
    clusters = lax.axis_size("clu")
    group_blocks = clusters * blocks
    sources = 3 * group_blocks
    pairs = group_blocks * sources
    chunk = 8 if slots % 8 == 0 else 1
    in_vmem, in_smem, in_hbm = (pl.BlockSpec(memory_space=m) for m in (pltpu.VMEM, pltpu.SMEM, pltpu.HBM))
    f32, bf16 = jnp.float32, jnp.bfloat16

    def call(body, shapes, args, specs=None, scratch=(), mib=8, flops=0, aliases=(), out_specs=None):
        single = not isinstance(shapes, tuple)
        return pl.pallas_call(
            body,
            out_shape=shapes,
            input_output_aliases=dict(aliases),
            in_specs=specs or [in_vmem] * len(args),
            out_specs=out_specs or (in_vmem if single else (in_vmem,) * len(shapes)),
            scratch_shapes=scratch,
            compiler_params=pltpu.CompilerParams(vmem_limit_bytes=mib << 20),
            cost_estimate=pl.CostEstimate(flops=flops, bytes_accessed=1 << 20, transcendentals=0),
        )(*args)

    def shape(*dims, kind=f32):
        return jax.ShapeDtypeStruct(dims, kind)

    zeros = [pltpu.VMEM((pairs, 2 * panels, panels), f32)] if pairs <= slots else []
    kept_ids = [pltpu.SMEM(x.shape, x.dtype) for x in (target_ids, source_ids)]
    mine, *ids = call(
        pack_kernel,
        (shape(2 * blocks * panels, width, kind=bf16), *kept_ids, *zeros),
        [pltpu.with_memory_space_constraint(x, pltpu.HBM) for x in (strengths, adjoint_weights, target_ids, source_ids)],
        [in_hbm] * 4,
        [pltpu.SemaphoreType.DMA((4,))],
        out_specs=(in_vmem, in_smem, in_smem) + (in_vmem,) * len(zeros),
        flops=1 << 34,
    )
    ids, zeros = ids[:2], ids[2:]
    slot_args = (live_slots, *(pltpu.with_memory_space_constraint(x, pltpu.SMEM) for x in ids))
    gathered = [exchange(mine, "clu", k) for k in range(clusters - 1, 0, -1)]
    gathered = [mine] + gathered[::-1]

    def group_strengths(token):
        return call(
            functools.partial(group_kernel, blocks, panels),
            shape(group_blocks * panels, width, kind=bf16),
            (token, *gathered),
            [in_hbm] + [in_vmem] * clusters,
        )

    def coded(count):
        return shape(count * panels + EXPONENT_ROWS * pl.cdiv(count, EXPONENT_ROWS), width, kind=jnp.int16)

    block_sums = shape(group_blocks, panels, width)
    if pairs <= slots:
        total = call(
            functools.partial(combine_kernel, group_blocks, blocks, chunk),
            pltpu.VMEM((pairs, 2 * panels, panels), f32),
            (*slot_args, *(pltpu.with_memory_space_constraint(x, pltpu.VMEM) for x in (kernels, *zeros))),
            [in_smem] * 3 + [in_vmem] * 2,
            flops=1 << 33,
            aliases=[(4, 0)],
        )
        own = group_strengths(total)
        first = exchange_beside(own, 0)
        total = pltpu.with_memory_space_constraint(total, pltpu.VMEM)
        second_pairs = pairs // 3
        kept_second, across, upper = call(
            functools.partial(second_kernel, blocks, panels, group_blocks),
            (
                pltpu.VMEM((2, second_pairs, 2 * panels, panels), bf16),
                shape(width, 2 * group_blocks * panels, kind=bf16),
                coded(2 * group_blocks),
            ),
            (own, total, *gathered),
            [in_hbm] + [in_vmem] * (1 + clusters),
            flops=1 << 33,
        )
        kept, middle, lower = call(
            functools.partial(first_kernel, group_blocks),
            (pltpu.VMEM((2, pairs - second_pairs, 2 * panels, panels), bf16), block_sums, coded(group_blocks)),
            (first, total, across),
            [in_hbm] + [in_vmem] * 2,
            flops=1 << 33,
        )
        kept, kept_second = (pltpu.with_memory_space_constraint(x, pltpu.VMEM) for x in (kept, kept_second))
        potential = call(functools.partial(forward_kernel, blocks), block_sums, (kept, first, *gathered))
        upper, lower = exchange_beside(upper, 1), exchange_beside(lower, 0)
        parts_body, parts_args = parts_kernel, (kept_second, potential, middle, lower, upper)
    else:
        own = group_strengths(mine)
        first, second = exchange_beside(own, 0), exchange_beside(own, 1)
        potential, adjoint = call(
            functools.partial(slots_kernel, blocks, panels, chunk),
            (block_sums, shape(sources, width, panels)),
            (*slot_args, pltpu.with_memory_space_constraint(kernels, pltpu.HBM), first, second, *gathered),
            [in_smem] * 3 + [in_hbm] + [in_vmem] * (2 + clusters),
            [
                pltpu.VMEM(kernels.shape, bf16),
                pltpu.VMEM((sources, 2 * panels, width), bf16),
                pltpu.VMEM((group_blocks, width, 2 * panels), bf16),
                pltpu.SemaphoreType.DMA((slots // chunk,)),
            ],
            mib=40,
        )
        lower, upper = call(code_kernel, (coded(group_blocks),) * 2, (adjoint,))
        upper, lower = exchange_beside(upper, 1), exchange_beside(lower, 0)
        parts_body, parts_args = slots_parts_kernel, (potential, adjoint, lower, upper)
    mine, *parts = call(
        functools.partial(parts_body, blocks),
        (shape(2 * blocks * panels, width),) + (coded(2 * blocks),) * (clusters - 1),
        parts_args,
    )
    parts = [exchange(parts[k - 1], "clu", k) for k in range(clusters - 1, 0, -1)]
    out = shape(blocks * panels, width)
    return tuple(call(functools.partial(finish_kernel, blocks, panels), (out, out), (mine, *parts)))


def solution(mesh):
    return jax.shard_map(
        local,
        mesh=mesh,
        in_specs=(
            P(("grp", "clu"), None),
            P(("grp", "clu"), None),
            P(("grp", "clu"), None, None, None),
            P(("grp", "clu")),
            P(("grp", "clu")),
            P(("grp", "clu")),
        ),
        out_specs=(P(("grp", "clu"), None), P(("grp", "clu"), None)),
        check_vma=False,
    )
```

```python
import functools

import jax
import jax.numpy as jnp
from jax import lax
from jax.experimental import pallas as pl
from jax.experimental.pallas import tpu as pltpu
from jax.sharding import PartitionSpec as P

EXPONENT_ROWS = 16
TINY = 2.0**-110


def exchange(value, axis, step):
    return lax.ppermute(value, axis, [(i, i ^ step) for i in range(lax.axis_size(axis))])


def exchange_beside(value, first):
    groups = lax.axis_size("grp")
    partner = [i + 1 if (i - first) % 2 == 0 else i - 1 for i in range(groups)]
    return lax.ppermute(value, "grp", [(i, j if 0 <= j < groups else i) for i, j in enumerate(partner)])


def rows_of(index, panels):
    return pl.ds(index * panels, panels)


def encode(values, out_ref):
    exponents = []
    for i, value in enumerate(values):
        largest = jnp.max(jnp.abs(value), axis=0, keepdims=True)
        exponent = jnp.floor(jnp.log2(jnp.maximum(largest, TINY))) + 1.0
        scaled = jnp.round(value * jnp.exp2(15.0 - exponent))
        scaled = jnp.minimum(jnp.maximum(scaled, -32767.0), 32767.0)
        out_ref[rows_of(i, value.shape[0])] = scaled.astype(jnp.int32).astype(jnp.int16)
        exponents.append(exponent)
    last = out_ref.shape[0] - EXPONENT_ROWS * pl.cdiv(len(values), EXPONENT_ROWS)
    exponents += [jnp.zeros_like(exponents[0])] * (out_ref.shape[0] - last - len(exponents))
    table = jnp.concatenate(exponents, axis=0)
    out_ref[last:] = table.astype(jnp.int32).astype(jnp.int16)


def decode(ref, count, panels):
    table = ref[count * panels :].astype(jnp.int32).astype(jnp.float32)
    for i in range(count):
        value = ref[rows_of(i, panels)].astype(jnp.int32).astype(jnp.float32)
        yield value * jnp.exp2(table[i : i + 1] - 15.0)


def turned(block):
    half = block.shape[1] // 2
    wide = pltpu.roll(block.astype(jnp.float32), half, axis=1)
    lane = lax.broadcasted_iota(jnp.int32, wide.shape, 1)
    return jnp.where(lane < half, -wide, wide).astype(block.dtype)


def turned_rows(block):
    half = block.shape[0] // 2
    return jnp.concatenate([-block[half:], block[:half]], axis=0)


def place(target_ref, source_ref, slot, group_blocks, blocks):
    group, mine = lax.axis_index("grp"), lax.axis_index("clu") * blocks
    target = (target_ref[slot] - group * group_blocks) ^ mine
    source = (source_ref[slot] - (group - 1) * group_blocks) ^ mine
    offset = lax.div(source, group_blocks) - 1
    return target, jnp.where(group % 2 == 0, source - 2 * offset * group_blocks, source)


def each_slot(chunk, live_ref, slots, work, wait=None):
    live = live_ref[0]

    @pl.loop(0, slots // chunk if wait else pl.cdiv(live, chunk))
    def _(c):
        if wait:
            wait(c)
        first = c * chunk

        @pl.when(first + chunk <= live)
        def _():
            for i in range(chunk):
                work(first + i)

        @pl.when(first + chunk > live)
        def _():
            @pl.loop(first, jnp.maximum(live, first))
            def _(slot):
                work(slot)


def combine_kernel(group_blocks, blocks, chunk, live_ref, target_ref, source_ref, kernels_ref, _, total):
    def add(slot):
        target, source = place(target_ref, source_ref, slot, group_blocks, blocks)
        pair = source * group_blocks + target
        total[pair] += kernels_ref[slot].reshape(total.shape[1:]).astype(jnp.float32)

    each_slot(chunk, live_ref, kernels_ref.shape[0], add)


def split(total, first, out_ref):
    @pl.loop(0, out_ref.shape[1])
    def _(pair):
        value = total[first + pair]
        high = value.astype(jnp.bfloat16)
        out_ref[0, pair] = high
        out_ref[1, pair] = (value - high.astype(jnp.float32)).astype(jnp.bfloat16)


def pack_kernel(strengths_ref, weights_ref, target_ref, source_ref, out_ref, *rest):
    *kept, sems = rest
    ids, zeros = kept[:2], kept[2:]
    rows = strengths_ref.shape[0]
    moves = [(ref, out_ref.at[pl.ds(i * rows, rows)]) for i, ref in enumerate((strengths_ref, weights_ref))]
    moves += zip((target_ref, source_ref), ids)
    copies = [pltpu.make_async_copy(ref, to, sems.at[i]) for i, (ref, to) in enumerate(moves)]
    for copy in copies:
        copy.start()
    for ref in zeros:

        @pl.loop(0, ref.shape[0])
        def _(i):
            ref[i] = jnp.zeros(ref.shape[1:], ref.dtype)

    for copy in copies:
        copy.wait()


def group_kernel(blocks, panels, _, *refs):
    *gathered, out_ref = refs
    for i, block in enumerate(part_of(gathered, blocks, panels, 0)):
        out_ref[i * panels : (i + 1) * panels] = block


def part_of(gathered, blocks, panels, part):
    for ref in gathered:
        for b in range(blocks):
            yield ref[pl.ds((part * blocks + b) * panels, panels), :]


def strengths_of(first_ref, gathered, second_ref, blocks, panels):
    for i in range(first_ref.shape[0] // panels):
        yield first_ref[rows_of(i, panels)]
    yield from part_of(gathered, blocks, panels, 0)
    for i in range(second_ref.shape[0] // panels):
        yield second_ref[rows_of(i, panels)]


def crossed(block):
    block = block.astype(jnp.float32).T
    return jnp.concatenate([block, turned_rows(block)], axis=1).astype(jnp.bfloat16)


def stacked(block):
    return jnp.concatenate([block, turned(block)], axis=0)


def adjoint_of(pairs_ref, across_ref, first, count):
    width = pairs_ref.shape[3]
    weights = across_ref[...]
    targets = weights.shape[1] // pairs_ref.shape[2]
    both = jnp.concatenate([weights, weights], axis=1)
    step = 2 if count % 2 == 0 else 1
    for i in range(0, count, step):
        columns = []
        for j in range(first + i, first + i + step):
            tiles = [pairs_ref[h, j * targets + t] for h in range(2) for t in range(targets)]
            columns.append(jnp.concatenate(tiles, axis=0))
        product = jnp.dot(both, jnp.concatenate(columns, axis=1), preferred_element_type=jnp.float32)
        for j in range(step):
            yield product[:, j * width : (j + 1) * width]


def second_kernel(blocks, panels, count, _, total, *refs):
    *gathered, pairs_ref, across_ref, out_ref = refs
    split(total, total.shape[0] - pairs_ref.shape[1], pairs_ref)
    for i, block in enumerate(part_of(gathered, blocks, panels, 1)):
        across_ref[:, 2 * i * panels : 2 * (i + 1) * panels] = crossed(block)
    strengths = [block.astype(jnp.float32) for block in part_of(gathered, blocks, panels, 0)]
    encode(strengths + list(adjoint_of(pairs_ref, across_ref, 0, count)), out_ref)


def first_kernel(count, _, total, across_ref, pairs_ref, middle_ref, out_ref):
    split(total, 0, pairs_ref)
    encode(list(adjoint_of(pairs_ref, across_ref, 0, count)), out_ref)
    for i, value in enumerate(adjoint_of(pairs_ref, across_ref, count, count)):
        middle_ref[i] = value


def forward_of(pairs_ref, strengths, targets):
    panels = pairs_ref.shape[2] // 2
    stack = jnp.concatenate([stacked(x) for x in strengths], axis=0)
    for t in range(targets):
        halves = []
        for h in range(2):
            tiles = []
            for pair in range(t, pairs_ref.shape[1], targets):
                tiles += [pairs_ref[h, pair, :panels], pairs_ref[h, pair, panels:]]
            halves.append(jnp.concatenate(tiles, axis=1))
        product = jnp.dot(jnp.concatenate(halves, axis=0), stack, preferred_element_type=jnp.float32)
        yield product[:panels] + product[panels:]


def forward_kernel(blocks, pairs_ref, first_ref, *refs):
    *gathered, potential_ref = refs
    targets, panels = potential_ref.shape[:2]
    strengths = [first_ref[rows_of(i, panels)] for i in range(targets)]
    strengths += part_of(gathered, blocks, panels, 0)
    for t, value in enumerate(forward_of(pairs_ref, strengths, targets)):
        potential_ref[t] = value


def parts_of(blocks, potential, adjoint, own_ref, out_ref):
    panels = potential[0].shape[0]
    me = lax.axis_index("clu")
    for i in range(blocks):
        own_ref[rows_of(i, panels)] = potential[i]
        own_ref[rows_of(blocks + i, panels)] = adjoint[i]
    out_ref[me] = jnp.zeros(out_ref.shape[1:], out_ref.dtype)
    for k in range(1, out_ref.shape[0]):
        rows = slice(k * blocks, (k + 1) * blocks)
        encode(potential[rows] + adjoint[rows], out_ref.at[me ^ k])


def parts_kernel(blocks, pairs_ref, potential_ref, middle_ref, first_ref, second_ref, *outs):
    count, panels = potential_ref.shape[:2]
    received = list(decode(second_ref, 2 * count, panels))
    strengths = [block.astype(jnp.bfloat16) for block in received[:count]]
    forward = forward_of(pairs_ref, strengths, count)
    potential = [potential_ref[i] + value for i, value in enumerate(forward)]
    others = zip(decode(first_ref, count, panels), received[count:])
    adjoint = [middle_ref[i] + first + second for i, (first, second) in enumerate(others)]
    parts_of(blocks, potential, adjoint, *outs)


def slots_parts_kernel(blocks, potential_ref, adjoint_ref, first_ref, second_ref, *outs):
    count, panels = potential_ref.shape[:2]
    others = zip(decode(first_ref, count, panels), decode(second_ref, count, panels))
    adjoint = [adjoint_ref[count + i] + first + second for i, (first, second) in enumerate(others)]
    parts_of(blocks, [potential_ref[i] for i in range(count)], adjoint, *outs)


def slots_kernel(blocks, panels, chunk, *refs):
    (live_ref, *ids, kernels_ref), (first_ref, second_ref, *gathered) = refs[:4], refs[4:-6]
    potential_ref, adjoint_ref, held, stack, across, sems = refs[-6:]
    group_blocks = potential_ref.shape[0]

    def fetch(c):
        rows = pl.ds(c * chunk, chunk)
        return pltpu.make_async_copy(kernels_ref.at[rows], held.at[rows], sems.at[c])

    def prepare():
        for c in range(held.shape[0] // chunk):
            fetch(c).start()
        potential_ref[...] = jnp.zeros(potential_ref.shape, potential_ref.dtype)
        adjoint_ref[...] = jnp.zeros(adjoint_ref.shape, adjoint_ref.dtype)
        for i, block in enumerate(strengths_of(first_ref, gathered, second_ref, blocks, panels)):
            stack[i] = stacked(block)
        for i, block in enumerate(part_of(gathered, blocks, panels, 1)):
            across[i] = crossed(block)

    def work(slot):
        target, source = place(*ids, slot, group_blocks, blocks)
        real, imag = held[slot, 0], held[slot, 1]
        potential_ref[target] += jnp.dot(
            jnp.concatenate([real, imag], axis=1), stack[source], preferred_element_type=jnp.float32
        )
        adjoint_ref[source] += jnp.dot(
            across[target], jnp.concatenate([real, imag], axis=0), preferred_element_type=jnp.float32
        )

    prepare()
    each_slot(chunk, live_ref, held.shape[0], work, lambda c: fetch(c).wait())


def code_kernel(adjoint_ref, *outs):
    count = adjoint_ref.shape[0] // 3
    for first, out_ref in zip((0, 2 * count), outs):
        encode([adjoint_ref[first + i] for i in range(count)], out_ref)


def finish_kernel(blocks, panels, own_ref, parts_ref, potential_ref, adjoint_ref):
    me = lax.axis_index("clu")
    total = [own_ref[rows_of(i, panels)] for i in range(2 * blocks)]
    for k in range(1, parts_ref.shape[0]):
        total = [a + b for a, b in zip(total, decode(parts_ref.at[me ^ k], 2 * blocks, panels))]
    for b in range(blocks):
        potential_ref[rows_of(b, panels)] = total[b]
        adjoint_ref[rows_of(b, panels)] = total[blocks + b].T


def local(strengths, adjoint_weights, kernels, target_ids, source_ids, live_slots):
    slots, _, panels, _ = kernels.shape
    width = strengths.shape[1]
    blocks = strengths.shape[0] // panels
    clusters = lax.axis_size("clu")
    group_blocks = clusters * blocks
    sources = 3 * group_blocks
    pairs = group_blocks * sources
    chunk = 8 if slots % 8 == 0 else 1
    in_vmem, in_smem, in_hbm = (pl.BlockSpec(memory_space=m) for m in (pltpu.VMEM, pltpu.SMEM, pltpu.HBM))
    f32, bf16 = jnp.float32, jnp.bfloat16

    def call(body, shapes, args, specs=None, scratch=(), mib=8, flops=0, aliases=(), out_specs=None):
        single = not isinstance(shapes, tuple)
        return pl.pallas_call(
            body,
            out_shape=shapes,
            input_output_aliases=dict(aliases),
            in_specs=specs or [in_vmem] * len(args),
            out_specs=out_specs or (in_vmem if single else (in_vmem,) * len(shapes)),
            scratch_shapes=scratch,
            compiler_params=pltpu.CompilerParams(vmem_limit_bytes=mib << 20),
            cost_estimate=pl.CostEstimate(flops=flops, bytes_accessed=1 << 20, transcendentals=0),
        )(*args)

    def shape(*dims, kind=f32):
        return jax.ShapeDtypeStruct(dims, kind)

    zeros = [pltpu.VMEM((pairs, 2 * panels, panels), f32)] if pairs <= slots else []
    kept_ids = [pltpu.SMEM(x.shape, x.dtype) for x in (target_ids, source_ids)]
    mine, *ids = call(
        pack_kernel,
        (shape(2 * blocks * panels, width, kind=bf16), *kept_ids, *zeros),
        [pltpu.with_memory_space_constraint(x, pltpu.HBM) for x in (strengths, adjoint_weights, target_ids, source_ids)],
        [in_hbm] * 4,
        [pltpu.SemaphoreType.DMA((4,))],
        out_specs=(in_vmem, in_smem, in_smem) + (in_vmem,) * len(zeros),
        flops=1 << 34,
    )
    ids, zeros = ids[:2], ids[2:]
    slot_args = (live_slots, *(pltpu.with_memory_space_constraint(x, pltpu.SMEM) for x in ids))
    gathered = [exchange(mine, "clu", k) for k in range(clusters - 1, 0, -1)]
    gathered = [mine] + gathered[::-1]

    def group_strengths(token):
        return call(
            functools.partial(group_kernel, blocks, panels),
            shape(group_blocks * panels, width, kind=bf16),
            (token, *gathered),
            [in_hbm] + [in_vmem] * clusters,
        )

    def coded(count):
        return shape(count * panels + EXPONENT_ROWS * pl.cdiv(count, EXPONENT_ROWS), width, kind=jnp.int16)

    block_sums = shape(group_blocks, panels, width)
    if pairs <= slots:
        total = call(
            functools.partial(combine_kernel, group_blocks, blocks, chunk),
            pltpu.VMEM((pairs, 2 * panels, panels), f32),
            (*slot_args, *(pltpu.with_memory_space_constraint(x, pltpu.VMEM) for x in (kernels, *zeros))),
            [in_smem] * 3 + [in_vmem] * 2,
            flops=1 << 33,
            aliases=[(4, 0)],
        )
        own = group_strengths(total)
        first = exchange_beside(own, 0)
        total = pltpu.with_memory_space_constraint(total, pltpu.VMEM)
        second_pairs = pairs // 3
        kept_second, across, upper = call(
            functools.partial(second_kernel, blocks, panels, group_blocks),
            (
                pltpu.VMEM((2, second_pairs, 2 * panels, panels), bf16),
                shape(width, 2 * group_blocks * panels, kind=bf16),
                coded(2 * group_blocks),
            ),
            (own, total, *gathered),
            [in_hbm] + [in_vmem] * (1 + clusters),
            flops=1 << 33,
        )
        kept, middle, lower = call(
            functools.partial(first_kernel, group_blocks),
            (pltpu.VMEM((2, pairs - second_pairs, 2 * panels, panels), bf16), block_sums, coded(group_blocks)),
            (first, total, across),
            [in_hbm] + [in_vmem] * 2,
            flops=1 << 33,
        )
        kept, kept_second = (pltpu.with_memory_space_constraint(x, pltpu.VMEM) for x in (kept, kept_second))
        potential = call(functools.partial(forward_kernel, blocks), block_sums, (kept, first, *gathered))
        upper, lower = exchange_beside(upper, 1), exchange_beside(lower, 0)
        parts_body, parts_args = parts_kernel, (kept_second, potential, middle, lower, upper)
    else:
        own = group_strengths(mine)
        first, second = exchange_beside(own, 0), exchange_beside(own, 1)
        potential, adjoint = call(
            functools.partial(slots_kernel, blocks, panels, chunk),
            (block_sums, shape(sources, width, panels)),
            (*slot_args, pltpu.with_memory_space_constraint(kernels, pltpu.HBM), first, second, *gathered),
            [in_smem] * 3 + [in_hbm] + [in_vmem] * (2 + clusters),
            [
                pltpu.VMEM(kernels.shape, bf16),
                pltpu.VMEM((sources, 2 * panels, width), bf16),
                pltpu.VMEM((group_blocks, width, 2 * panels), bf16),
                pltpu.SemaphoreType.DMA((slots // chunk,)),
            ],
            mib=40,
        )
        lower, upper = call(code_kernel, (coded(group_blocks),) * 2, (adjoint,))
        upper, lower = exchange_beside(upper, 1), exchange_beside(lower, 0)
        parts_body, parts_args = slots_parts_kernel, (potential, adjoint, lower, upper)
    mine, parts = call(
        functools.partial(parts_body, blocks),
        (shape(2 * blocks * panels, width), shape(clusters, *coded(2 * blocks).shape, kind=jnp.int16)),
        parts_args,
    )
    parts = lax.all_to_all(parts, "clu", 0, 0, tiled=True)
    out = shape(blocks * panels, width)
    return tuple(call(functools.partial(finish_kernel, blocks, panels), (out, out), (mine, parts)))


def solution(mesh):
    return jax.shard_map(
        local,
        mesh=mesh,
        in_specs=(
            P(("grp", "clu"), None),
            P(("grp", "clu"), None),
            P(("grp", "clu"), None, None, None),
            P(("grp", "clu")),
            P(("grp", "clu")),
            P(("grp", "clu")),
        ),
        out_specs=(P(("grp", "clu"), None), P(("grp", "clu"), None)),
        check_vma=False,
    )
```

```python
import functools

import jax
import jax.numpy as jnp
from jax import lax
from jax.experimental import pallas as pl
from jax.experimental.pallas import tpu as pltpu
from jax.sharding import PartitionSpec as P

EXPONENT_ROWS = 16
TINY = 2.0**-110


def exchange(value, axis, step):
    return lax.ppermute(value, axis, [(i, i ^ step) for i in range(lax.axis_size(axis))])


def exchange_beside(value, first):
    groups = lax.axis_size("grp")
    partner = [i + 1 if (i - first) % 2 == 0 else i - 1 for i in range(groups)]
    return lax.ppermute(value, "grp", [(i, j if 0 <= j < groups else i) for i, j in enumerate(partner)])


def rows_of(index, panels):
    return pl.ds(index * panels, panels)


def encode(values, out_ref):
    exponents = []
    for i, value in enumerate(values):
        largest = jnp.max(jnp.abs(value), axis=0, keepdims=True)
        exponent = jnp.floor(jnp.log2(jnp.maximum(largest, TINY))) + 1.0
        scaled = jnp.round(value * jnp.exp2(15.0 - exponent))
        scaled = jnp.minimum(jnp.maximum(scaled, -32767.0), 32767.0)
        out_ref[rows_of(i, value.shape[0])] = scaled.astype(jnp.int32).astype(jnp.int16)
        exponents.append(exponent)
    last = out_ref.shape[0] - EXPONENT_ROWS * pl.cdiv(len(values), EXPONENT_ROWS)
    exponents += [jnp.zeros_like(exponents[0])] * (out_ref.shape[0] - last - len(exponents))
    table = jnp.concatenate(exponents, axis=0)
    out_ref[last:] = table.astype(jnp.int32).astype(jnp.int16)


def decode(ref, count, panels):
    table = ref[count * panels :].astype(jnp.int32).astype(jnp.float32)
    for i in range(count):
        value = ref[rows_of(i, panels)].astype(jnp.int32).astype(jnp.float32)
        yield value * jnp.exp2(table[i : i + 1] - 15.0)


def turned(block):
    half = block.shape[1] // 2
    wide = pltpu.roll(block.astype(jnp.float32), half, axis=1)
    lane = lax.broadcasted_iota(jnp.int32, wide.shape, 1)
    return jnp.where(lane < half, -wide, wide).astype(block.dtype)


def turned_rows(block):
    half = block.shape[0] // 2
    return jnp.concatenate([-block[half:], block[:half]], axis=0)


def place(target_ref, source_ref, slot, group_blocks, blocks):
    group, mine = lax.axis_index("grp"), lax.axis_index("clu") * blocks
    target = (target_ref[slot] - group * group_blocks) ^ mine
    source = (source_ref[slot] - (group - 1) * group_blocks) ^ mine
    offset = lax.div(source, group_blocks) - 1
    return target, jnp.where(group % 2 == 0, source - 2 * offset * group_blocks, source)


def each_slot(chunk, live_ref, slots, work, wait=None):
    live = live_ref[0]

    @pl.loop(0, slots // chunk if wait else pl.cdiv(live, chunk))
    def _(c):
        if wait:
            wait(c)
        first = c * chunk

        @pl.when(first + chunk <= live)
        def _():
            for i in range(chunk):
                work(first + i)

        @pl.when(first + chunk > live)
        def _():
            @pl.loop(first, jnp.maximum(live, first))
            def _(slot):
                work(slot)


def combine_kernel(group_blocks, blocks, chunk, live_ref, target_ref, source_ref, kernels_ref, _, total):
    def add(slot):
        target, source = place(target_ref, source_ref, slot, group_blocks, blocks)
        pair = source * group_blocks + target
        total[pair] += kernels_ref[slot].reshape(total.shape[1:]).astype(jnp.float32)

    each_slot(chunk, live_ref, kernels_ref.shape[0], add)


def split(total, first, out_ref):
    @pl.loop(0, out_ref.shape[1])
    def _(pair):
        value = total[first + pair]
        high = value.astype(jnp.bfloat16)
        out_ref[0, pair] = high
        out_ref[1, pair] = (value - high.astype(jnp.float32)).astype(jnp.bfloat16)


def pack_kernel(strengths_ref, weights_ref, target_ref, source_ref, out_ref, *rest):
    *kept, sems = rest
    ids, zeros = kept[:2], kept[2:]
    rows = strengths_ref.shape[0]
    moves = [(ref, out_ref.at[pl.ds(i * rows, rows)]) for i, ref in enumerate((strengths_ref, weights_ref))]
    moves += zip((target_ref, source_ref), ids)
    copies = [pltpu.make_async_copy(ref, to, sems.at[i]) for i, (ref, to) in enumerate(moves)]
    for copy in copies:
        copy.start()
    for ref in zeros:

        @pl.loop(0, ref.shape[0])
        def _(i):
            ref[i] = jnp.zeros(ref.shape[1:], ref.dtype)

    for copy in copies:
        copy.wait()


def group_kernel(blocks, panels, _, *refs):
    *gathered, out_ref = refs
    for i, block in enumerate(part_of(gathered, blocks, panels, 0)):
        out_ref[i * panels : (i + 1) * panels] = block


def part_of(gathered, blocks, panels, part):
    for ref in gathered:
        for b in range(blocks):
            yield ref[pl.ds((part * blocks + b) * panels, panels), :]


def strengths_of(first_ref, gathered, second_ref, blocks, panels):
    for i in range(first_ref.shape[0] // panels):
        yield first_ref[rows_of(i, panels)]
    yield from part_of(gathered, blocks, panels, 0)
    for i in range(second_ref.shape[0] // panels):
        yield second_ref[rows_of(i, panels)]


def crossed(block):
    block = block.astype(jnp.float32).T
    return jnp.concatenate([block, turned_rows(block)], axis=1).astype(jnp.bfloat16)


def stacked(block):
    return jnp.concatenate([block, turned(block)], axis=0)


def adjoint_of(pairs_ref, across_ref, first, count):
    width = pairs_ref.shape[3]
    weights = across_ref[...]
    targets = weights.shape[1] // pairs_ref.shape[2]
    both = jnp.concatenate([weights, weights], axis=1)
    step = 2 if count % 2 == 0 else 1
    for i in range(0, count, step):
        columns = []
        for j in range(first + i, first + i + step):
            tiles = [pairs_ref[h, j * targets + t] for h in range(2) for t in range(targets)]
            columns.append(jnp.concatenate(tiles, axis=0))
        product = jnp.dot(both, jnp.concatenate(columns, axis=1), preferred_element_type=jnp.float32)
        for j in range(step):
            yield product[:, j * width : (j + 1) * width]


def second_kernel(blocks, panels, count, _, total, *refs):
    *gathered, pairs_ref, across_ref, out_ref = refs
    split(total, total.shape[0] - pairs_ref.shape[1], pairs_ref)
    for i, block in enumerate(part_of(gathered, blocks, panels, 1)):
        across_ref[:, 2 * i * panels : 2 * (i + 1) * panels] = crossed(block)
    strengths = [block.astype(jnp.float32) for block in part_of(gathered, blocks, panels, 0)]
    encode(strengths + list(adjoint_of(pairs_ref, across_ref, 0, count)), out_ref)


def first_kernel(count, _, total, across_ref, pairs_ref, out_ref):
    split(total, 0, pairs_ref)
    encode(list(adjoint_of(pairs_ref, across_ref, 0, count)), out_ref)


def forward_of(pairs_ref, strengths, targets):
    panels = pairs_ref.shape[2] // 2
    stack = jnp.concatenate([stacked(x) for x in strengths], axis=0)
    for t in range(targets):
        halves = []
        for h in range(2):
            tiles = []
            for pair in range(t, pairs_ref.shape[1], targets):
                tiles += [pairs_ref[h, pair, :panels], pairs_ref[h, pair, panels:]]
            halves.append(jnp.concatenate(tiles, axis=1))
        product = jnp.dot(jnp.concatenate(halves, axis=0), stack, preferred_element_type=jnp.float32)
        yield product[:panels] + product[panels:]


def inner_kernel(blocks, total, across_ref, first_pairs_ref, first_ref, *refs):
    *gathered, potential_ref, middle_ref, pairs_ref = refs
    targets, panels = potential_ref.shape[:2]
    split(total, pairs_ref.shape[1], pairs_ref)
    for i, value in enumerate(adjoint_of(pairs_ref, across_ref, 0, targets)):
        middle_ref[i] = value
    strengths = [first_ref[rows_of(i, panels)] for i in range(targets)]
    own = list(part_of(gathered, blocks, panels, 0))
    for t, value in enumerate(forward_of(first_pairs_ref, strengths, targets)):
        potential_ref[t] = value
    for t, value in enumerate(forward_of(pairs_ref, own, targets)):
        potential_ref[t] += value


def parts_of(blocks, potential, adjoint, own_ref, *outs):
    panels = potential[0].shape[0]
    for i in range(blocks):
        own_ref[rows_of(i, panels)] = potential[i]
        own_ref[rows_of(blocks + i, panels)] = adjoint[i]
    for k, out_ref in enumerate(outs, 1):
        rows = slice(k * blocks, (k + 1) * blocks)
        encode(potential[rows] + adjoint[rows], out_ref)


def parts_kernel(blocks, pairs_ref, potential_ref, middle_ref, first_ref, second_ref, *outs):
    count, panels = potential_ref.shape[:2]
    received = list(decode(second_ref, 2 * count, panels))
    strengths = [block.astype(jnp.bfloat16) for block in received[:count]]
    forward = forward_of(pairs_ref, strengths, count)
    potential = [potential_ref[i] + value for i, value in enumerate(forward)]
    others = zip(decode(first_ref, count, panels), received[count:])
    adjoint = [middle_ref[i] + first + second for i, (first, second) in enumerate(others)]
    parts_of(blocks, potential, adjoint, *outs)


def slots_parts_kernel(blocks, potential_ref, adjoint_ref, first_ref, second_ref, *outs):
    count, panels = potential_ref.shape[:2]
    others = zip(decode(first_ref, count, panels), decode(second_ref, count, panels))
    adjoint = [adjoint_ref[count + i] + first + second for i, (first, second) in enumerate(others)]
    parts_of(blocks, [potential_ref[i] for i in range(count)], adjoint, *outs)


def slots_kernel(blocks, panels, chunk, *refs):
    (live_ref, *ids, kernels_ref), (first_ref, second_ref, *gathered) = refs[:4], refs[4:-6]
    potential_ref, adjoint_ref, held, stack, across, sems = refs[-6:]
    group_blocks = potential_ref.shape[0]

    def fetch(c):
        rows = pl.ds(c * chunk, chunk)
        return pltpu.make_async_copy(kernels_ref.at[rows], held.at[rows], sems.at[c])

    def prepare():
        for c in range(held.shape[0] // chunk):
            fetch(c).start()
        potential_ref[...] = jnp.zeros(potential_ref.shape, potential_ref.dtype)
        adjoint_ref[...] = jnp.zeros(adjoint_ref.shape, adjoint_ref.dtype)
        for i, block in enumerate(strengths_of(first_ref, gathered, second_ref, blocks, panels)):
            stack[i] = stacked(block)
        for i, block in enumerate(part_of(gathered, blocks, panels, 1)):
            across[i] = crossed(block)

    def work(slot):
        target, source = place(*ids, slot, group_blocks, blocks)
        real, imag = held[slot, 0], held[slot, 1]
        potential_ref[target] += jnp.dot(
            jnp.concatenate([real, imag], axis=1), stack[source], preferred_element_type=jnp.float32
        )
        adjoint_ref[source] += jnp.dot(
            across[target], jnp.concatenate([real, imag], axis=0), preferred_element_type=jnp.float32
        )

    prepare()
    each_slot(chunk, live_ref, held.shape[0], work, lambda c: fetch(c).wait())


def code_kernel(adjoint_ref, *outs):
    count = adjoint_ref.shape[0] // 3
    for first, out_ref in zip((0, 2 * count), outs):
        encode([adjoint_ref[first + i] for i in range(count)], out_ref)


def finish_kernel(blocks, panels, own_ref, *refs):
    *parts, potential_ref, adjoint_ref = refs
    total = [own_ref[rows_of(i, panels)] for i in range(2 * blocks)]
    for ref in parts:
        total = [a + b for a, b in zip(total, decode(ref, 2 * blocks, panels))]
    for b in range(blocks):
        potential_ref[rows_of(b, panels)] = total[b]
        adjoint_ref[rows_of(b, panels)] = total[blocks + b].T


def local(strengths, adjoint_weights, kernels, target_ids, source_ids, live_slots):
    slots, _, panels, _ = kernels.shape
    width = strengths.shape[1]
    blocks = strengths.shape[0] // panels
    clusters = lax.axis_size("clu")
    group_blocks = clusters * blocks
    sources = 3 * group_blocks
    pairs = group_blocks * sources
    chunk = 8 if slots % 8 == 0 else 1
    in_vmem, in_smem, in_hbm = (pl.BlockSpec(memory_space=m) for m in (pltpu.VMEM, pltpu.SMEM, pltpu.HBM))
    f32, bf16 = jnp.float32, jnp.bfloat16

    def call(body, shapes, args, specs=None, scratch=(), mib=8, flops=0, aliases=(), out_specs=None):
        single = not isinstance(shapes, tuple)
        return pl.pallas_call(
            body,
            out_shape=shapes,
            input_output_aliases=dict(aliases),
            in_specs=specs or [in_vmem] * len(args),
            out_specs=out_specs or (in_vmem if single else (in_vmem,) * len(shapes)),
            scratch_shapes=scratch,
            compiler_params=pltpu.CompilerParams(vmem_limit_bytes=mib << 20),
            cost_estimate=pl.CostEstimate(flops=flops, bytes_accessed=1 << 20, transcendentals=0),
        )(*args)

    def shape(*dims, kind=f32):
        return jax.ShapeDtypeStruct(dims, kind)

    zeros = [pltpu.VMEM((pairs, 2 * panels, panels), f32)] if pairs <= slots else []
    kept_ids = [pltpu.SMEM(x.shape, x.dtype) for x in (target_ids, source_ids)]
    mine, *ids = call(
        pack_kernel,
        (shape(2 * blocks * panels, width, kind=bf16), *kept_ids, *zeros),
        [pltpu.with_memory_space_constraint(x, pltpu.HBM) for x in (strengths, adjoint_weights, target_ids, source_ids)],
        [in_hbm] * 4,
        [pltpu.SemaphoreType.DMA((4,))],
        out_specs=(in_vmem, in_smem, in_smem) + (in_vmem,) * len(zeros),
        flops=1 << 34,
    )
    ids, zeros = ids[:2], ids[2:]
    slot_args = (live_slots, *(pltpu.with_memory_space_constraint(x, pltpu.SMEM) for x in ids))
    gathered = [exchange(mine, "clu", k) for k in range(clusters - 1, 0, -1)]
    gathered = [mine] + gathered[::-1]

    def group_strengths(token):
        return call(
            functools.partial(group_kernel, blocks, panels),
            shape(group_blocks * panels, width, kind=bf16),
            (token, *gathered),
            [in_hbm] + [in_vmem] * clusters,
        )

    def coded(count):
        return shape(count * panels + EXPONENT_ROWS * pl.cdiv(count, EXPONENT_ROWS), width, kind=jnp.int16)

    block_sums = shape(group_blocks, panels, width)
    if pairs <= slots:
        total = call(
            functools.partial(combine_kernel, group_blocks, blocks, chunk),
            pltpu.VMEM((pairs, 2 * panels, panels), f32),
            (*slot_args, *(pltpu.with_memory_space_constraint(x, pltpu.VMEM) for x in (kernels, *zeros))),
            [in_smem] * 3 + [in_vmem] * 2,
            flops=1 << 33,
            aliases=[(4, 0)],
        )
        own = group_strengths(total)
        first = exchange_beside(own, 0)
        total = pltpu.with_memory_space_constraint(total, pltpu.VMEM)
        kept_shape = pltpu.VMEM((2, pairs // 3, 2 * panels, panels), bf16)
        kept_second, across, upper = call(
            functools.partial(second_kernel, blocks, panels, group_blocks),
            (
                kept_shape,
                shape(width, 2 * group_blocks * panels, kind=bf16),
                coded(2 * group_blocks),
            ),
            (own, total, *gathered),
            [in_hbm] + [in_vmem] * (1 + clusters),
            flops=1 << 33,
        )
        kept_first, lower = call(
            functools.partial(first_kernel, group_blocks),
            (kept_shape, coded(group_blocks)),
            (first, total, across),
            [in_hbm] + [in_vmem] * 2,
            flops=1 << 33,
        )
        kept_first, kept_second = (pltpu.with_memory_space_constraint(x, pltpu.VMEM) for x in (kept_first, kept_second))
        potential, middle = call(
            functools.partial(inner_kernel, blocks),
            (block_sums, block_sums),
            (total, across, kept_first, first, *gathered),
            scratch=[kept_shape],
        )
        upper, lower = exchange_beside(upper, 1), exchange_beside(lower, 0)
        parts_body, parts_args = parts_kernel, (kept_second, potential, middle, lower, upper)
    else:
        own = group_strengths(mine)
        first, second = exchange_beside(own, 0), exchange_beside(own, 1)
        potential, adjoint = call(
            functools.partial(slots_kernel, blocks, panels, chunk),
            (block_sums, shape(sources, width, panels)),
            (*slot_args, pltpu.with_memory_space_constraint(kernels, pltpu.HBM), first, second, *gathered),
            [in_smem] * 3 + [in_hbm] + [in_vmem] * (2 + clusters),
            [
                pltpu.VMEM(kernels.shape, bf16),
                pltpu.VMEM((sources, 2 * panels, width), bf16),
                pltpu.VMEM((group_blocks, width, 2 * panels), bf16),
                pltpu.SemaphoreType.DMA((slots // chunk,)),
            ],
            mib=40,
        )
        lower, upper = call(code_kernel, (coded(group_blocks),) * 2, (adjoint,))
        upper, lower = exchange_beside(upper, 1), exchange_beside(lower, 0)
        parts_body, parts_args = slots_parts_kernel, (potential, adjoint, lower, upper)
    mine, *parts = call(
        functools.partial(parts_body, blocks),
        (shape(2 * blocks * panels, width),) + (coded(2 * blocks),) * (clusters - 1),
        parts_args,
    )
    parts = [exchange(parts[k - 1], "clu", k) for k in range(clusters - 1, 0, -1)]
    out = shape(blocks * panels, width)
    return tuple(call(functools.partial(finish_kernel, blocks, panels), (out, out), (mine, *parts)))


def solution(mesh):
    return jax.shard_map(
        local,
        mesh=mesh,
        in_specs=(
            P(("grp", "clu"), None),
            P(("grp", "clu"), None),
            P(("grp", "clu"), None, None, None),
            P(("grp", "clu")),
            P(("grp", "clu")),
            P(("grp", "clu")),
        ),
        out_specs=(P(("grp", "clu"), None), P(("grp", "clu"), None)),
        check_vma=False,
    )
```

```python
import functools

import jax
import jax.numpy as jnp
from jax import lax
from jax.experimental import pallas as pl
from jax.experimental.pallas import tpu as pltpu
from jax.sharding import PartitionSpec as P

EXPONENT_ROWS = 16
TINY = 2.0**-110


def exchange(value, axis, step):
    return lax.ppermute(value, axis, [(i, i ^ step) for i in range(lax.axis_size(axis))])


def exchange_beside(value, first):
    groups = lax.axis_size("grp")
    partner = [i + 1 if (i - first) % 2 == 0 else i - 1 for i in range(groups)]
    return lax.ppermute(value, "grp", [(i, j if 0 <= j < groups else i) for i, j in enumerate(partner)])


def rows_of(index, panels):
    return pl.ds(index * panels, panels)


def encode(values, out_ref):
    exponents = []
    for i, value in enumerate(values):
        largest = jnp.max(jnp.abs(value), axis=0, keepdims=True)
        exponent = jnp.floor(jnp.log2(jnp.maximum(largest, TINY))) + 1.0
        scaled = jnp.round(value * jnp.exp2(15.0 - exponent))
        scaled = jnp.minimum(jnp.maximum(scaled, -32767.0), 32767.0)
        out_ref[rows_of(i, value.shape[0])] = scaled.astype(jnp.int32).astype(jnp.int16)
        exponents.append(exponent)
    last = out_ref.shape[0] - EXPONENT_ROWS * pl.cdiv(len(values), EXPONENT_ROWS)
    exponents += [jnp.zeros_like(exponents[0])] * (out_ref.shape[0] - last - len(exponents))
    table = jnp.concatenate(exponents, axis=0)
    out_ref[last:] = table.astype(jnp.int32).astype(jnp.int16)


def decode(ref, count, panels):
    table = ref[count * panels :].astype(jnp.int32).astype(jnp.float32)
    for i in range(count):
        value = ref[rows_of(i, panels)].astype(jnp.int32).astype(jnp.float32)
        yield value * jnp.exp2(table[i : i + 1] - 15.0)


def turned(block):
    half = block.shape[1] // 2
    wide = pltpu.roll(block.astype(jnp.float32), half, axis=1)
    lane = lax.broadcasted_iota(jnp.int32, wide.shape, 1)
    return jnp.where(lane < half, -wide, wide).astype(block.dtype)


def turned_rows(block):
    half = block.shape[0] // 2
    return jnp.concatenate([-block[half:], block[:half]], axis=0)


def place(target_ref, source_ref, slot, group_blocks, blocks):
    group, mine = lax.axis_index("grp"), lax.axis_index("clu") * blocks
    target = (target_ref[slot] - group * group_blocks) ^ mine
    source = (source_ref[slot] - (group - 1) * group_blocks) ^ mine
    offset = lax.div(source, group_blocks) - 1
    return target, jnp.where(group % 2 == 0, source - 2 * offset * group_blocks, source)


def each_slot(chunk, live_ref, slots, work, wait=None):
    live = live_ref[0]

    @pl.loop(0, slots // chunk if wait else pl.cdiv(live, chunk))
    def _(c):
        if wait:
            wait(c)
        first = c * chunk

        @pl.when(first + chunk <= live)
        def _():
            for i in range(chunk):
                work(first + i)

        @pl.when(first + chunk > live)
        def _():
            @pl.loop(first, jnp.maximum(live, first))
            def _(slot):
                work(slot)


def combine_kernel(group_blocks, blocks, chunk, live_ref, target_ref, source_ref, kernels_ref, _, total):
    def add(slot):
        target, source = place(target_ref, source_ref, slot, group_blocks, blocks)
        pair = source * group_blocks + target
        total[pair] += kernels_ref[slot].reshape(total.shape[1:]).astype(jnp.float32)

    each_slot(chunk, live_ref, kernels_ref.shape[0], add)


def split(total, first, out_ref):
    @pl.loop(0, out_ref.shape[1])
    def _(pair):
        value = total[first + pair]
        high = value.astype(jnp.bfloat16)
        out_ref[0, pair] = high
        out_ref[1, pair] = (value - high.astype(jnp.float32)).astype(jnp.bfloat16)


def pack_kernel(strengths_ref, weights_ref, target_ref, source_ref, out_ref, *rest):
    *kept, sems = rest
    ids, zeros = kept[:2], kept[2:]
    rows = strengths_ref.shape[0]
    moves = [(ref, out_ref.at[pl.ds(i * rows, rows)]) for i, ref in enumerate((strengths_ref, weights_ref))]
    moves += zip((target_ref, source_ref), ids)
    copies = [pltpu.make_async_copy(ref, to, sems.at[i]) for i, (ref, to) in enumerate(moves)]
    for copy in copies:
        copy.start()
    for ref in zeros:

        @pl.loop(0, ref.shape[0])
        def _(i):
            ref[i] = jnp.zeros(ref.shape[1:], ref.dtype)

    for copy in copies:
        copy.wait()


def group_kernel(blocks, panels, _, *refs):
    *gathered, out_ref = refs
    for i, block in enumerate(part_of(gathered, blocks, panels, 0)):
        out_ref[i * panels : (i + 1) * panels] = block


def part_of(gathered, blocks, panels, part):
    for ref in gathered:
        for b in range(blocks):
            yield ref[pl.ds((part * blocks + b) * panels, panels), :]


def strengths_of(first_ref, gathered, second_ref, blocks, panels):
    for i in range(first_ref.shape[0] // panels):
        yield first_ref[rows_of(i, panels)]
    yield from part_of(gathered, blocks, panels, 0)
    for i in range(second_ref.shape[0] // panels):
        yield second_ref[rows_of(i, panels)]


def crossed(block):
    block = block.astype(jnp.float32).T
    return jnp.concatenate([block, turned_rows(block)], axis=1).astype(jnp.bfloat16)


def stacked(block):
    return jnp.concatenate([block, turned(block)], axis=0)


def adjoint_of(pairs_ref, across_ref, first, count):
    width = pairs_ref.shape[3]
    weights = across_ref[...]
    targets = weights.shape[1] // pairs_ref.shape[2]
    both = jnp.concatenate([weights, weights], axis=1)
    step = 2 if count % 2 == 0 else 1
    for i in range(0, count, step):
        columns = []
        for j in range(first + i, first + i + step):
            tiles = [pairs_ref[h, j * targets + t] for h in range(2) for t in range(targets)]
            columns.append(jnp.concatenate(tiles, axis=0))
        product = jnp.dot(both, jnp.concatenate(columns, axis=1), preferred_element_type=jnp.float32)
        for j in range(step):
            yield product[:, j * width : (j + 1) * width]


def second_kernel(blocks, panels, count, _, total, *refs):
    *gathered, pairs_ref, across_ref, out_ref = refs
    split(total, total.shape[0] - pairs_ref.shape[1], pairs_ref)
    for i, block in enumerate(part_of(gathered, blocks, panels, 1)):
        across_ref[:, 2 * i * panels : 2 * (i + 1) * panels] = crossed(block)
    strengths = [block.astype(jnp.float32) for block in part_of(gathered, blocks, panels, 0)]
    encode(strengths + list(adjoint_of(pairs_ref, across_ref, 0, count)), out_ref)


def first_kernel(count, _, total, across_ref, pairs_ref, out_ref):
    split(total, 0, pairs_ref)
    encode(list(adjoint_of(pairs_ref, across_ref, 0, count)), out_ref)


def forward_of(pairs_ref, strengths, targets):
    panels = pairs_ref.shape[2] // 2
    stack = jnp.concatenate([stacked(x) for x in strengths], axis=0)
    for t in range(targets):
        halves = []
        for h in range(2):
            tiles = []
            for pair in range(t, pairs_ref.shape[1], targets):
                tiles += [pairs_ref[h, pair, :panels], pairs_ref[h, pair, panels:]]
            halves.append(jnp.concatenate(tiles, axis=1))
        product = jnp.dot(jnp.concatenate(halves, axis=0), stack, preferred_element_type=jnp.float32)
        yield product[:panels] + product[panels:]


def inner_kernel(blocks, total, across_ref, first_pairs_ref, first_ref, *refs):
    *gathered, potential_ref, middle_ref, pairs_ref = refs
    targets, panels = potential_ref.shape[:2]
    split(total, pairs_ref.shape[1], pairs_ref)
    for i, value in enumerate(adjoint_of(pairs_ref, across_ref, 0, targets)):
        middle_ref[i] = value
    strengths = [first_ref[rows_of(i, panels)] for i in range(targets)]
    own = list(part_of(gathered, blocks, panels, 0))
    for t, value in enumerate(forward_of(first_pairs_ref, strengths, targets)):
        potential_ref[t] = value
    for t, value in enumerate(forward_of(pairs_ref, own, targets)):
        potential_ref[t] += value


def parts_of(blocks, potential, adjoint, own_ref, *outs):
    panels = potential[0].shape[0]
    for i in range(blocks):
        own_ref[rows_of(i, panels)] = potential[i]
        own_ref[rows_of(blocks + i, panels)] = adjoint[i]
    for k, out_ref in enumerate(outs, 1):
        rows = slice(k * blocks, (k + 1) * blocks)
        encode(potential[rows] + adjoint[rows], out_ref)


def parts_kernel(blocks, pairs_ref, potential_ref, middle_ref, first_ref, second_ref, *outs):
    count, panels = potential_ref.shape[:2]
    received = list(decode(second_ref, 2 * count, panels))
    strengths = [block.astype(jnp.bfloat16) for block in received[:count]]
    forward = forward_of(pairs_ref, strengths, count)
    potential = [potential_ref[i] + value for i, value in enumerate(forward)]
    others = zip(decode(first_ref, count, panels), received[count:])
    adjoint = [middle_ref[i] + first + second for i, (first, second) in enumerate(others)]
    parts_of(blocks, potential, adjoint, *outs)


def slots_parts_kernel(blocks, potential_ref, adjoint_ref, first_ref, second_ref, *outs):
    count, panels = potential_ref.shape[:2]
    others = zip(decode(first_ref, count, panels), decode(second_ref, count, panels))
    adjoint = [adjoint_ref[count + i] + first + second for i, (first, second) in enumerate(others)]
    parts_of(blocks, [potential_ref[i] for i in range(count)], adjoint, *outs)


def slots_kernel(blocks, panels, chunk, *refs):
    (live_ref, *ids, kernels_ref), (first_ref, second_ref, *gathered) = refs[:4], refs[4:-6]
    potential_ref, adjoint_ref, held, stack, across, sems = refs[-6:]
    group_blocks = potential_ref.shape[0]

    def fetch(c):
        rows = pl.ds(c * chunk, chunk)
        return pltpu.make_async_copy(kernels_ref.at[rows], held.at[rows], sems.at[c])

    def prepare():
        for c in range(held.shape[0] // chunk):
            fetch(c).start()
        potential_ref[...] = jnp.zeros(potential_ref.shape, potential_ref.dtype)
        adjoint_ref[...] = jnp.zeros(adjoint_ref.shape, adjoint_ref.dtype)
        for i, block in enumerate(strengths_of(first_ref, gathered, second_ref, blocks, panels)):
            stack[i] = stacked(block)
        for i, block in enumerate(part_of(gathered, blocks, panels, 1)):
            across[i] = crossed(block)

    def work(slot):
        target, source = place(*ids, slot, group_blocks, blocks)
        real, imag = held[slot, 0], held[slot, 1]
        potential_ref[target] += jnp.dot(
            jnp.concatenate([real, imag], axis=1), stack[source], preferred_element_type=jnp.float32
        )
        adjoint_ref[source] += jnp.dot(
            across[target], jnp.concatenate([real, imag], axis=0), preferred_element_type=jnp.float32
        )

    prepare()
    each_slot(chunk, live_ref, held.shape[0], work, lambda c: fetch(c).wait())


def code_kernel(adjoint_ref, *outs):
    count = adjoint_ref.shape[0] // 3
    for first, out_ref in zip((0, 2 * count), outs):
        encode([adjoint_ref[first + i] for i in range(count)], out_ref)


def add_kernel(blocks, panels, own_ref, *refs):
    *parts, out_ref = refs
    total = [own_ref[rows_of(i, panels)] for i in range(2 * blocks)]
    for ref in parts:
        total = [a + b for a, b in zip(total, decode(ref, 2 * blocks, panels))]
    for i, value in enumerate(total):
        out_ref[rows_of(i, panels)] = value


def finish_kernel(blocks, panels, sum_ref, last_ref, potential_ref, adjoint_ref):
    for i, value in enumerate(decode(last_ref, 2 * blocks, panels)):
        total = sum_ref[rows_of(i, panels)] + value
        if i < blocks:
            potential_ref[rows_of(i, panels)] = total
        else:
            adjoint_ref[rows_of(i - blocks, panels)] = total.T


def local(strengths, adjoint_weights, kernels, target_ids, source_ids, live_slots):
    slots, _, panels, _ = kernels.shape
    width = strengths.shape[1]
    blocks = strengths.shape[0] // panels
    clusters = lax.axis_size("clu")
    group_blocks = clusters * blocks
    sources = 3 * group_blocks
    pairs = group_blocks * sources
    chunk = 8 if slots % 8 == 0 else 1
    in_vmem, in_smem, in_hbm = (pl.BlockSpec(memory_space=m) for m in (pltpu.VMEM, pltpu.SMEM, pltpu.HBM))
    f32, bf16 = jnp.float32, jnp.bfloat16

    def call(body, shapes, args, specs=None, scratch=(), mib=8, flops=0, aliases=(), out_specs=None):
        single = not isinstance(shapes, tuple)
        return pl.pallas_call(
            body,
            out_shape=shapes,
            input_output_aliases=dict(aliases),
            in_specs=specs or [in_vmem] * len(args),
            out_specs=out_specs or (in_vmem if single else (in_vmem,) * len(shapes)),
            scratch_shapes=scratch,
            compiler_params=pltpu.CompilerParams(vmem_limit_bytes=mib << 20),
            cost_estimate=pl.CostEstimate(flops=flops, bytes_accessed=1 << 20, transcendentals=0),
        )(*args)

    def shape(*dims, kind=f32):
        return jax.ShapeDtypeStruct(dims, kind)

    zeros = [pltpu.VMEM((pairs, 2 * panels, panels), f32)] if pairs <= slots else []
    kept_ids = [pltpu.SMEM(x.shape, x.dtype) for x in (target_ids, source_ids)]
    mine, *ids = call(
        pack_kernel,
        (shape(2 * blocks * panels, width, kind=bf16), *kept_ids, *zeros),
        [pltpu.with_memory_space_constraint(x, pltpu.HBM) for x in (strengths, adjoint_weights, target_ids, source_ids)],
        [in_hbm] * 4,
        [pltpu.SemaphoreType.DMA((4,))],
        out_specs=(in_vmem, in_smem, in_smem) + (in_vmem,) * len(zeros),
        flops=1 << 34,
    )
    ids, zeros = ids[:2], ids[2:]
    slot_args = (live_slots, *(pltpu.with_memory_space_constraint(x, pltpu.SMEM) for x in ids))
    gathered = [exchange(mine, "clu", k) for k in range(clusters - 1, 0, -1)]
    gathered = [mine] + gathered[::-1]

    def group_strengths(token):
        return call(
            functools.partial(group_kernel, blocks, panels),
            shape(group_blocks * panels, width, kind=bf16),
            (token, *gathered),
            [in_hbm] + [in_vmem] * clusters,
        )

    def coded(count):
        return shape(count * panels + EXPONENT_ROWS * pl.cdiv(count, EXPONENT_ROWS), width, kind=jnp.int16)

    block_sums = shape(group_blocks, panels, width)
    if pairs <= slots:
        total = call(
            functools.partial(combine_kernel, group_blocks, blocks, chunk),
            pltpu.VMEM((pairs, 2 * panels, panels), f32),
            (*slot_args, *(pltpu.with_memory_space_constraint(x, pltpu.VMEM) for x in (kernels, *zeros))),
            [in_smem] * 3 + [in_vmem] * 2,
            flops=1 << 33,
            aliases=[(4, 0)],
        )
        own = group_strengths(total)
        first = exchange_beside(own, 0)
        total = pltpu.with_memory_space_constraint(total, pltpu.VMEM)
        kept_shape = pltpu.VMEM((2, pairs // 3, 2 * panels, panels), bf16)
        kept_second, across, upper = call(
            functools.partial(second_kernel, blocks, panels, group_blocks),
            (
                kept_shape,
                shape(width, 2 * group_blocks * panels, kind=bf16),
                coded(2 * group_blocks),
            ),
            (own, total, *gathered),
            [in_hbm] + [in_vmem] * (1 + clusters),
            flops=1 << 33,
        )
        kept_first, lower = call(
            functools.partial(first_kernel, group_blocks),
            (kept_shape, coded(group_blocks)),
            (first, total, across),
            [in_hbm] + [in_vmem] * 2,
            flops=1 << 33,
        )
        kept_first, kept_second = (pltpu.with_memory_space_constraint(x, pltpu.VMEM) for x in (kept_first, kept_second))
        potential, middle = call(
            functools.partial(inner_kernel, blocks),
            (block_sums, block_sums),
            (total, across, kept_first, first, *gathered),
            scratch=[kept_shape],
        )
        upper, lower = exchange_beside(upper, 1), exchange_beside(lower, 0)
        parts_body, parts_args = parts_kernel, (kept_second, potential, middle, lower, upper)
    else:
        own = group_strengths(mine)
        first, second = exchange_beside(own, 0), exchange_beside(own, 1)
        potential, adjoint = call(
            functools.partial(slots_kernel, blocks, panels, chunk),
            (block_sums, shape(sources, width, panels)),
            (*slot_args, pltpu.with_memory_space_constraint(kernels, pltpu.HBM), first, second, *gathered),
            [in_smem] * 3 + [in_hbm] + [in_vmem] * (2 + clusters),
            [
                pltpu.VMEM(kernels.shape, bf16),
                pltpu.VMEM((sources, 2 * panels, width), bf16),
                pltpu.VMEM((group_blocks, width, 2 * panels), bf16),
                pltpu.SemaphoreType.DMA((slots // chunk,)),
            ],
            mib=40,
        )
        lower, upper = call(code_kernel, (coded(group_blocks),) * 2, (adjoint,))
        upper, lower = exchange_beside(upper, 1), exchange_beside(lower, 0)
        parts_body, parts_args = slots_parts_kernel, (potential, adjoint, lower, upper)
    mine, *parts = call(
        functools.partial(parts_body, blocks),
        (shape(2 * blocks * panels, width),) + (coded(2 * blocks),) * (clusters - 1),
        parts_args,
    )
    order = sorted(range(1, clusters), key=lambda k: (k == 1, k & 1))
    *early, last = [exchange(parts[k - 1], "clu", k) for k in order]
    early = call(functools.partial(add_kernel, blocks, panels), shape(2 * blocks * panels, width), (mine, *early))
    out = shape(blocks * panels, width)
    return tuple(call(functools.partial(finish_kernel, blocks, panels), (out, out), (early, last)))


def solution(mesh):
    return jax.shard_map(
        local,
        mesh=mesh,
        in_specs=(
            P(("grp", "clu"), None),
            P(("grp", "clu"), None),
            P(("grp", "clu"), None, None, None),
            P(("grp", "clu")),
            P(("grp", "clu")),
            P(("grp", "clu")),
        ),
        out_specs=(P(("grp", "clu"), None), P(("grp", "clu"), None)),
        check_vma=False,
    )
```

```python
import functools

import jax
import jax.numpy as jnp
from jax import lax
from jax.experimental import pallas as pl
from jax.experimental.pallas import tpu as pltpu
from jax.sharding import PartitionSpec as P

EXPONENT_ROWS = 16
TINY = 2.0**-110


def exchange(value, axis, step):
    return lax.ppermute(value, axis, [(i, i ^ step) for i in range(lax.axis_size(axis))])


def exchange_beside(value, first):
    groups = lax.axis_size("grp")
    partner = [i + 1 if (i - first) % 2 == 0 else i - 1 for i in range(groups)]
    return lax.ppermute(value, "grp", [(i, j if 0 <= j < groups else i) for i, j in enumerate(partner)])


def rows_of(index, panels):
    return pl.ds(index * panels, panels)


def encode(values, out_ref):
    exponents = []
    for i, value in enumerate(values):
        largest = jnp.max(jnp.abs(value), axis=0, keepdims=True)
        exponent = jnp.floor(jnp.log2(jnp.maximum(largest, TINY))) + 1.0
        scaled = jnp.round(value * jnp.exp2(15.0 - exponent))
        scaled = jnp.minimum(jnp.maximum(scaled, -32767.0), 32767.0)
        out_ref[rows_of(i, value.shape[0])] = scaled.astype(jnp.int32).astype(jnp.int16)
        exponents.append(exponent)
    last = out_ref.shape[0] - EXPONENT_ROWS * pl.cdiv(len(values), EXPONENT_ROWS)
    exponents += [jnp.zeros_like(exponents[0])] * (out_ref.shape[0] - last - len(exponents))
    table = jnp.concatenate(exponents, axis=0)
    out_ref[last:] = table.astype(jnp.int32).astype(jnp.int16)


def decode(ref, count, panels):
    table = ref[count * panels :].astype(jnp.int32).astype(jnp.float32)
    for i in range(count):
        value = ref[rows_of(i, panels)].astype(jnp.int32).astype(jnp.float32)
        yield value * jnp.exp2(table[i : i + 1] - 15.0)


def turned(block):
    half = block.shape[1] // 2
    wide = pltpu.roll(block.astype(jnp.float32), half, axis=1)
    lane = lax.broadcasted_iota(jnp.int32, wide.shape, 1)
    return jnp.where(lane < half, -wide, wide).astype(block.dtype)


def turned_rows(block):
    half = block.shape[0] // 2
    return jnp.concatenate([-block[half:], block[:half]], axis=0)


def place(target_ref, source_ref, slot, group_blocks, blocks):
    group, mine = lax.axis_index("grp"), lax.axis_index("clu") * blocks
    target = (target_ref[slot] - group * group_blocks) ^ mine
    source = (source_ref[slot] - (group - 1) * group_blocks) ^ mine
    offset = lax.div(source, group_blocks) - 1
    return target, jnp.where(group % 2 == 0, source - 2 * offset * group_blocks, source)


def each_slot(chunk, live_ref, slots, work, wait=None):
    live = live_ref[0]

    @pl.loop(0, slots // chunk if wait else pl.cdiv(live, chunk))
    def _(c):
        if wait:
            wait(c)
        first = c * chunk

        @pl.when(first + chunk <= live)
        def _():
            for i in range(chunk):
                work(first + i)

        @pl.when(first + chunk > live)
        def _():
            @pl.loop(first, jnp.maximum(live, first))
            def _(slot):
                work(slot)


def combine_kernel(group_blocks, blocks, chunk, live_ref, target_ref, source_ref, kernels_ref, _, total):
    def add(slot):
        target, source = place(target_ref, source_ref, slot, group_blocks, blocks)
        pair = source * group_blocks + target
        total[pair] += kernels_ref[slot].reshape(total.shape[1:]).astype(jnp.float32)

    each_slot(chunk, live_ref, kernels_ref.shape[0], add)


def split(total, first, out_ref):
    @pl.loop(0, out_ref.shape[1])
    def _(pair):
        value = total[first + pair]
        high = value.astype(jnp.bfloat16)
        out_ref[0, pair] = high
        out_ref[1, pair] = (value - high.astype(jnp.float32)).astype(jnp.bfloat16)


def pack_kernel(strengths_ref, weights_ref, target_ref, source_ref, out_ref, *rest):
    *kept, sems = rest
    ids, zeros = kept[:2], kept[2:]
    rows = strengths_ref.shape[0]
    moves = [(ref, out_ref.at[pl.ds(i * rows, rows)]) for i, ref in enumerate((strengths_ref, weights_ref))]
    moves += zip((target_ref, source_ref), ids)
    copies = [pltpu.make_async_copy(ref, to, sems.at[i]) for i, (ref, to) in enumerate(moves)]
    for copy in copies:
        copy.start()
    for ref in zeros:

        @pl.loop(0, ref.shape[0])
        def _(i):
            ref[i] = jnp.zeros(ref.shape[1:], ref.dtype)

    for copy in copies:
        copy.wait()


def group_kernel(blocks, panels, _, *refs):
    *gathered, out_ref = refs
    for i, block in enumerate(part_of(gathered, blocks, panels, 0)):
        out_ref[i * panels : (i + 1) * panels] = block


def part_of(gathered, blocks, panels, part):
    for ref in gathered:
        for b in range(blocks):
            yield ref[pl.ds((part * blocks + b) * panels, panels), :]


def strengths_of(first_ref, gathered, second_ref, blocks, panels):
    for i in range(first_ref.shape[0] // panels):
        yield first_ref[rows_of(i, panels)]
    yield from part_of(gathered, blocks, panels, 0)
    for i in range(second_ref.shape[0] // panels):
        yield second_ref[rows_of(i, panels)]


def crossed(block):
    block = block.astype(jnp.float32).T
    return jnp.concatenate([block, turned_rows(block)], axis=1).astype(jnp.bfloat16)


def stacked(block):
    return jnp.concatenate([block, turned(block)], axis=0)


def adjoint_of(pairs_ref, across_ref, first, count):
    width = pairs_ref.shape[3]
    weights = across_ref[...]
    targets = weights.shape[1] // pairs_ref.shape[2]
    both = jnp.concatenate([weights, weights], axis=1)
    step = 2 if count % 2 == 0 else 1
    for i in range(0, count, step):
        columns = []
        for j in range(first + i, first + i + step):
            tiles = [pairs_ref[h, j * targets + t] for h in range(2) for t in range(targets)]
            columns.append(jnp.concatenate(tiles, axis=0))
        product = jnp.dot(both, jnp.concatenate(columns, axis=1), preferred_element_type=jnp.float32)
        for j in range(step):
            yield product[:, j * width : (j + 1) * width]


def second_kernel(blocks, panels, count, total, *refs):
    *gathered, pairs_ref, across_ref, out_ref = refs
    split(total, total.shape[0] - pairs_ref.shape[1], pairs_ref)
    for i, block in enumerate(part_of(gathered, blocks, panels, 1)):
        across_ref[:, 2 * i * panels : 2 * (i + 1) * panels] = crossed(block)
    strengths = [block.astype(jnp.float32) for block in part_of(gathered, blocks, panels, 0)]
    encode(strengths + list(adjoint_of(pairs_ref, across_ref, 0, count)), out_ref)


def first_kernel(count, total, across_ref, pairs_ref, out_ref):
    split(total, 0, pairs_ref)
    encode(list(adjoint_of(pairs_ref, across_ref, 0, count)), out_ref)


def forward_of(pairs_ref, strengths, targets):
    panels = pairs_ref.shape[2] // 2
    stack = jnp.concatenate([stacked(x) for x in strengths], axis=0)
    for t in range(targets):
        halves = []
        for h in range(2):
            tiles = []
            for pair in range(t, pairs_ref.shape[1], targets):
                tiles += [pairs_ref[h, pair, :panels], pairs_ref[h, pair, panels:]]
            halves.append(jnp.concatenate(tiles, axis=1))
        product = jnp.dot(jnp.concatenate(halves, axis=0), stack, preferred_element_type=jnp.float32)
        yield product[:panels] + product[panels:]


def own_kernel(blocks, total, across_ref, *refs):
    *gathered, potential_ref, middle_ref, pairs_ref = refs
    targets, panels = potential_ref.shape[:2]
    split(total, pairs_ref.shape[1], pairs_ref)
    for i, value in enumerate(adjoint_of(pairs_ref, across_ref, 0, targets)):
        middle_ref[i] = value
    strengths = list(part_of(gathered, blocks, panels, 0))
    for t, value in enumerate(forward_of(pairs_ref, strengths, targets)):
        potential_ref[t] = value


def forward_kernel(pairs_ref, first_ref, own_ref, potential_ref):
    targets, panels = potential_ref.shape[:2]
    strengths = [first_ref[rows_of(i, panels)] for i in range(targets)]
    for t, value in enumerate(forward_of(pairs_ref, strengths, targets)):
        potential_ref[t] = own_ref[t] + value


def parts_of(blocks, potential, adjoint, own_ref, *outs):
    panels = potential[0].shape[0]
    for i in range(blocks):
        own_ref[rows_of(i, panels)] = potential[i]
        own_ref[rows_of(blocks + i, panels)] = adjoint[i]
    for k, out_ref in enumerate(outs, 1):
        rows = slice(k * blocks, (k + 1) * blocks)
        encode(potential[rows] + adjoint[rows], out_ref)


def parts_kernel(blocks, pairs_ref, potential_ref, middle_ref, first_ref, second_ref, *outs):
    count, panels = potential_ref.shape[:2]
    received = list(decode(second_ref, 2 * count, panels))
    strengths = [block.astype(jnp.bfloat16) for block in received[:count]]
    forward = forward_of(pairs_ref, strengths, count)
    potential = [potential_ref[i] + value for i, value in enumerate(forward)]
    others = zip(decode(first_ref, count, panels), received[count:])
    adjoint = [middle_ref[i] + first + second for i, (first, second) in enumerate(others)]
    parts_of(blocks, potential, adjoint, *outs)


def slots_parts_kernel(blocks, potential_ref, adjoint_ref, first_ref, second_ref, *outs):
    count, panels = potential_ref.shape[:2]
    others = zip(decode(first_ref, count, panels), decode(second_ref, count, panels))
    adjoint = [adjoint_ref[count + i] + first + second for i, (first, second) in enumerate(others)]
    parts_of(blocks, [potential_ref[i] for i in range(count)], adjoint, *outs)


def slots_kernel(blocks, panels, chunk, *refs):
    (live_ref, *ids, kernels_ref), (first_ref, second_ref, *gathered) = refs[:4], refs[4:-6]
    potential_ref, adjoint_ref, held, stack, across, sems = refs[-6:]
    group_blocks = potential_ref.shape[0]

    def fetch(c):
        rows = pl.ds(c * chunk, chunk)
        return pltpu.make_async_copy(kernels_ref.at[rows], held.at[rows], sems.at[c])

    def prepare():
        for c in range(held.shape[0] // chunk):
            fetch(c).start()
        potential_ref[...] = jnp.zeros(potential_ref.shape, potential_ref.dtype)
        adjoint_ref[...] = jnp.zeros(adjoint_ref.shape, adjoint_ref.dtype)
        for i, block in enumerate(strengths_of(first_ref, gathered, second_ref, blocks, panels)):
            stack[i] = stacked(block)
        for i, block in enumerate(part_of(gathered, blocks, panels, 1)):
            across[i] = crossed(block)

    def work(slot):
        target, source = place(*ids, slot, group_blocks, blocks)
        real, imag = held[slot, 0], held[slot, 1]
        potential_ref[target] += jnp.dot(
            jnp.concatenate([real, imag], axis=1), stack[source], preferred_element_type=jnp.float32
        )
        adjoint_ref[source] += jnp.dot(
            across[target], jnp.concatenate([real, imag], axis=0), preferred_element_type=jnp.float32
        )

    prepare()
    each_slot(chunk, live_ref, held.shape[0], work, lambda c: fetch(c).wait())


def code_kernel(adjoint_ref, *outs):
    count = adjoint_ref.shape[0] // 3
    for first, out_ref in zip((0, 2 * count), outs):
        encode([adjoint_ref[first + i] for i in range(count)], out_ref)


def finish_kernel(blocks, panels, own_ref, *refs):
    *parts, potential_ref, adjoint_ref = refs
    total = [own_ref[rows_of(i, panels)] for i in range(2 * blocks)]
    for ref in parts:
        total = [a + b for a, b in zip(total, decode(ref, 2 * blocks, panels))]
    for b in range(blocks):
        potential_ref[rows_of(b, panels)] = total[b]
        adjoint_ref[rows_of(b, panels)] = total[blocks + b].T


def local(strengths, adjoint_weights, kernels, target_ids, source_ids, live_slots):
    slots, _, panels, _ = kernels.shape
    width = strengths.shape[1]
    blocks = strengths.shape[0] // panels
    clusters = lax.axis_size("clu")
    group_blocks = clusters * blocks
    sources = 3 * group_blocks
    pairs = group_blocks * sources
    chunk = 8 if slots % 8 == 0 else 1
    in_vmem, in_smem, in_hbm = (pl.BlockSpec(memory_space=m) for m in (pltpu.VMEM, pltpu.SMEM, pltpu.HBM))
    f32, bf16 = jnp.float32, jnp.bfloat16

    def call(body, shapes, args, specs=None, scratch=(), mib=8, flops=0, aliases=(), out_specs=None):
        single = not isinstance(shapes, tuple)
        return pl.pallas_call(
            body,
            out_shape=shapes,
            input_output_aliases=dict(aliases),
            in_specs=specs or [in_vmem] * len(args),
            out_specs=out_specs or (in_vmem if single else (in_vmem,) * len(shapes)),
            scratch_shapes=scratch,
            compiler_params=pltpu.CompilerParams(vmem_limit_bytes=mib << 20),
            cost_estimate=pl.CostEstimate(flops=flops, bytes_accessed=1 << 20, transcendentals=0),
        )(*args)

    def shape(*dims, kind=f32):
        return jax.ShapeDtypeStruct(dims, kind)

    zeros = [pltpu.VMEM((pairs, 2 * panels, panels), f32)] if pairs <= slots else []
    kept_ids = [pltpu.SMEM(x.shape, x.dtype) for x in (target_ids, source_ids)]
    mine, *ids = call(
        pack_kernel,
        (shape(2 * blocks * panels, width, kind=bf16), *kept_ids, *zeros),
        [pltpu.with_memory_space_constraint(x, pltpu.HBM) for x in (strengths, adjoint_weights, target_ids, source_ids)],
        [in_hbm] * 4,
        [pltpu.SemaphoreType.DMA((4,))],
        out_specs=(in_vmem, in_smem, in_smem) + (in_vmem,) * len(zeros),
        flops=1 << 34,
    )
    ids, zeros = ids[:2], ids[2:]
    slot_args = (live_slots, *(pltpu.with_memory_space_constraint(x, pltpu.SMEM) for x in ids))
    gathered = [exchange(mine, "clu", k) for k in range(clusters - 1, 0, -1)]
    gathered = [mine] + gathered[::-1]

    def group_strengths(token):
        return call(
            functools.partial(group_kernel, blocks, panels),
            shape(group_blocks * panels, width, kind=bf16),
            (token, *gathered),
            [in_hbm] + [in_vmem] * clusters,
        )

    def coded(count):
        return shape(count * panels + EXPONENT_ROWS * pl.cdiv(count, EXPONENT_ROWS), width, kind=jnp.int16)

    block_sums = shape(group_blocks, panels, width)
    if pairs <= slots:
        total = call(
            functools.partial(combine_kernel, group_blocks, blocks, chunk),
            pltpu.VMEM((pairs, 2 * panels, panels), f32),
            (*slot_args, *(pltpu.with_memory_space_constraint(x, pltpu.VMEM) for x in (kernels, *zeros))),
            [in_smem] * 3 + [in_vmem] * 2,
            flops=1 << 33,
            aliases=[(4, 0)],
        )
        total = pltpu.with_memory_space_constraint(total, pltpu.VMEM)
        kept_shape = pltpu.VMEM((2, pairs // 3, 2 * panels, panels), bf16)
        kept_second, across, upper = call(
            functools.partial(second_kernel, blocks, panels, group_blocks),
            (
                kept_shape,
                shape(width, 2 * group_blocks * panels, kind=bf16),
                coded(2 * group_blocks),
            ),
            (total, *gathered),
            flops=1 << 33,
        )
        kept_first, lower = call(
            functools.partial(first_kernel, group_blocks),
            (kept_shape, coded(group_blocks)),
            (total, across),
            flops=1 << 33,
        )
        first = exchange_beside(group_strengths(lower), 0)
        kept_first, kept_second = (pltpu.with_memory_space_constraint(x, pltpu.VMEM) for x in (kept_first, kept_second))
        own, middle = call(
            functools.partial(own_kernel, blocks),
            (block_sums, block_sums),
            (total, across, *gathered),
            scratch=[kept_shape],
        )
        potential = call(forward_kernel, block_sums, (kept_first, first, own))
        upper, lower = exchange_beside(upper, 1), exchange_beside(lower, 0)
        parts_body, parts_args = parts_kernel, (kept_second, potential, middle, lower, upper)
    else:
        own = group_strengths(mine)
        first, second = exchange_beside(own, 0), exchange_beside(own, 1)
        potential, adjoint = call(
            functools.partial(slots_kernel, blocks, panels, chunk),
            (block_sums, shape(sources, width, panels)),
            (*slot_args, pltpu.with_memory_space_constraint(kernels, pltpu.HBM), first, second, *gathered),
            [in_smem] * 3 + [in_hbm] + [in_vmem] * (2 + clusters),
            [
                pltpu.VMEM(kernels.shape, bf16),
                pltpu.VMEM((sources, 2 * panels, width), bf16),
                pltpu.VMEM((group_blocks, width, 2 * panels), bf16),
                pltpu.SemaphoreType.DMA((slots // chunk,)),
            ],
            mib=40,
        )
        lower, upper = call(code_kernel, (coded(group_blocks),) * 2, (adjoint,))
        upper, lower = exchange_beside(upper, 1), exchange_beside(lower, 0)
        parts_body, parts_args = slots_parts_kernel, (potential, adjoint, lower, upper)
    mine, *parts = call(
        functools.partial(parts_body, blocks),
        (shape(2 * blocks * panels, width),) + (coded(2 * blocks),) * (clusters - 1),
        parts_args,
    )
    parts = [exchange(parts[k - 1], "clu", k) for k in range(clusters - 1, 0, -1)]
    out = shape(blocks * panels, width)
    return tuple(call(functools.partial(finish_kernel, blocks, panels), (out, out), (mine, *parts)))


def solution(mesh):
    return jax.shard_map(
        local,
        mesh=mesh,
        in_specs=(
            P(("grp", "clu"), None),
            P(("grp", "clu"), None),
            P(("grp", "clu"), None, None, None),
            P(("grp", "clu")),
            P(("grp", "clu")),
            P(("grp", "clu")),
        ),
        out_specs=(P(("grp", "clu"), None), P(("grp", "clu"), None)),
        check_vma=False,
    )
```

```python
import functools

import jax
import jax.numpy as jnp
from jax import lax
from jax.experimental import pallas as pl
from jax.experimental.pallas import tpu as pltpu
from jax.sharding import PartitionSpec as P

EXPONENT_ROWS = 16
TINY = 2.0**-110


def exchange(value, axis, step):
    return lax.ppermute(value, axis, [(i, i ^ step) for i in range(lax.axis_size(axis))])


def exchange_beside(value, first):
    groups = lax.axis_size("grp")
    partner = [i + 1 if (i - first) % 2 == 0 else i - 1 for i in range(groups)]
    return lax.ppermute(value, "grp", [(i, j if 0 <= j < groups else i) for i, j in enumerate(partner)])


def rows_of(index, panels):
    return pl.ds(index * panels, panels)


def encode(values, out_ref):
    exponents = []
    for i, value in enumerate(values):
        largest = jnp.max(jnp.abs(value), axis=0, keepdims=True)
        exponent = jnp.floor(jnp.log2(jnp.maximum(largest, TINY))) + 1.0
        scaled = jnp.round(value * jnp.exp2(15.0 - exponent))
        scaled = jnp.minimum(jnp.maximum(scaled, -32767.0), 32767.0)
        out_ref[rows_of(i, value.shape[0])] = scaled.astype(jnp.int32).astype(jnp.int16)
        exponents.append(exponent)
    last = out_ref.shape[0] - EXPONENT_ROWS * pl.cdiv(len(values), EXPONENT_ROWS)
    exponents += [jnp.zeros_like(exponents[0])] * (out_ref.shape[0] - last - len(exponents))
    table = jnp.concatenate(exponents, axis=0)
    out_ref[last:] = table.astype(jnp.int32).astype(jnp.int16)


def decode(ref, count, panels):
    table = ref[count * panels :].astype(jnp.int32).astype(jnp.float32)
    for i in range(count):
        value = ref[rows_of(i, panels)].astype(jnp.int32).astype(jnp.float32)
        yield value * jnp.exp2(table[i : i + 1] - 15.0)


def turned(block):
    half = block.shape[1] // 2
    wide = pltpu.roll(block.astype(jnp.float32), half, axis=1)
    lane = lax.broadcasted_iota(jnp.int32, wide.shape, 1)
    return jnp.where(lane < half, -wide, wide).astype(block.dtype)


def turned_rows(block):
    half = block.shape[0] // 2
    return jnp.concatenate([-block[half:], block[:half]], axis=0)


def place(target_ref, source_ref, slot, group_blocks, blocks):
    group, mine = lax.axis_index("grp"), lax.axis_index("clu") * blocks
    target = (target_ref[slot] - group * group_blocks) ^ mine
    source = (source_ref[slot] - (group - 1) * group_blocks) ^ mine
    offset = lax.div(source, group_blocks) - 1
    return target, jnp.where(group % 2 == 0, source - 2 * offset * group_blocks, source)


def each_slot(chunk, live_ref, slots, work, wait=None):
    live = live_ref[0]

    @pl.loop(0, slots // chunk if wait else pl.cdiv(live, chunk))
    def _(c):
        if wait:
            wait(c)
        first = c * chunk

        @pl.when(first + chunk <= live)
        def _():
            for i in range(chunk):
                work(first + i)

        @pl.when(first + chunk > live)
        def _():
            @pl.loop(first, jnp.maximum(live, first))
            def _(slot):
                work(slot)


def combine_kernel(group_blocks, blocks, chunk, live_ref, target_ref, source_ref, kernels_ref, _, total):
    def add(slot):
        target, source = place(target_ref, source_ref, slot, group_blocks, blocks)
        pair = source * group_blocks + target
        total[pair] += kernels_ref[slot].reshape(total.shape[1:]).astype(jnp.float32)

    each_slot(chunk, live_ref, kernels_ref.shape[0], add)


def split(total, first, out_ref):
    @pl.loop(0, out_ref.shape[1])
    def _(pair):
        value = total[first + pair]
        high = value.astype(jnp.bfloat16)
        out_ref[0, pair] = high
        out_ref[1, pair] = (value - high.astype(jnp.float32)).astype(jnp.bfloat16)


def pack_kernel(strengths_ref, weights_ref, target_ref, source_ref, out_ref, *rest):
    *kept, sems = rest
    ids, zeros = kept[:2], kept[2:]
    rows = strengths_ref.shape[0]
    moves = [(ref, out_ref.at[pl.ds(i * rows, rows)]) for i, ref in enumerate((strengths_ref, weights_ref))]
    moves += zip((target_ref, source_ref), ids)
    copies = [pltpu.make_async_copy(ref, to, sems.at[i]) for i, (ref, to) in enumerate(moves)]
    for copy in copies:
        copy.start()
    for ref in zeros:

        @pl.loop(0, ref.shape[0])
        def _(i):
            ref[i] = jnp.zeros(ref.shape[1:], ref.dtype)

    for copy in copies:
        copy.wait()


def group_kernel(blocks, panels, _, *refs):
    *gathered, out_ref = refs
    for i, block in enumerate(part_of(gathered, blocks, panels, 0)):
        out_ref[i * panels : (i + 1) * panels] = block


def part_of(gathered, blocks, panels, part):
    for ref in gathered:
        for b in range(blocks):
            yield ref[pl.ds((part * blocks + b) * panels, panels), :]


def strengths_of(first_ref, gathered, second_ref, blocks, panels):
    for i in range(first_ref.shape[0] // panels):
        yield first_ref[rows_of(i, panels)]
    yield from part_of(gathered, blocks, panels, 0)
    for i in range(second_ref.shape[0] // panels):
        yield second_ref[rows_of(i, panels)]


def crossed(block):
    block = block.astype(jnp.float32).T
    return jnp.concatenate([block, turned_rows(block)], axis=1).astype(jnp.bfloat16)


def stacked(block):
    return jnp.concatenate([block, turned(block)], axis=0)


def adjoint_of(pairs_ref, across_ref, first, count):
    width = pairs_ref.shape[3]
    weights = across_ref[...]
    targets = weights.shape[1] // pairs_ref.shape[2]
    both = jnp.concatenate([weights, weights], axis=1)
    step = 2 if count % 2 == 0 else 1
    for i in range(0, count, step):
        columns = []
        for j in range(first + i, first + i + step):
            tiles = [pairs_ref[h, j * targets + t] for h in range(2) for t in range(targets)]
            columns.append(jnp.concatenate(tiles, axis=0))
        product = jnp.dot(both, jnp.concatenate(columns, axis=1), preferred_element_type=jnp.float32)
        for j in range(step):
            yield product[:, j * width : (j + 1) * width]


def second_kernel(blocks, panels, count, _, total, *refs):
    *gathered, pairs_ref, across_ref, out_ref = refs
    split(total, total.shape[0] - pairs_ref.shape[1], pairs_ref)
    for i, block in enumerate(part_of(gathered, blocks, panels, 1)):
        across_ref[:, 2 * i * panels : 2 * (i + 1) * panels] = crossed(block)
    strengths = [block.astype(jnp.float32) for block in part_of(gathered, blocks, panels, 0)]
    encode(strengths + list(adjoint_of(pairs_ref, across_ref, 0, count)), out_ref)


def first_kernel(count, _, total, across_ref, pairs_ref, out_ref):
    split(total, 0, pairs_ref)
    encode(list(adjoint_of(pairs_ref, across_ref, 0, count)), out_ref)


def forward_of(pairs_ref, strengths, targets):
    panels = pairs_ref.shape[2] // 2
    stack = jnp.concatenate([stacked(x) for x in strengths], axis=0)
    for t in range(targets):
        halves = []
        for h in range(2):
            tiles = []
            for pair in range(t, pairs_ref.shape[1], targets):
                tiles += [pairs_ref[h, pair, :panels], pairs_ref[h, pair, panels:]]
            halves.append(jnp.concatenate(tiles, axis=1))
        product = jnp.dot(jnp.concatenate(halves, axis=0), stack, preferred_element_type=jnp.float32)
        yield product[:panels] + product[panels:]


def inner_kernel(blocks, total, across_ref, first_pairs_ref, first_ref, *refs):
    *gathered, potential_ref, middle_ref, pairs_ref = refs
    targets, panels = potential_ref.shape[:2]
    split(total, pairs_ref.shape[1], pairs_ref)
    for i, value in enumerate(adjoint_of(pairs_ref, across_ref, 0, targets)):
        middle_ref[i] = value
    strengths = [first_ref[rows_of(i, panels)] for i in range(targets)]
    own = list(part_of(gathered, blocks, panels, 0))
    for t, value in enumerate(forward_of(first_pairs_ref, strengths, targets)):
        potential_ref[t] = value
    for t, value in enumerate(forward_of(pairs_ref, own, targets)):
        potential_ref[t] += value


def parts_of(blocks, potential, adjoint, own_ref, *outs):
    panels = potential[0].shape[0]
    for i in range(blocks):
        own_ref[rows_of(i, panels)] = potential[i]
        own_ref[rows_of(blocks + i, panels)] = adjoint[i]
    for k, out_ref in enumerate(outs, 1):
        rows = slice(k * blocks, (k + 1) * blocks)
        encode(potential[rows] + adjoint[rows], out_ref)


def parts_kernel(blocks, pairs_ref, potential_ref, middle_ref, first_ref, second_ref, *outs):
    count, panels = potential_ref.shape[:2]
    received = list(decode(second_ref, 2 * count, panels))
    strengths = [block.astype(jnp.bfloat16) for block in received[:count]]
    forward = forward_of(pairs_ref, strengths, count)
    potential = [potential_ref[i] + value for i, value in enumerate(forward)]
    others = zip(decode(first_ref, count, panels), received[count:])
    adjoint = [middle_ref[i] + first + second for i, (first, second) in enumerate(others)]
    parts_of(blocks, potential, adjoint, *outs)


def slots_parts_kernel(blocks, potential_ref, adjoint_ref, first_ref, second_ref, *outs):
    count, panels = potential_ref.shape[:2]
    others = zip(decode(first_ref, count, panels), decode(second_ref, count, panels))
    adjoint = [adjoint_ref[count + i] + first + second for i, (first, second) in enumerate(others)]
    parts_of(blocks, [potential_ref[i] for i in range(count)], adjoint, *outs)


def slots_kernel(blocks, panels, chunk, *refs):
    (live_ref, *ids, kernels_ref), (first_ref, second_ref, *gathered) = refs[:4], refs[4:-6]
    potential_ref, adjoint_ref, held, stack, across, sems = refs[-6:]
    group_blocks = potential_ref.shape[0]

    def fetch(c):
        rows = pl.ds(c * chunk, chunk)
        return pltpu.make_async_copy(kernels_ref.at[rows], held.at[rows], sems.at[c])

    def prepare():
        for c in range(held.shape[0] // chunk):
            fetch(c).start()
        potential_ref[...] = jnp.zeros(potential_ref.shape, potential_ref.dtype)
        adjoint_ref[...] = jnp.zeros(adjoint_ref.shape, adjoint_ref.dtype)
        for i, block in enumerate(strengths_of(first_ref, gathered, second_ref, blocks, panels)):
            stack[i] = stacked(block)
        for i, block in enumerate(part_of(gathered, blocks, panels, 1)):
            across[i] = crossed(block)

    def work(slot):
        target, source = place(*ids, slot, group_blocks, blocks)
        real, imag = held[slot, 0], held[slot, 1]
        potential_ref[target] += jnp.dot(
            jnp.concatenate([real, imag], axis=1), stack[source], preferred_element_type=jnp.float32
        )
        adjoint_ref[source] += jnp.dot(
            across[target], jnp.concatenate([real, imag], axis=0), preferred_element_type=jnp.float32
        )

    prepare()
    each_slot(chunk, live_ref, held.shape[0], work, lambda c: fetch(c).wait())


def code_kernel(adjoint_ref, *outs):
    count = adjoint_ref.shape[0] // 3
    for first, out_ref in zip((0, 2 * count), outs):
        encode([adjoint_ref[first + i] for i in range(count)], out_ref)


def finish_kernel(blocks, panels, own_ref, *refs):
    *parts, potential_ref, adjoint_ref = refs
    total = [own_ref[rows_of(i, panels)] for i in range(2 * blocks)]
    for ref in parts:
        total = [a + b for a, b in zip(total, decode(ref, 2 * blocks, panels))]
    for b in range(blocks):
        potential_ref[rows_of(b, panels)] = total[b]
        adjoint_ref[rows_of(b, panels)] = total[blocks + b].T


def local(strengths, adjoint_weights, kernels, target_ids, source_ids, live_slots):
    slots, _, panels, _ = kernels.shape
    width = strengths.shape[1]
    blocks = strengths.shape[0] // panels
    clusters = lax.axis_size("clu")
    group_blocks = clusters * blocks
    sources = 3 * group_blocks
    pairs = group_blocks * sources
    chunk = 8 if slots % 8 == 0 else 1
    in_vmem, in_smem, in_hbm = (pl.BlockSpec(memory_space=m) for m in (pltpu.VMEM, pltpu.SMEM, pltpu.HBM))
    f32, bf16 = jnp.float32, jnp.bfloat16

    def call(body, shapes, args, specs=None, scratch=(), mib=8, flops=0, aliases=(), out_specs=None):
        single = not isinstance(shapes, tuple)
        return pl.pallas_call(
            body,
            out_shape=shapes,
            input_output_aliases=dict(aliases),
            in_specs=specs or [in_vmem] * len(args),
            out_specs=out_specs or (in_vmem if single else (in_vmem,) * len(shapes)),
            scratch_shapes=scratch,
            compiler_params=pltpu.CompilerParams(vmem_limit_bytes=mib << 20),
            cost_estimate=pl.CostEstimate(flops=flops, bytes_accessed=1 << 20, transcendentals=0),
        )(*args)

    def shape(*dims, kind=f32):
        return jax.ShapeDtypeStruct(dims, kind)

    zeros = [pltpu.VMEM((pairs, 2 * panels, panels), f32)] if pairs <= slots else []
    kept_ids = [pltpu.SMEM(x.shape, x.dtype) for x in (target_ids, source_ids)]
    mine, *ids = call(
        pack_kernel,
        (shape(2 * blocks * panels, width, kind=bf16), *kept_ids, *zeros),
        [pltpu.with_memory_space_constraint(x, pltpu.HBM) for x in (strengths, adjoint_weights, target_ids, source_ids)],
        [in_hbm] * 4,
        [pltpu.SemaphoreType.DMA((4,))],
        out_specs=(in_vmem, in_smem, in_smem) + (in_vmem,) * len(zeros),
        flops=1 << 34,
    )
    ids, zeros = ids[:2], ids[2:]
    slot_args = (live_slots, *(pltpu.with_memory_space_constraint(x, pltpu.SMEM) for x in ids))
    gathered = [exchange(mine, "clu", k) for k in range(clusters - 1, 0, -1)]
    gathered = [mine] + gathered[::-1]

    def group_strengths(token):
        return call(
            functools.partial(group_kernel, blocks, panels),
            shape(group_blocks * panels, width, kind=bf16),
            (token, *gathered),
            [in_hbm] + [in_vmem] * clusters,
        )

    def coded(count):
        return shape(count * panels + EXPONENT_ROWS * pl.cdiv(count, EXPONENT_ROWS), width, kind=jnp.int16)

    block_sums = shape(group_blocks, panels, width)
    if pairs <= slots:
        total = call(
            functools.partial(combine_kernel, group_blocks, blocks, chunk),
            pltpu.VMEM((pairs, 2 * panels, panels), f32),
            (*slot_args, *(pltpu.with_memory_space_constraint(x, pltpu.VMEM) for x in (kernels, *zeros))),
            [in_smem] * 3 + [in_vmem] * 2,
            flops=1 << 33,
            aliases=[(4, 0)],
        )
        own = group_strengths(total)
        first = exchange_beside(own, 0)
        total = pltpu.with_memory_space_constraint(total, pltpu.VMEM)
        kept_shape = pltpu.VMEM((2, pairs // 3, 2 * panels, panels), bf16)
        kept_second, across, upper = call(
            functools.partial(second_kernel, blocks, panels, group_blocks),
            (
                kept_shape,
                shape(width, 2 * group_blocks * panels, kind=bf16),
                coded(2 * group_blocks),
            ),
            (own, total, *gathered),
            [in_hbm] + [in_vmem] * (1 + clusters),
            flops=1 << 33,
        )
        kept_first, lower = call(
            functools.partial(first_kernel, group_blocks),
            (kept_shape, coded(group_blocks)),
            (first, total, across),
            [in_hbm] + [in_vmem] * 2,
            flops=1 << 33,
        )
        kept_first, kept_second = (pltpu.with_memory_space_constraint(x, pltpu.VMEM) for x in (kept_first, kept_second))
        potential, middle = call(
            functools.partial(inner_kernel, blocks),
            (block_sums, block_sums),
            (total, across, kept_first, first, *gathered),
            scratch=[kept_shape],
        )
        upper, lower = exchange_beside(upper, 1), exchange_beside(lower, 0)
        parts_body, parts_args = parts_kernel, (kept_second, potential, middle, lower, upper)
    else:
        own = group_strengths(mine)
        first, second = exchange_beside(own, 0), exchange_beside(own, 1)
        potential, adjoint = call(
            functools.partial(slots_kernel, blocks, panels, chunk),
            (block_sums, shape(sources, width, panels)),
            (*slot_args, pltpu.with_memory_space_constraint(kernels, pltpu.HBM), first, second, *gathered),
            [in_smem] * 3 + [in_hbm] + [in_vmem] * (2 + clusters),
            [
                pltpu.VMEM(kernels.shape, bf16),
                pltpu.VMEM((sources, 2 * panels, width), bf16),
                pltpu.VMEM((group_blocks, width, 2 * panels), bf16),
                pltpu.SemaphoreType.DMA((slots // chunk,)),
            ],
            mib=40,
        )
        lower, upper = call(code_kernel, (coded(group_blocks),) * 2, (adjoint,))
        upper, lower = exchange_beside(upper, 1), exchange_beside(lower, 0)
        parts_body, parts_args = slots_parts_kernel, (potential, adjoint, lower, upper)
    mine, *parts = call(
        functools.partial(parts_body, blocks),
        (shape(2 * blocks * panels, width),) + (coded(2 * blocks),) * (clusters - 1),
        parts_args,
    )
    order = sorted(range(1, clusters), key=lambda k: -k.bit_count())
    parts = [exchange(parts[k - 1], "clu", k) for k in order]
    out = shape(blocks * panels, width)
    return tuple(call(functools.partial(finish_kernel, blocks, panels), (out, out), (mine, *parts)))


def solution(mesh):
    return jax.shard_map(
        local,
        mesh=mesh,
        in_specs=(
            P(("grp", "clu"), None),
            P(("grp", "clu"), None),
            P(("grp", "clu"), None, None, None),
            P(("grp", "clu")),
            P(("grp", "clu")),
            P(("grp", "clu")),
        ),
        out_specs=(P(("grp", "clu"), None), P(("grp", "clu"), None)),
        check_vma=False,
    )
```

```python
import functools

import jax
import jax.numpy as jnp
from jax import lax
from jax.experimental import pallas as pl
from jax.experimental.pallas import tpu as pltpu
from jax.sharding import PartitionSpec as P

EXPONENT_ROWS = 16
TINY = 2.0**-110


def exchange(value, axis, step):
    return lax.ppermute(value, axis, [(i, i ^ step) for i in range(lax.axis_size(axis))])


def exchange_beside(value, first):
    groups = lax.axis_size("grp")
    partner = [i + 1 if (i - first) % 2 == 0 else i - 1 for i in range(groups)]
    return lax.ppermute(value, "grp", [(i, j if 0 <= j < groups else i) for i, j in enumerate(partner)])


def rows_of(index, panels):
    return pl.ds(index * panels, panels)


def encode(values, out_ref):
    exponents = []
    for i, value in enumerate(values):
        largest = jnp.max(jnp.abs(value), axis=0, keepdims=True)
        exponent = jnp.floor(jnp.log2(jnp.maximum(largest, TINY))) + 1.0
        scaled = jnp.round(value * jnp.exp2(15.0 - exponent))
        scaled = jnp.minimum(jnp.maximum(scaled, -32767.0), 32767.0)
        out_ref[rows_of(i, value.shape[0])] = scaled.astype(jnp.int32).astype(jnp.int16)
        exponents.append(exponent)
    last = out_ref.shape[0] - EXPONENT_ROWS * pl.cdiv(len(values), EXPONENT_ROWS)
    exponents += [jnp.zeros_like(exponents[0])] * (out_ref.shape[0] - last - len(exponents))
    table = jnp.concatenate(exponents, axis=0)
    out_ref[last:] = table.astype(jnp.int32).astype(jnp.int16)


def decode(ref, count, panels):
    table = ref[count * panels :].astype(jnp.int32).astype(jnp.float32)
    for i in range(count):
        value = ref[rows_of(i, panels)].astype(jnp.int32).astype(jnp.float32)
        yield value * jnp.exp2(table[i : i + 1] - 15.0)


def turned(block):
    half = block.shape[1] // 2
    wide = pltpu.roll(block.astype(jnp.float32), half, axis=1)
    lane = lax.broadcasted_iota(jnp.int32, wide.shape, 1)
    return jnp.where(lane < half, -wide, wide).astype(block.dtype)


def turned_rows(block):
    half = block.shape[0] // 2
    return jnp.concatenate([-block[half:], block[:half]], axis=0)


def place(target_ref, source_ref, slot, group_blocks, blocks):
    group, mine = lax.axis_index("grp"), lax.axis_index("clu") * blocks
    target = (target_ref[slot] - group * group_blocks) ^ mine
    source = (source_ref[slot] - (group - 1) * group_blocks) ^ mine
    offset = lax.div(source, group_blocks) - 1
    return target, jnp.where(group % 2 == 0, source - 2 * offset * group_blocks, source)


def each_slot(chunk, live_ref, slots, work, wait=None):
    live = live_ref[0]

    @pl.loop(0, slots // chunk if wait else pl.cdiv(live, chunk))
    def _(c):
        if wait:
            wait(c)
        first = c * chunk

        @pl.when(first + chunk <= live)
        def _():
            for i in range(chunk):
                work(first + i)

        @pl.when(first + chunk > live)
        def _():
            @pl.loop(first, jnp.maximum(live, first))
            def _(slot):
                work(slot)


def combine_kernel(group_blocks, blocks, chunk, live_ref, target_ref, source_ref, kernels_ref, _, total):
    def add(slot):
        target, source = place(target_ref, source_ref, slot, group_blocks, blocks)
        pair = source * group_blocks + target
        total[pair] += kernels_ref[slot].reshape(total.shape[1:]).astype(jnp.float32)

    each_slot(chunk, live_ref, kernels_ref.shape[0], add)


def split(total, first, out_ref):
    @pl.loop(0, out_ref.shape[1])
    def _(pair):
        value = total[first + pair]
        high = value.astype(jnp.bfloat16)
        out_ref[0, pair] = high
        out_ref[1, pair] = (value - high.astype(jnp.float32)).astype(jnp.bfloat16)


def pack_kernel(strengths_ref, weights_ref, target_ref, source_ref, out_ref, *rest):
    *kept, sems = rest
    ids, zeros = kept[:2], kept[2:]
    rows = strengths_ref.shape[0]
    moves = [(ref, out_ref.at[pl.ds(i * rows, rows)]) for i, ref in enumerate((strengths_ref, weights_ref))]
    moves += zip((target_ref, source_ref), ids)
    copies = [pltpu.make_async_copy(ref, to, sems.at[i]) for i, (ref, to) in enumerate(moves)]
    for copy in copies:
        copy.start()
    for ref in zeros:

        @pl.loop(0, ref.shape[0])
        def _(i):
            ref[i] = jnp.zeros(ref.shape[1:], ref.dtype)

    for copy in copies:
        copy.wait()


def group_kernel(blocks, panels, _, *refs):
    *gathered, out_ref = refs
    for i, block in enumerate(part_of(gathered, blocks, panels, 0)):
        out_ref[i * panels : (i + 1) * panels] = block


def part_of(gathered, blocks, panels, part):
    for ref in gathered:
        for b in range(blocks):
            yield ref[pl.ds((part * blocks + b) * panels, panels), :]


def strengths_of(first_ref, gathered, second_ref, blocks, panels):
    for i in range(first_ref.shape[0] // panels):
        yield first_ref[rows_of(i, panels)]
    yield from part_of(gathered, blocks, panels, 0)
    for i in range(second_ref.shape[0] // panels):
        yield second_ref[rows_of(i, panels)]


def crossed(block):
    block = block.astype(jnp.float32).T
    return jnp.concatenate([block, turned_rows(block)], axis=1).astype(jnp.bfloat16)


def stacked(block):
    return jnp.concatenate([block, turned(block)], axis=0)


def adjoint_of(pairs_ref, across_ref, first, count):
    width = pairs_ref.shape[3]
    weights = across_ref[...]
    targets = weights.shape[1] // pairs_ref.shape[2]
    both = jnp.concatenate([weights, weights], axis=1)
    step = 2 if count % 2 == 0 else 1
    for i in range(0, count, step):
        columns = []
        for j in range(first + i, first + i + step):
            tiles = [pairs_ref[h, j * targets + t] for h in range(2) for t in range(targets)]
            columns.append(jnp.concatenate(tiles, axis=0))
        product = jnp.dot(both, jnp.concatenate(columns, axis=1), preferred_element_type=jnp.float32)
        for j in range(step):
            yield product[:, j * width : (j + 1) * width]


def second_kernel(blocks, panels, count, _, total, *refs):
    *gathered, pairs_ref, across_ref, out_ref = refs
    split(total, total.shape[0] - pairs_ref.shape[1], pairs_ref)
    for i, block in enumerate(part_of(gathered, blocks, panels, 1)):
        across_ref[:, 2 * i * panels : 2 * (i + 1) * panels] = crossed(block)
    strengths = [block.astype(jnp.float32) for block in part_of(gathered, blocks, panels, 0)]
    encode(strengths + list(adjoint_of(pairs_ref, across_ref, 0, count)), out_ref)


def first_kernel(count, _, total, across_ref, pairs_ref, out_ref):
    split(total, 0, pairs_ref)
    encode(list(adjoint_of(pairs_ref, across_ref, 0, count)), out_ref)


def forward_of(pairs_ref, strengths, targets):
    panels = pairs_ref.shape[2] // 2
    stack = jnp.concatenate([stacked(x) for x in strengths], axis=0)
    for t in range(targets):
        halves = []
        for h in range(2):
            tiles = []
            for pair in range(t, pairs_ref.shape[1], targets):
                tiles += [pairs_ref[h, pair, :panels], pairs_ref[h, pair, panels:]]
            halves.append(jnp.concatenate(tiles, axis=1))
        product = jnp.dot(jnp.concatenate(halves, axis=0), stack, preferred_element_type=jnp.float32)
        yield product[:panels] + product[panels:]


def inner_kernel(blocks, total, across_ref, first_pairs_ref, first_ref, *refs):
    *gathered, potential_ref, middle_ref, pairs_ref = refs
    targets, panels = potential_ref.shape[:2]
    split(total, pairs_ref.shape[1], pairs_ref)
    for i, value in enumerate(adjoint_of(pairs_ref, across_ref, 0, targets)):
        middle_ref[i] = value
    strengths = [first_ref[rows_of(i, panels)] for i in range(targets)]
    own = list(part_of(gathered, blocks, panels, 0))
    for t, value in enumerate(forward_of(first_pairs_ref, strengths, targets)):
        potential_ref[t] = value
    for t, value in enumerate(forward_of(pairs_ref, own, targets)):
        potential_ref[t] += value


def parts_of(blocks, potential, adjoint, own_ref, *outs):
    panels = potential[0].shape[0]
    for i in range(blocks):
        own_ref[rows_of(i, panels)] = potential[i]
        own_ref[rows_of(blocks + i, panels)] = adjoint[i]
    for k, out_ref in enumerate(outs, 1):
        rows = slice(k * blocks, (k + 1) * blocks)
        encode(potential[rows] + adjoint[rows], out_ref)


def parts_kernel(blocks, pairs_ref, potential_ref, middle_ref, first_ref, second_ref, *outs):
    count, panels = potential_ref.shape[:2]
    received = list(decode(second_ref, 2 * count, panels))
    strengths = [block.astype(jnp.bfloat16) for block in received[:count]]
    forward = forward_of(pairs_ref, strengths, count)
    potential = [potential_ref[i] + value for i, value in enumerate(forward)]
    others = zip(decode(first_ref, count, panels), received[count:])
    adjoint = [middle_ref[i] + first + second for i, (first, second) in enumerate(others)]
    parts_of(blocks, potential, adjoint, *outs)


def slots_parts_kernel(blocks, potential_ref, adjoint_ref, first_ref, second_ref, *outs):
    count, panels = potential_ref.shape[:2]
    others = zip(decode(first_ref, count, panels), decode(second_ref, count, panels))
    adjoint = [adjoint_ref[count + i] + first + second for i, (first, second) in enumerate(others)]
    parts_of(blocks, [potential_ref[i] for i in range(count)], adjoint, *outs)


def slots_kernel(blocks, panels, chunk, *refs):
    (live_ref, *ids, kernels_ref), (first_ref, second_ref, *gathered) = refs[:4], refs[4:-6]
    potential_ref, adjoint_ref, held, stack, across, sems = refs[-6:]
    group_blocks = potential_ref.shape[0]

    def fetch(c):
        rows = pl.ds(c * chunk, chunk)
        return pltpu.make_async_copy(kernels_ref.at[rows], held.at[rows], sems.at[c])

    def prepare():
        for c in range(held.shape[0] // chunk):
            fetch(c).start()
        potential_ref[...] = jnp.zeros(potential_ref.shape, potential_ref.dtype)
        adjoint_ref[...] = jnp.zeros(adjoint_ref.shape, adjoint_ref.dtype)
        for i, block in enumerate(strengths_of(first_ref, gathered, second_ref, blocks, panels)):
            stack[i] = stacked(block)
        for i, block in enumerate(part_of(gathered, blocks, panels, 1)):
            across[i] = crossed(block)

    def work(slot):
        target, source = place(*ids, slot, group_blocks, blocks)
        real, imag = held[slot, 0], held[slot, 1]
        potential_ref[target] += jnp.dot(
            jnp.concatenate([real, imag], axis=1), stack[source], preferred_element_type=jnp.float32
        )
        adjoint_ref[source] += jnp.dot(
            across[target], jnp.concatenate([real, imag], axis=0), preferred_element_type=jnp.float32
        )

    prepare()
    each_slot(chunk, live_ref, held.shape[0], work, lambda c: fetch(c).wait())


def code_kernel(adjoint_ref, *outs):
    count = adjoint_ref.shape[0] // 3
    for first, out_ref in zip((0, 2 * count), outs):
        encode([adjoint_ref[first + i] for i in range(count)], out_ref)


def finish_kernel(blocks, panels, own_ref, *refs):
    *parts, potential_ref, adjoint_ref = refs
    total = [own_ref[rows_of(i, panels)] for i in range(2 * blocks)]
    for ref in parts:
        total = [a + b for a, b in zip(total, decode(ref, 2 * blocks, panels))]
    for b in range(blocks):
        potential_ref[rows_of(b, panels)] = total[b]
        adjoint_ref[rows_of(b, panels)] = total[blocks + b].T


def local(strengths, adjoint_weights, kernels, target_ids, source_ids, live_slots):
    slots, _, panels, _ = kernels.shape
    width = strengths.shape[1]
    blocks = strengths.shape[0] // panels
    clusters = lax.axis_size("clu")
    group_blocks = clusters * blocks
    sources = 3 * group_blocks
    pairs = group_blocks * sources
    chunk = 16 if slots % 16 == 0 else 1
    in_vmem, in_smem, in_hbm = (pl.BlockSpec(memory_space=m) for m in (pltpu.VMEM, pltpu.SMEM, pltpu.HBM))
    f32, bf16 = jnp.float32, jnp.bfloat16

    def call(body, shapes, args, specs=None, scratch=(), mib=8, flops=0, aliases=(), out_specs=None):
        single = not isinstance(shapes, tuple)
        return pl.pallas_call(
            body,
            out_shape=shapes,
            input_output_aliases=dict(aliases),
            in_specs=specs or [in_vmem] * len(args),
            out_specs=out_specs or (in_vmem if single else (in_vmem,) * len(shapes)),
            scratch_shapes=scratch,
            compiler_params=pltpu.CompilerParams(vmem_limit_bytes=mib << 20),
            cost_estimate=pl.CostEstimate(flops=flops, bytes_accessed=1 << 20, transcendentals=0),
        )(*args)

    def shape(*dims, kind=f32):
        return jax.ShapeDtypeStruct(dims, kind)

    zeros = [pltpu.VMEM((pairs, 2 * panels, panels), f32)] if pairs <= slots else []
    kept_ids = [pltpu.SMEM(x.shape, x.dtype) for x in (target_ids, source_ids)]
    mine, *ids = call(
        pack_kernel,
        (shape(2 * blocks * panels, width, kind=bf16), *kept_ids, *zeros),
        [pltpu.with_memory_space_constraint(x, pltpu.HBM) for x in (strengths, adjoint_weights, target_ids, source_ids)],
        [in_hbm] * 4,
        [pltpu.SemaphoreType.DMA((4,))],
        out_specs=(in_vmem, in_smem, in_smem) + (in_vmem,) * len(zeros),
        flops=1 << 34,
    )
    ids, zeros = ids[:2], ids[2:]
    slot_args = (live_slots, *(pltpu.with_memory_space_constraint(x, pltpu.SMEM) for x in ids))
    gathered = [exchange(mine, "clu", k) for k in range(clusters - 1, 0, -1)]
    gathered = [mine] + gathered[::-1]

    def group_strengths(token):
        return call(
            functools.partial(group_kernel, blocks, panels),
            shape(group_blocks * panels, width, kind=bf16),
            (token, *gathered),
            [in_hbm] + [in_vmem] * clusters,
        )

    def coded(count):
        return shape(count * panels + EXPONENT_ROWS * pl.cdiv(count, EXPONENT_ROWS), width, kind=jnp.int16)

    block_sums = shape(group_blocks, panels, width)
    if pairs <= slots:
        total = call(
            functools.partial(combine_kernel, group_blocks, blocks, chunk),
            pltpu.VMEM((pairs, 2 * panels, panels), f32),
            (*slot_args, *(pltpu.with_memory_space_constraint(x, pltpu.VMEM) for x in (kernels, *zeros))),
            [in_smem] * 3 + [in_vmem] * 2,
            flops=1 << 33,
            aliases=[(4, 0)],
        )
        own = group_strengths(total)
        first = exchange_beside(own, 0)
        total = pltpu.with_memory_space_constraint(total, pltpu.VMEM)
        kept_shape = pltpu.VMEM((2, pairs // 3, 2 * panels, panels), bf16)
        kept_second, across, upper = call(
            functools.partial(second_kernel, blocks, panels, group_blocks),
            (
                kept_shape,
                shape(width, 2 * group_blocks * panels, kind=bf16),
                coded(2 * group_blocks),
            ),
            (own, total, *gathered),
            [in_hbm] + [in_vmem] * (1 + clusters),
            flops=1 << 33,
        )
        kept_first, lower = call(
            functools.partial(first_kernel, group_blocks),
            (kept_shape, coded(group_blocks)),
            (first, total, across),
            [in_hbm] + [in_vmem] * 2,
            flops=1 << 33,
        )
        kept_first, kept_second = (pltpu.with_memory_space_constraint(x, pltpu.VMEM) for x in (kept_first, kept_second))
        potential, middle = call(
            functools.partial(inner_kernel, blocks),
            (block_sums, block_sums),
            (total, across, kept_first, first, *gathered),
            scratch=[kept_shape],
        )
        upper, lower = exchange_beside(upper, 1), exchange_beside(lower, 0)
        parts_body, parts_args = parts_kernel, (kept_second, potential, middle, lower, upper)
    else:
        own = group_strengths(mine)
        first, second = exchange_beside(own, 0), exchange_beside(own, 1)
        potential, adjoint = call(
            functools.partial(slots_kernel, blocks, panels, chunk),
            (block_sums, shape(sources, width, panels)),
            (*slot_args, pltpu.with_memory_space_constraint(kernels, pltpu.HBM), first, second, *gathered),
            [in_smem] * 3 + [in_hbm] + [in_vmem] * (2 + clusters),
            [
                pltpu.VMEM(kernels.shape, bf16),
                pltpu.VMEM((sources, 2 * panels, width), bf16),
                pltpu.VMEM((group_blocks, width, 2 * panels), bf16),
                pltpu.SemaphoreType.DMA((slots // chunk,)),
            ],
            mib=40,
        )
        lower, upper = call(code_kernel, (coded(group_blocks),) * 2, (adjoint,))
        upper, lower = exchange_beside(upper, 1), exchange_beside(lower, 0)
        parts_body, parts_args = slots_parts_kernel, (potential, adjoint, lower, upper)
    mine, *parts = call(
        functools.partial(parts_body, blocks),
        (shape(2 * blocks * panels, width),) + (coded(2 * blocks),) * (clusters - 1),
        parts_args,
    )
    parts = [exchange(parts[k - 1], "clu", k) for k in range(clusters - 1, 0, -1)]
    out = shape(blocks * panels, width)
    return tuple(call(functools.partial(finish_kernel, blocks, panels), (out, out), (mine, *parts)))


def solution(mesh):
    return jax.shard_map(
        local,
        mesh=mesh,
        in_specs=(
            P(("grp", "clu"), None),
            P(("grp", "clu"), None),
            P(("grp", "clu"), None, None, None),
            P(("grp", "clu")),
            P(("grp", "clu")),
            P(("grp", "clu")),
        ),
        out_specs=(P(("grp", "clu"), None), P(("grp", "clu"), None)),
        check_vma=False,
    )
```

```python
import functools

import jax
import jax.numpy as jnp
from jax import lax
from jax.experimental import pallas as pl
from jax.experimental.pallas import tpu as pltpu
from jax.sharding import PartitionSpec as P

EXPONENT_ROWS = 16
TINY = 2.0**-110


def exchange(value, axis, step):
    return lax.ppermute(value, axis, [(i, i ^ step) for i in range(lax.axis_size(axis))])


def exchange_beside(value, first):
    groups = lax.axis_size("grp")
    partner = [i + 1 if (i - first) % 2 == 0 else i - 1 for i in range(groups)]
    return lax.ppermute(value, "grp", [(i, j if 0 <= j < groups else i) for i, j in enumerate(partner)])


def rows_of(index, panels):
    return pl.ds(index * panels, panels)


def encode(values, out_ref):
    exponents = []
    for i, value in enumerate(values):
        largest = jnp.max(jnp.abs(value), axis=0, keepdims=True)
        exponent = jnp.floor(jnp.log2(jnp.maximum(largest, TINY))) + 1.0
        scaled = jnp.round(value * jnp.exp2(15.0 - exponent))
        scaled = jnp.minimum(jnp.maximum(scaled, -32767.0), 32767.0)
        out_ref[rows_of(i, value.shape[0])] = scaled.astype(jnp.int32).astype(jnp.int16)
        exponents.append(exponent)
    last = out_ref.shape[0] - EXPONENT_ROWS * pl.cdiv(len(values), EXPONENT_ROWS)
    exponents += [jnp.zeros_like(exponents[0])] * (out_ref.shape[0] - last - len(exponents))
    table = jnp.concatenate(exponents, axis=0)
    out_ref[last:] = table.astype(jnp.int32).astype(jnp.int16)


def decode(ref, count, panels):
    table = ref[count * panels :].astype(jnp.int32).astype(jnp.float32)
    for i in range(count):
        value = ref[rows_of(i, panels)].astype(jnp.int32).astype(jnp.float32)
        yield value * jnp.exp2(table[i : i + 1] - 15.0)


def turned(block):
    half = block.shape[1] // 2
    wide = pltpu.roll(block.astype(jnp.float32), half, axis=1)
    lane = lax.broadcasted_iota(jnp.int32, wide.shape, 1)
    return jnp.where(lane < half, -wide, wide).astype(block.dtype)


def turned_rows(block):
    half = block.shape[0] // 2
    return jnp.concatenate([-block[half:], block[:half]], axis=0)


def place(target_ref, source_ref, slot, group_blocks, blocks):
    group, mine = lax.axis_index("grp"), lax.axis_index("clu") * blocks
    target = (target_ref[slot] - group * group_blocks) ^ mine
    source = (source_ref[slot] - (group - 1) * group_blocks) ^ mine
    offset = lax.div(source, group_blocks) - 1
    return target, jnp.where(group % 2 == 0, source - 2 * offset * group_blocks, source)


def each_slot(chunk, live_ref, slots, work, wait=None):
    live = live_ref[0]

    @pl.loop(0, slots // chunk if wait else pl.cdiv(live, chunk))
    def _(c):
        if wait:
            wait(c)
        first = c * chunk

        @pl.when(first + chunk <= live)
        def _():
            for i in range(chunk):
                work(first + i)

        @pl.when(first + chunk > live)
        def _():
            @pl.loop(first, jnp.maximum(live, first))
            def _(slot):
                work(slot)


def combine_kernel(group_blocks, blocks, chunk, live_ref, target_ref, source_ref, kernels_ref, _, total):
    def add(slot):
        target, source = place(target_ref, source_ref, slot, group_blocks, blocks)
        pair = source * group_blocks + target
        total[pair] += kernels_ref[slot].reshape(total.shape[1:]).astype(jnp.float32)

    each_slot(chunk, live_ref, kernels_ref.shape[0], add)


def split(total, first, out_ref):
    @pl.loop(0, out_ref.shape[1], unroll=4 if out_ref.shape[1] % 4 == 0 else 1)
    def _(pair):
        value = total[first + pair]
        high = value.astype(jnp.bfloat16)
        out_ref[0, pair] = high
        out_ref[1, pair] = (value - high.astype(jnp.float32)).astype(jnp.bfloat16)


def pack_kernel(strengths_ref, weights_ref, target_ref, source_ref, out_ref, *rest):
    *kept, sems = rest
    ids, zeros = kept[:2], kept[2:]
    rows = strengths_ref.shape[0]
    moves = [(ref, out_ref.at[pl.ds(i * rows, rows)]) for i, ref in enumerate((strengths_ref, weights_ref))]
    moves += zip((target_ref, source_ref), ids)
    copies = [pltpu.make_async_copy(ref, to, sems.at[i]) for i, (ref, to) in enumerate(moves)]
    for copy in copies:
        copy.start()
    for ref in zeros:

        @pl.loop(0, ref.shape[0])
        def _(i):
            ref[i] = jnp.zeros(ref.shape[1:], ref.dtype)

    for copy in copies:
        copy.wait()


def group_kernel(blocks, panels, _, *refs):
    *gathered, out_ref = refs
    for i, block in enumerate(part_of(gathered, blocks, panels, 0)):
        out_ref[i * panels : (i + 1) * panels] = block


def part_of(gathered, blocks, panels, part):
    for ref in gathered:
        for b in range(blocks):
            yield ref[pl.ds((part * blocks + b) * panels, panels), :]


def strengths_of(first_ref, gathered, second_ref, blocks, panels):
    for i in range(first_ref.shape[0] // panels):
        yield first_ref[rows_of(i, panels)]
    yield from part_of(gathered, blocks, panels, 0)
    for i in range(second_ref.shape[0] // panels):
        yield second_ref[rows_of(i, panels)]


def crossed(block):
    block = block.astype(jnp.float32).T
    return jnp.concatenate([block, turned_rows(block)], axis=1).astype(jnp.bfloat16)


def stacked(block):
    return jnp.concatenate([block, turned(block)], axis=0)


def adjoint_of(pairs_ref, across_ref, first, count):
    width = pairs_ref.shape[3]
    weights = across_ref[...]
    targets = weights.shape[1] // pairs_ref.shape[2]
    both = jnp.concatenate([weights, weights], axis=1)
    step = 2 if count % 2 == 0 else 1
    for i in range(0, count, step):
        columns = []
        for j in range(first + i, first + i + step):
            tiles = [pairs_ref[h, j * targets + t] for h in range(2) for t in range(targets)]
            columns.append(jnp.concatenate(tiles, axis=0))
        product = jnp.dot(both, jnp.concatenate(columns, axis=1), preferred_element_type=jnp.float32)
        for j in range(step):
            yield product[:, j * width : (j + 1) * width]


def second_kernel(blocks, panels, count, _, total, *refs):
    *gathered, pairs_ref, across_ref, out_ref = refs
    split(total, total.shape[0] - pairs_ref.shape[1], pairs_ref)
    for i, block in enumerate(part_of(gathered, blocks, panels, 1)):
        across_ref[:, 2 * i * panels : 2 * (i + 1) * panels] = crossed(block)
    strengths = [block.astype(jnp.float32) for block in part_of(gathered, blocks, panels, 0)]
    encode(strengths + list(adjoint_of(pairs_ref, across_ref, 0, count)), out_ref)


def first_kernel(count, _, total, across_ref, pairs_ref, out_ref):
    split(total, 0, pairs_ref)
    encode(list(adjoint_of(pairs_ref, across_ref, 0, count)), out_ref)


def forward_of(pairs_ref, strengths, targets):
    panels = pairs_ref.shape[2] // 2
    stack = jnp.concatenate([stacked(x) for x in strengths], axis=0)
    for t in range(targets):
        halves = []
        for h in range(2):
            tiles = []
            for pair in range(t, pairs_ref.shape[1], targets):
                tiles += [pairs_ref[h, pair, :panels], pairs_ref[h, pair, panels:]]
            halves.append(jnp.concatenate(tiles, axis=1))
        product = jnp.dot(jnp.concatenate(halves, axis=0), stack, preferred_element_type=jnp.float32)
        yield product[:panels] + product[panels:]


def inner_kernel(blocks, total, across_ref, first_pairs_ref, first_ref, *refs):
    *gathered, potential_ref, middle_ref, pairs_ref = refs
    targets, panels = potential_ref.shape[:2]
    split(total, pairs_ref.shape[1], pairs_ref)
    for i, value in enumerate(adjoint_of(pairs_ref, across_ref, 0, targets)):
        middle_ref[i] = value
    strengths = [first_ref[rows_of(i, panels)] for i in range(targets)]
    own = list(part_of(gathered, blocks, panels, 0))
    for t, value in enumerate(forward_of(first_pairs_ref, strengths, targets)):
        potential_ref[t] = value
    for t, value in enumerate(forward_of(pairs_ref, own, targets)):
        potential_ref[t] += value


def parts_of(blocks, potential, adjoint, own_ref, *outs):
    panels = potential[0].shape[0]
    for i in range(blocks):
        own_ref[rows_of(i, panels)] = potential[i]
        own_ref[rows_of(blocks + i, panels)] = adjoint[i]
    for k, out_ref in enumerate(outs, 1):
        rows = slice(k * blocks, (k + 1) * blocks)
        encode(potential[rows] + adjoint[rows], out_ref)


def parts_kernel(blocks, pairs_ref, potential_ref, middle_ref, first_ref, second_ref, *outs):
    count, panels = potential_ref.shape[:2]
    received = list(decode(second_ref, 2 * count, panels))
    strengths = [block.astype(jnp.bfloat16) for block in received[:count]]
    forward = forward_of(pairs_ref, strengths, count)
    potential = [potential_ref[i] + value for i, value in enumerate(forward)]
    others = zip(decode(first_ref, count, panels), received[count:])
    adjoint = [middle_ref[i] + first + second for i, (first, second) in enumerate(others)]
    parts_of(blocks, potential, adjoint, *outs)


def slots_parts_kernel(blocks, potential_ref, adjoint_ref, first_ref, second_ref, *outs):
    count, panels = potential_ref.shape[:2]
    others = zip(decode(first_ref, count, panels), decode(second_ref, count, panels))
    adjoint = [adjoint_ref[count + i] + first + second for i, (first, second) in enumerate(others)]
    parts_of(blocks, [potential_ref[i] for i in range(count)], adjoint, *outs)


def slots_kernel(blocks, panels, chunk, *refs):
    (live_ref, *ids, kernels_ref), (first_ref, second_ref, *gathered) = refs[:4], refs[4:-6]
    potential_ref, adjoint_ref, held, stack, across, sems = refs[-6:]
    group_blocks = potential_ref.shape[0]

    def fetch(c):
        rows = pl.ds(c * chunk, chunk)
        return pltpu.make_async_copy(kernels_ref.at[rows], held.at[rows], sems.at[c])

    def prepare():
        for c in range(held.shape[0] // chunk):
            fetch(c).start()
        potential_ref[...] = jnp.zeros(potential_ref.shape, potential_ref.dtype)
        adjoint_ref[...] = jnp.zeros(adjoint_ref.shape, adjoint_ref.dtype)
        for i, block in enumerate(strengths_of(first_ref, gathered, second_ref, blocks, panels)):
            stack[i] = stacked(block)
        for i, block in enumerate(part_of(gathered, blocks, panels, 1)):
            across[i] = crossed(block)

    def work(slot):
        target, source = place(*ids, slot, group_blocks, blocks)
        real, imag = held[slot, 0], held[slot, 1]
        potential_ref[target] += jnp.dot(
            jnp.concatenate([real, imag], axis=1), stack[source], preferred_element_type=jnp.float32
        )
        adjoint_ref[source] += jnp.dot(
            across[target], jnp.concatenate([real, imag], axis=0), preferred_element_type=jnp.float32
        )

    prepare()
    each_slot(chunk, live_ref, held.shape[0], work, lambda c: fetch(c).wait())


def code_kernel(adjoint_ref, *outs):
    count = adjoint_ref.shape[0] // 3
    for first, out_ref in zip((0, 2 * count), outs):
        encode([adjoint_ref[first + i] for i in range(count)], out_ref)


def finish_kernel(blocks, panels, own_ref, *refs):
    *parts, potential_ref, adjoint_ref = refs
    total = [own_ref[rows_of(i, panels)] for i in range(2 * blocks)]
    for ref in parts:
        total = [a + b for a, b in zip(total, decode(ref, 2 * blocks, panels))]
    for b in range(blocks):
        potential_ref[rows_of(b, panels)] = total[b]
        adjoint_ref[rows_of(b, panels)] = total[blocks + b].T


def local(strengths, adjoint_weights, kernels, target_ids, source_ids, live_slots):
    slots, _, panels, _ = kernels.shape
    width = strengths.shape[1]
    blocks = strengths.shape[0] // panels
    clusters = lax.axis_size("clu")
    group_blocks = clusters * blocks
    sources = 3 * group_blocks
    pairs = group_blocks * sources
    chunk = 8 if slots % 8 == 0 else 1
    in_vmem, in_smem, in_hbm = (pl.BlockSpec(memory_space=m) for m in (pltpu.VMEM, pltpu.SMEM, pltpu.HBM))
    f32, bf16 = jnp.float32, jnp.bfloat16

    def call(body, shapes, args, specs=None, scratch=(), mib=8, flops=0, aliases=(), out_specs=None):
        single = not isinstance(shapes, tuple)
        return pl.pallas_call(
            body,
            out_shape=shapes,
            input_output_aliases=dict(aliases),
            in_specs=specs or [in_vmem] * len(args),
            out_specs=out_specs or (in_vmem if single else (in_vmem,) * len(shapes)),
            scratch_shapes=scratch,
            compiler_params=pltpu.CompilerParams(vmem_limit_bytes=mib << 20),
            cost_estimate=pl.CostEstimate(flops=flops, bytes_accessed=1 << 20, transcendentals=0),
        )(*args)

    def shape(*dims, kind=f32):
        return jax.ShapeDtypeStruct(dims, kind)

    zeros = [pltpu.VMEM((pairs, 2 * panels, panels), f32)] if pairs <= slots else []
    kept_ids = [pltpu.SMEM(x.shape, x.dtype) for x in (target_ids, source_ids)]
    mine, *ids = call(
        pack_kernel,
        (shape(2 * blocks * panels, width, kind=bf16), *kept_ids, *zeros),
        [pltpu.with_memory_space_constraint(x, pltpu.HBM) for x in (strengths, adjoint_weights, target_ids, source_ids)],
        [in_hbm] * 4,
        [pltpu.SemaphoreType.DMA((4,))],
        out_specs=(in_vmem, in_smem, in_smem) + (in_vmem,) * len(zeros),
        flops=1 << 34,
    )
    ids, zeros = ids[:2], ids[2:]
    slot_args = (live_slots, *(pltpu.with_memory_space_constraint(x, pltpu.SMEM) for x in ids))
    gathered = [exchange(mine, "clu", k) for k in range(clusters - 1, 0, -1)]
    gathered = [mine] + gathered[::-1]

    def group_strengths(token):
        return call(
            functools.partial(group_kernel, blocks, panels),
            shape(group_blocks * panels, width, kind=bf16),
            (token, *gathered),
            [in_hbm] + [in_vmem] * clusters,
        )

    def coded(count):
        return shape(count * panels + EXPONENT_ROWS * pl.cdiv(count, EXPONENT_ROWS), width, kind=jnp.int16)

    block_sums = shape(group_blocks, panels, width)
    if pairs <= slots:
        total = call(
            functools.partial(combine_kernel, group_blocks, blocks, chunk),
            pltpu.VMEM((pairs, 2 * panels, panels), f32),
            (*slot_args, *(pltpu.with_memory_space_constraint(x, pltpu.VMEM) for x in (kernels, *zeros))),
            [in_smem] * 3 + [in_vmem] * 2,
            flops=1 << 33,
            aliases=[(4, 0)],
        )
        own = group_strengths(total)
        first = exchange_beside(own, 0)
        total = pltpu.with_memory_space_constraint(total, pltpu.VMEM)
        kept_shape = pltpu.VMEM((2, pairs // 3, 2 * panels, panels), bf16)
        kept_second, across, upper = call(
            functools.partial(second_kernel, blocks, panels, group_blocks),
            (
                kept_shape,
                shape(width, 2 * group_blocks * panels, kind=bf16),
                coded(2 * group_blocks),
            ),
            (own, total, *gathered),
            [in_hbm] + [in_vmem] * (1 + clusters),
            flops=1 << 33,
        )
        kept_first, lower = call(
            functools.partial(first_kernel, group_blocks),
            (kept_shape, coded(group_blocks)),
            (first, total, across),
            [in_hbm] + [in_vmem] * 2,
            flops=1 << 33,
        )
        kept_first, kept_second = (pltpu.with_memory_space_constraint(x, pltpu.VMEM) for x in (kept_first, kept_second))
        potential, middle = call(
            functools.partial(inner_kernel, blocks),
            (block_sums, block_sums),
            (total, across, kept_first, first, *gathered),
            scratch=[kept_shape],
        )
        upper, lower = exchange_beside(upper, 1), exchange_beside(lower, 0)
        parts_body, parts_args = parts_kernel, (kept_second, potential, middle, lower, upper)
    else:
        own = group_strengths(mine)
        first, second = exchange_beside(own, 0), exchange_beside(own, 1)
        potential, adjoint = call(
            functools.partial(slots_kernel, blocks, panels, chunk),
            (block_sums, shape(sources, width, panels)),
            (*slot_args, pltpu.with_memory_space_constraint(kernels, pltpu.HBM), first, second, *gathered),
            [in_smem] * 3 + [in_hbm] + [in_vmem] * (2 + clusters),
            [
                pltpu.VMEM(kernels.shape, bf16),
                pltpu.VMEM((sources, 2 * panels, width), bf16),
                pltpu.VMEM((group_blocks, width, 2 * panels), bf16),
                pltpu.SemaphoreType.DMA((slots // chunk,)),
            ],
            mib=40,
        )
        lower, upper = call(code_kernel, (coded(group_blocks),) * 2, (adjoint,))
        upper, lower = exchange_beside(upper, 1), exchange_beside(lower, 0)
        parts_body, parts_args = slots_parts_kernel, (potential, adjoint, lower, upper)
    mine, *parts = call(
        functools.partial(parts_body, blocks),
        (shape(2 * blocks * panels, width),) + (coded(2 * blocks),) * (clusters - 1),
        parts_args,
    )
    parts = [exchange(parts[k - 1], "clu", k) for k in range(clusters - 1, 0, -1)]
    out = shape(blocks * panels, width)
    return tuple(call(functools.partial(finish_kernel, blocks, panels), (out, out), (mine, *parts)))


def solution(mesh):
    return jax.shard_map(
        local,
        mesh=mesh,
        in_specs=(
            P(("grp", "clu"), None),
            P(("grp", "clu"), None),
            P(("grp", "clu"), None, None, None),
            P(("grp", "clu")),
            P(("grp", "clu")),
            P(("grp", "clu")),
        ),
        out_specs=(P(("grp", "clu"), None), P(("grp", "clu"), None)),
        check_vma=False,
    )
```
